32 devices in a mesh: grp: 2 (over x), tile: 16 (over z, y, core).
Axes of the slice: x: 2, y: 2, z: 4, core: 2. Of those that a mesh axis runs over, the one named last changes fastest.
Arguments:
- ct_tracer: float32 [48, 256, 1280], P(None, ('grp', 'tile')), parts along dimension 1, may hold values from -6 to 6
- ct_surface: float32 [256, 1280], P(('grp', 'tile')), parts along dimension 0, may hold values from -6 to 6
- kappa: float32 [48, 128, 1280], P(None, 'tile'), may hold values from 0.02 to 0.2
- kvert: float32 [48, 128, 1280], P(None, 'tile'), may hold values from 0.1 to 10
- land: int32 [48, 128, 1280], P(None, 'tile'), may hold values 0 or 1
- kmt: int32 [128, 1280], P('tile'), may hold values from 24 to 48
- screen: float32 [128, 1280], P('tile'), may hold values from 0.05 to 1
- layer_weight: float32 [48], replicated, may hold values from 0.5 to 2
Outputs:
- adj_tracer: float32 [48, 256, 1280], P(None, ('grp', 'tile')), parts along dimension 1
- adj_surface: float32 [256, 1280], P(('grp', 'tile')), parts along dimension 0
The draws below stay inside these ranges and needn't reach their ends.
There are 2 independent parts, one for each index of `grp`. The reference program is written for one: setup_inputs(seed, part) draws one part's arguments, and reference() takes and returns one part's arrays. A program takes and returns all parts, laid end to end along the dimension named above; an argument that names none is the same for every part. Nothing has to cross between parts.
All inputs are finite; a program needn't handle non-finite values. No bound on the sum of `land` on one device may be relied on, other than what follows from the above.
Results may differ from the reference program's by a relative error of at most 0.0001.
Values sent between devices are 32-bit elements; how exact they have to be, the bound alone decides.
No kernel may reach another device: no remote copies, remote signals or barrier semaphores. Data moves between devices by JAX's collectives and lax.ppermute only.
A program may use at most 64 MiB of HBM per device.

```python
import math
import jax
import jax.numpy as jnp

NZ = 48
NX = 1280
ITERS = 3
SUBSTEPS = 2
NY = 128


def place_ends(values, rng, least, high):
    place = [jax.random.randint(jax.random.fold_in(rng, axis), (), 0, length) for axis, length in enumerate(values.shape)]
    widest = values.shape.index(max(values.shape))
    next_to = place[:widest] + [(place[widest] + 1) % values.shape[widest]] + place[widest + 1:]
    return values.at[tuple(place)].set(least).at[tuple(next_to)].set(high)


def shard_levels(own_key, dims, shards, low, largest):
    loudness = 1.0
    for position, blocks in shards:
        steps = jax.random.uniform(jax.random.fold_in(jax.random.fold_in(own_key, 6), position), (blocks,), jnp.float32, low / len(shards), largest / len(shards))
        loudness = loudness * jnp.repeat(jnp.exp(steps), dims[position] // blocks).reshape((-1,) + (1,) * (len(dims) - 1 - position))
    return loudness


def normal_values(rng, extent, width, limit, shards=(), held_as=jnp.bfloat16):
    values = jax.random.normal(rng, extent, jnp.float32) * width
    if len(shards) > 0:
        values = shard_levels(rng, extent, shards, -0.22, 0.18) * values
    return jnp.clip(values, min=-limit, max=limit).astype(held_as)


def setup_inputs(seed: int = 0, part: int = 0) -> dict:
    arg_keys = jax.random.split(jax.random.key(seed), 9)
    part_splits = jax.random.split(jax.random.fold_in(arg_keys[8], part), 9)
    return {
        "ct_tracer": normal_values(part_splits[0], (NZ, NY, NX), 1.0, 6.0, ((1, 16),), jnp.float32),
        "ct_surface": normal_values(part_splits[1], (NY, NX), 1.0, 6.0, ((0, 16),), jnp.float32),
        "kappa": jnp.clip(jnp.exp(math.log(0.2) - 2.3025851 * jax.random.uniform(arg_keys[2], (NZ, NY, NX), jnp.float32) ** shard_levels(arg_keys[2], (NZ, NY, NX), ((1, 16),), -0.2, 0.2)), 0.02, 0.2),
        "kvert": jnp.clip(jnp.exp(math.log(10.0) - 4.6051702 * jax.random.uniform(arg_keys[3], (NZ, NY, NX), jnp.float32) ** shard_levels(arg_keys[3], (NZ, NY, NX), ((1, 16),), -0.2, 0.2)), 0.1, 10.0),
        "land": place_ends((jax.random.randint(arg_keys[4], (NZ, NY, NX), 0, 10) < 9).astype(jnp.int32), jax.random.fold_in(arg_keys[4], 1), 0, 1),
        "kmt": place_ends(jax.random.randint(arg_keys[5], (NY, NX), NZ // 2, NZ + 1), jax.random.fold_in(arg_keys[5], 1), NZ // 2, NZ).astype(jnp.int32),
        "screen": jnp.clip(jnp.exp(math.log(1.0) - 2.9957323 * jax.random.uniform(arg_keys[6], (NY, NX), jnp.float32) ** shard_levels(arg_keys[6], (NY, NX), ((0, 16),), -0.2, 0.2)), 0.05, 1.0),
        "layer_weight": jnp.clip(jnp.exp(jax.random.uniform(arg_keys[7], (NZ,), jnp.float32, math.log(0.5), math.log(2.0))), 0.5, 2.0),
    }


def wet_cells(land, kmt):
    levels = jnp.arange(land.shape[0], dtype=jnp.int32)[:, None, None]
    return (land * (levels < kmt[None, :, :]).astype(jnp.int32)).astype(jnp.float32)


def solve_columns(source, coupling):
    depth_count = source.shape[0]
    ratios = []
    carried = []
    ratio_prev = jnp.zeros_like(source[0])
    carry_prev = jnp.zeros_like(source[0])
    above_link = jnp.zeros_like(source[0])
    for level_index in range(depth_count):
        divisor = 1.0 + coupling[level_index] + above_link + above_link * ratio_prev
        ratio_prev = -coupling[level_index] / divisor
        carry_prev = (source[level_index] + above_link * carry_prev) / divisor
        ratios.append(ratio_prev)
        carried.append(carry_prev)
        above_link = coupling[level_index]
    result = [carried[-1]]
    for level_index in range(depth_count - 2, -1, -1):
        result.append(carried[level_index] - ratios[level_index] * result[-1])
    return jnp.stack(result[::-1])


def diffuse(values, kappa, wet):
    face_x = 0.5 * (kappa + jnp.roll(kappa, -1, 2)) * wet * jnp.roll(wet, -1, 2)
    flux_x = face_x * (jnp.roll(values, -1, 2) - values)
    face_y = 0.5 * (kappa[:, 1:] + kappa[:, :-1]) * wet[:, 1:] * wet[:, :-1]
    flux_y = face_y * (values[:, 1:] - values[:, :-1])
    rim_zero = jnp.zeros_like(values[:, :1])
    north = jnp.concatenate([flux_y, rim_zero], 1)
    south = jnp.concatenate([rim_zero, flux_y], 1)
    return values + flux_x - jnp.roll(flux_x, 1, 2) + north - south


def surface_apply(values, height, surface, screen):
    face_x = 0.5 * (height + jnp.roll(height, -1, 1)) * surface * jnp.roll(surface, -1, 1)
    flux_x = face_x * (jnp.roll(values, -1, 1) - values)
    face_y = 0.5 * (height[1:] + height[:-1]) * surface[1:] * surface[:-1]
    flux_y = face_y * (values[1:] - values[:-1])
    rim_zero = jnp.zeros_like(values[:1])
    north = jnp.concatenate([flux_y, rim_zero], 0)
    south = jnp.concatenate([rim_zero, flux_y], 0)
    return screen * values - (flux_x - jnp.roll(flux_x, 1, 1) + north - south)


def reference(ct_tracer, ct_surface, kappa, kvert, land, kmt, screen, layer_weight):
    wet = wet_cells(land, kmt)
    share = layer_weight / jnp.sum(layer_weight)
    height = jnp.sum(share[:, None, None] * wet, axis=0)
    surface = wet[0]
    solution = jnp.zeros_like(ct_surface)
    residual = ct_surface
    direction = ct_surface
    norm_now = jnp.sum(residual * residual)
    for iteration in range(ITERS):
        image = surface_apply(direction, height, surface, screen)
        alpha = norm_now / jnp.sum(direction * image)
        solution = solution + alpha * direction
        residual = residual - alpha * image
        norm_next = jnp.sum(residual * residual)
        direction = residual + (norm_next / norm_now) * direction
        norm_now = norm_next
    column = ct_tracer + wet * share[:, None, None] * solution[None]
    coupling = kvert * wet * jnp.concatenate([wet[1:], jnp.zeros_like(wet[:1])], 0)
    values = solve_columns(column, coupling)
    for sub_index in range(SUBSTEPS):
        values = diffuse(values, kappa, wet)
    return values, solution
```

```python
import jax
import jax.numpy as jnp
from jax import lax
from jax.sharding import PartitionSpec as P

ITERS = 3
SUBSTEPS = 2


def extended(array, sides, width):
    for axis, dim in sides:
        count, length = (lax.axis_size(axis), array.shape[dim])
        up = [(i, (i + 1) % count) for i in range(count - 1)]
        down = [(j, i) for i, j in up]
        last = lax.slice_in_dim(array, length - width, length, axis=dim)
        leading = lax.slice_in_dim(array, 0, width, axis=dim)
        before = lax.ppermute(last, axis, up)
        after = lax.ppermute(leading, axis, down)
        array = jnp.concatenate([before, array, after], axis=dim)
    return array


def wet_cells(land, kmt):
    levels = jnp.arange(land.shape[0], dtype=jnp.int32)[:, None, None]
    return (land * (levels < kmt[None, :, :]).astype(jnp.int32)).astype(jnp.float32)


def solve_columns(source, coupling):
    depth_count = source.shape[0]
    ratios = []
    carried = []
    ratio_prev = jnp.zeros_like(source[0])
    carry_prev = jnp.zeros_like(source[0])
    above_link = jnp.zeros_like(source[0])
    for level_index in range(depth_count):
        divisor = 1.0 + coupling[level_index] + above_link + above_link * ratio_prev
        ratio_prev = -coupling[level_index] / divisor
        carry_prev = (source[level_index] + above_link * carry_prev) / divisor
        ratios.append(ratio_prev)
        carried.append(carry_prev)
        above_link = coupling[level_index]
    result = [carried[-1]]
    for level_index in range(depth_count - 2, -1, -1):
        result.append(carried[level_index] - ratios[level_index] * result[-1])
    return jnp.stack(result[::-1])


def vertical_coupling(kvert, wet):
    return kvert * wet * jnp.concatenate([wet[1:], jnp.zeros_like(wet[:1])], 0)


def diffuse_rows(padded, kap_pad, wet_pad):
    inner = padded[:, 1:-1]
    kap_own = kap_pad[:, 1:-1]
    wet_own = wet_pad[:, 1:-1]
    face_x = 0.5 * (kap_own + jnp.roll(kap_own, -1, 2)) * wet_own * jnp.roll(wet_own, -1, 2)
    flux_x = face_x * (jnp.roll(inner, -1, 2) - inner)
    face_y = 0.5 * (kap_pad[:, 1:] + kap_pad[:, :-1]) * wet_pad[:, 1:] * wet_pad[:, :-1]
    flux_y = face_y * (padded[:, 1:] - padded[:, :-1])
    return inner + flux_x - jnp.roll(flux_x, 1, 2) + flux_y[:, 1:] - flux_y[:, :-1]


LOW = 0.05
HIGH = 9.0
MID = 0.5 * (HIGH + LOW)
HALF = 0.5 * (HIGH - LOW)


def neighbours(array, width):
    count = lax.axis_size("tile")
    up = [(i, i + 1) for i in range(count - 1)]
    down = [(i + 1, i) for i in range(count - 1)]
    return lax.ppermute(array[-width:], "tile", up), lax.ppermute(array[:width], "tile", down)


def surface_image(values, height, surface, screen):
    face_x = 0.5 * (height + jnp.roll(height, -1, 1)) * surface * jnp.roll(surface, -1, 1)
    flux_x = face_x * (jnp.roll(values, -1, 1) - values)
    face_y = 0.5 * (height[1:] + height[:-1]) * surface[1:] * surface[:-1]
    flux_y = face_y * (values[1:] - values[:-1])
    across = flux_x - jnp.roll(flux_x, 1, 1)
    return screen[1:-1] * values[1:-1] - (across[1:-1] + flux_y[1:] - flux_y[:-1])


def quadratic(left, form):
    return sum(left[i] * left[j] * form[i][j] for i in range(3) for j in range(3))


def weights(sums):
    s0, s1, s2, s3, s4, s5 = sums
    g02 = 2.0 * s2 - s0
    gram = ((s0, s1, g02), (s1, s2, s3), (g02, s3, s4))
    shift = ((s1, s2, s3), (s2, 0.5 * (s3 + s1), 0.5 * (s4 + g02)), (s3, 0.5 * (s4 + g02), s5))
    form = [[MID * gram[i][j] + HALF * shift[i][j] for j in range(3)] for i in range(3)]
    one, zero = jnp.ones_like(s0), jnp.zeros_like(s0)
    x, r, d = [zero] * 3, [one, zero, zero], [one, zero, zero]
    rr = s0
    for step in range(ITERS):
        alpha = jnp.clip(rr / quadratic(d, form), 1.0 / HIGH, 1.0 / LOW)
        x = [x[i] + alpha * d[i] for i in range(3)]
        if step + 1 < ITERS:
            image = [
                MID * d[0] + HALF * 0.5 * d[1],
                MID * d[1] + HALF * (d[0] + 0.5 * d[2]),
                MID * d[2] + HALF * 0.5 * d[1],
            ]
            r = [r[i] - alpha * image[i] for i in range(3)]
            new = quadratic(r, gram)
            beta = jnp.clip(new / rr, 0.0, HIGH / LOW)
            d = [r[i] + beta * d[i] for i in range(3)]
            rr = new
    return x


def body(ct_tracer, ct_surface, kappa, kvert, land, kmt, screen, layer_weight):
    wet = wet_cells(land, kmt)
    share = layer_weight / jnp.sum(layer_weight)
    height = jnp.sum(share[:, None, None] * wet, axis=0)
    own = jnp.stack([ct_surface, height, wet[0], screen], 1)
    before, after = neighbours(own, 3)
    rows = jnp.concatenate([before, own, after], 0)
    base0, high_ext, surf_ext, screen_ext = (rows[:, i] for i in range(4))

    def shifted(values, cut):
        cut_rows = slice(cut, rows.shape[0] - cut)
        image = surface_image(values, high_ext[cut_rows], surf_ext[cut_rows], screen_ext[cut_rows])
        return (image - MID * values[1:-1]) / HALF

    base1 = shifted(base0, 0)
    base2 = 2.0 * shifted(base1, 1) - base0[2:-2]
    next2 = shifted(base2, 2)
    b0, b1, b2 = base0[3:-3], base1[2:-2], base2[1:-1]
    partial = jnp.stack([jnp.sum(p * q) for p, q in ((b0, b0), (b0, b1), (b1, b1), (b1, b2), (b2, b2), (b2, next2))])
    count = lax.axis_size("tile")
    spread = jnp.broadcast_to(jnp.pad(partial, (0, 122))[None], (count, 128))
    total = jnp.sum(lax.all_to_all(spread, "tile", 0, 0, tiled=True), 0)
    mix = weights([total[i] for i in range(6)])
    solution = mix[0] * b0 + mix[1] * b1 + mix[2] * b2
    stacked = extended(jnp.stack([kappa, wet]), (("tile", 2),), 1)
    kap_pad, wet_pad = stacked[0], stacked[1]
    column = ct_tracer + wet * share[:, None, None] * solution[None]
    values = solve_columns(column, vertical_coupling(kvert, wet))
    remaining = SUBSTEPS
    for sub_index in range(remaining):
        padded = extended(values, (("tile", 1),), 1)
        values = diffuse_rows(padded, kap_pad, wet_pad)
    return (values, solution)


def solution(mesh):
    in_specs = (
        P(None, ("grp", "tile"), None),
        P(("grp", "tile"), None),
        P(None, "tile", None),
        P(None, "tile", None),
        P(None, "tile", None),
        P("tile", None),
        P("tile", None),
        P(),
    )
    out_specs = (P(None, ("grp", "tile"), None), P(("grp", "tile"), None))
    return jax.shard_map(body, mesh=mesh, in_specs=in_specs, out_specs=out_specs, check_vma=False)
```

```python
import functools

import jax
import jax.numpy as jnp
from jax import lax
from jax.experimental import pallas as pl
from jax.experimental.pallas import tpu as pltpu
from jax.sharding import PartitionSpec as P

ITERS = 3
ROWS = 8
LOW = 0.05
HIGH = 9.0
MID = 0.5 * (HIGH + LOW)
HALF = 0.5 * (HIGH - LOW)
FLOAT = jnp.float32
LIMIT = 12 * 1024 * 1024


def east(values):
    return pltpu.roll(values, values.shape[1] - 1, 1)


def west(values):
    return pltpu.roll(values, 1, 1)


def north(values):
    return pltpu.roll(values, values.shape[0] - 1, 0)


def south(values):
    return pltpu.roll(values, 1, 0)


def stacked(values):
    return jnp.concatenate([values[:, i : i + 128] for i in range(0, values.shape[1], 128)], axis=0)


def unstacked(values):
    return jnp.concatenate([values[i : i + ROWS, :] for i in range(0, values.shape[0], ROWS)], axis=1)


def lane_index(values):
    return lax.broadcasted_iota(jnp.int32, values.shape, 1)


def east_of(values):
    turned = pltpu.roll(values, 127, 1)
    further = jnp.concatenate([turned[ROWS:, :], turned[:ROWS, :]], axis=0)
    return jnp.where(lane_index(values) == 127, further, turned)


def west_of(values):
    turned = pltpu.roll(values, 1, 1)
    further = jnp.concatenate([turned[-ROWS:, :], turned[:-ROWS, :]], axis=0)
    return jnp.where(lane_index(values) == 0, further, turned)


def turned_rows(values, shift):
    return pltpu.roll(values.reshape(-1, ROWS, 128), shift, 1).reshape(values.shape)


def north_of(values):
    return turned_rows(values, ROWS - 1)


def south_of(values):
    return turned_rows(values, 1)


def row_of(ref, block, row, width):
    tall = width // 128 * ROWS
    return jnp.concatenate(
        [ref[pl.ds(block * 8 * tall + j * ROWS + row, 8, stride=tall), :] for j in range(width // 128)], axis=1
    )


def level_at(k, width):
    tall = width // 128 * ROWS
    return pl.ds(pl.multiple_of(k * tall, tall), tall)


def rows_at(k):
    return pl.ds(pl.multiple_of(k * ROWS, ROWS), ROWS)


def row_index(values):
    return lax.broadcasted_iota(jnp.int32, values.shape, 0)


def spread(row, like):
    return jnp.broadcast_to(row, like.shape)


def kernel(body, outs, ins, name, scratch=(), cost=1000000):
    return pl.pallas_call(
        body,
        out_shape=[pltpu.VMEM(shape, FLOAT) for shape in outs],
        in_specs=ins,
        out_specs=[pl.BlockSpec(memory_space=pltpu.VMEM)] * len(outs),
        scratch_shapes=[pltpu.VMEM(shape, FLOAT) for shape in scratch],
        name=name,
        cost_estimate=pl.CostEstimate(flops=cost, bytes_accessed=cost, transcendentals=0),
        compiler_params=pltpu.CompilerParams(vmem_limit_bytes=LIMIT),
    )


def in_vmem(count):
    return [pl.BlockSpec(memory_space=pltpu.VMEM)] * count


def held(array):
    return pltpu.with_memory_space_constraint(array, pltpu.VMEM)


def setup_body(levels, weight, land, kmt, ct, screen, wet_ref, height_ref, surface_ref,
               fx_ref, fn_ref, dg_ref, q1_ref, up_ref, down_ref, buffer, sems):
    chunk = levels // 4
    copies = [
        pltpu.make_async_copy(
            land.at[pl.ds(i * chunk * ROWS, chunk * ROWS)],
            buffer.at[pl.ds(i * chunk * ROWS, chunk * ROWS)],
            sems.at[i],
        )
        for i in range(4)
    ]
    for copy in copies:
        copy.start()
    total = weight[0]
    for k in range(1, levels):
        total = total + weight[k]
    depth = kmt[...]
    height = jnp.zeros(depth.shape, FLOAT)
    for i, copy in enumerate(copies):
        copy.wait()

        def level(k, height):
            wet = jnp.where(k < depth, buffer[rows_at(k), :], 0).astype(FLOAT)
            wet_ref[level_at(k, depth.shape[1]), :] = stacked(wet)
            return height + weight[k] * wet

        height = lax.fori_loop(i * chunk, (i + 1) * chunk, level, height, unroll=4)
    height = height / total
    surface = jnp.where(0 < depth, buffer[0:ROWS, :], 0).astype(FLOAT)
    height_ref[...] = height
    surface_ref[...] = surface
    base = ct[...]
    rows = row_index(base)
    scale = 0.5 / HALF
    fx = scale * (height + east(height)) * surface * east(surface)
    fn = scale * (height + north(height)) * surface * north(surface)
    fn = jnp.where(rows < ROWS - 1, fn, 0.0)
    fs = south(fn)
    fw = west(fx)
    dg = (screen[...] - MID) * (1.0 / HALF) + fx + fw + fn + fs

    def apply(v):
        return dg * v - fx * east(v) - fw * west(v) - fn * north(v) - fs * south(v)

    q1 = apply(base)
    q2 = apply(q1)
    fx_ref[...] = fx
    fn_ref[...] = fn
    dg_ref[...] = dg
    q1_ref[...] = q1
    for ref, row in ((down_ref, 0), (up_ref, ROWS - 1)):
        for place, values in enumerate((base, q1, q2, fx, dg, height, surface)):
            ref[place : place + 1, :] = values[row : row + 1, :]
        ref[7:8, :] = jnp.zeros_like(base[0:1, :])


def basis_body(count, ct, height, surface, fx_ref, fn_ref, dg_ref, q1_ref, before, after, b1_ref, b2_ref, sums_ref):
    b0 = ct[...]
    rows = row_index(b0)
    first, last = rows == 0, rows == ROWS - 1
    fx, fn, dg = fx_ref[...], fn_ref[...], dg_ref[...]
    fw, fs = west(fx), south(fn)

    def halo(ref, row):
        b0_h, q1_h, q2_h, fx_h, dg_h, high_h, wet_h = (ref[i : i + 1, :] for i in range(7))
        face = (0.5 / HALF) * (high_h + height[row : row + 1, :]) * wet_h * surface[row : row + 1, :]
        extra = face * (b0_h - ct[row : row + 1, :])
        return b0_h, q1_h + extra, q2_h, fx_h, dg_h, face, extra

    def lift(row):
        return jnp.broadcast_to(row, b0.shape)

    sides = (halo(before, 0), halo(after, ROWS - 1))
    face_b, face_a = lift(sides[0][5]), lift(sides[1][5])
    b1 = q1_ref[...] - jnp.where(first, lift(sides[0][6]), 0.0) - jnp.where(last, lift(sides[1][6]), 0.0)
    dg = dg + jnp.where(first, face_b, 0.0) + jnp.where(last, face_a, 0.0)
    fn = jnp.where(last, face_a, fn)
    fs = jnp.where(first, face_b, fs)

    def apply(v, v_before, v_after):
        v_n = jnp.where(last, lift(v_after), north(v))
        v_s = jnp.where(first, lift(v_before), south(v))
        return dg * v - fx * east(v) - fw * west(v) - fn * v_n - fs * v_s

    b2 = 2.0 * apply(b1, sides[0][1], sides[1][1]) - b0

    def outer(side, own):
        b0_h, b1_h, q2_h, fx_h, dg_h, face, extra = side
        b0_h, b1_h, q2_h, fx_h, dg_h, face, extra, own = (lift(v) for v in (b0_h, b1_h, q2_h, fx_h, dg_h, face, extra, own))
        turned = dg_h * extra - fx_h * east(extra) - west(fx_h) * west(extra)
        return (2.0 * (q2_h + turned + face * (b1_h - own)) - b0_h)[0:1, :]

    b2_b = outer(sides[0], b1[0:1, :])
    b2_a = outer(sides[1], b1[ROWS - 1 : ROWS, :])
    next2 = apply(b2, b2_b, b2_a)
    b1_ref[...] = b1
    b2_ref[...] = b2
    tile_rows = lax.broadcasted_iota(jnp.int32, (8, 128), 0)
    packed = jnp.zeros((8, 128), FLOAT)
    for place, (p, q) in enumerate(((b0, b0), (b0, b1), (b1, b1), (b1, b2), (b2, b2), (b2, next2))):
        product = p * q
        folded = product[:, 0:128]
        for j in range(1, product.shape[1] // 128):
            folded = folded + product[:, j * 128 : (j + 1) * 128]
        packed = jnp.where(tile_rows == place, jnp.sum(folded, axis=0, keepdims=True), packed)
    for j in range(count):
        sums_ref[j * 8 : (j + 1) * 8, :] = packed


def quadratic(left, form):
    total = None
    for i in range(3):
        for j in range(3):
            if left[i] is not None and left[j] is not None:
                term = left[i] * left[j] * form[i][j]
                total = term if total is None else total + term
    return total


def plus(p, q):
    return q if p is None else p if q is None else p + q


def times(scale, p):
    return None if p is None else scale * p


def weights(sums):
    s0, s1, s2, s3, s4, s5 = sums
    g02 = 2.0 * s2 - s0
    gram = ((s0, s1, g02), (s1, s2, s3), (g02, s3, s4))
    b11, b12 = 0.5 * (s3 + s1), 0.5 * (s4 + g02)
    shift = ((s1, s2, s3), (s2, b11, b12), (s3, b12, s5))
    form = [[MID * gram[i][j] + HALF * shift[i][j] for j in range(3)] for i in range(3)]
    one = jnp.ones_like(s0)
    x, r, d = [None] * 3, [one, None, None], [one, None, None]
    rr = s0
    for step in range(ITERS):
        alpha = jnp.clip(rr / quadratic(d, form), 1.0 / HIGH, 1.0 / LOW)
        x = [plus(x[i], times(alpha, d[i])) for i in range(3)]
        if step + 1 < ITERS:
            image = [
                plus(times(MID, d[0]), times(0.5 * HALF, d[1])),
                plus(plus(times(MID, d[1]), times(HALF, d[0])), times(0.5 * HALF, d[2])),
                plus(times(MID, d[2]), times(0.5 * HALF, d[1])),
            ]
            r = [plus(r[i], times(-1.0, times(alpha, image[i]))) for i in range(3)]
            new = quadratic(r, gram)
            beta = jnp.clip(new / rr, 0.0, HIGH / LOW)
            d = [plus(r[i], times(beta, d[i])) for i in range(3)]
            rr = new
    return x


def edges_body(levels, count, sums, ct, b1, b2, m0, w, fx, fn, s_ref, up_ref, down_ref):
    total = sums[0:8, :]
    for j in range(1, count):
        total = total + sums[j * 8 : (j + 1) * 8, :]
    total = jnp.sum(total, axis=1, keepdims=True)
    mix = weights([total[i : i + 1, :] for i in range(6)])
    s = mix[0] * ct[...] + mix[1] * b1[...] + mix[2] * b2[...]
    s_ref[...] = s
    s_rows = {r: spread(s[r : r + 1, :], s) for r in (0, 1, ROWS - 2, ROWS - 1)}

    def packed(ref, block, r):
        return row_of(ref, block, r, ct.shape[1])

    def across(u, face):
        flux = face * (east(u) - u)
        return flux - west(flux)

    for block in range(levels // 8):
        u = {r: packed(m0, block, r) + s_rows[r] * packed(w, block, r) for r in s_rows}
        at, below = pl.ds(block * 8, 8), pl.ds(levels + block * 8, 8)
        for ref, row, inner, link in ((down_ref, 0, 1, 0), (up_ref, ROWS - 1, ROWS - 2, ROWS - 2)):
            ref[at, :] = u[row]
            ref[below, :] = u[row] + across(u[row], packed(fx, block, row)) + packed(fn, block, link) * (u[inner] - u[row])


def columns_body(levels, weight, source, kvert, wet, m0, w, ratio):
    total = weight[0]
    for k in range(1, levels):
        total = total + weight[k]
    width = source.shape[1]
    shape = (ROWS * width // 128, 128)
    inverse = 1.0 / jnp.full(shape, total, FLOAT)

    def down(k, carry):
        link, m_in, w_in = carry
        at = level_at(k, width)
        here = wet[at, :]
        below = jnp.where(k + 1 < levels, wet[level_at(jnp.minimum(k + 1, levels - 1), width), :], 0.0)
        coupling = stacked(kvert[rows_at(k), :]) * here * below
        over = 1.0 / (1.0 + coupling + link)
        m_here = (stacked(source[rows_at(k), :]) + m_in) * over
        w_here = (here * (weight[k] * inverse) + w_in) * over
        part = coupling * over
        ratio[at, :] = part
        m0[at, :] = m_here
        w[at, :] = w_here
        return coupling - coupling * part, coupling * m_here, coupling * w_here

    zero = jnp.zeros(shape, FLOAT)
    lax.fori_loop(0, levels, down, (zero, zero, zero))

    def up(i, carry):
        at = level_at(levels - 2 - i, width)
        m_below, w_below = carry
        part = ratio[at, :]
        m_here = m0[at, :] + part * m_below
        w_here = w[at, :] + part * w_below
        m0[at, :] = m_here
        w[at, :] = w_here
        return m_here, w_here

    last = level_at(levels - 1, width)
    lax.fori_loop(0, levels - 1, up, (m0[last, :], w[last, :]))


def faces_body(levels, kappa, wet, fx_ref, fn_ref):
    width = kappa.shape[1]
    shape = (ROWS * width // 128, 128)
    inside = lax.rem(lax.broadcasted_iota(jnp.int32, shape, 0), ROWS) < ROWS - 1

    def level(k, carry):
        at = level_at(k, width)
        kap, here = 0.5 * stacked(kappa[rows_at(k), :]), wet[at, :]
        fx_ref[at, :] = (kap + east_of(kap)) * here * east_of(here)
        fn_ref[at, :] = jnp.where(inside, (kap + north_of(kap)) * here * north_of(here), 0.0)
        return carry

    lax.fori_loop(0, levels, level, 0)


def rims_body(levels, kappa, wet, up_ref, down_ref, buffer):
    width = kappa.shape[1]

    def level(k, carry):
        buffer[level_at(k, width), :] = stacked(kappa[rows_at(k), :])
        return carry

    lax.fori_loop(0, levels, level, 0, unroll=4)
    for ref, row in ((down_ref, 0), (up_ref, ROWS - 1)):
        for block in range(levels // 8):
            ref[pl.ds(block * 8, 8), :] = row_of(buffer, block, row, width)
            ref[pl.ds(levels + block * 8, 8), :] = row_of(wet, block, row, width)


def inner_body(levels, m0, w, s_ref, fx_ref, fn_ref, u2_ref):
    width = s_ref.shape[1]
    s = stacked(s_ref[...])

    def level(k, carry):
        at = level_at(k, width)
        fx, fn = fx_ref[at, :], fn_ref[at, :]
        u = m0[at, :] + s * w[at, :]
        for _ in range(2):
            flux_x = fx * (east_of(u) - u)
            flux_y = fn * (north_of(u) - u)
            u = u + (flux_x - west_of(flux_x)) + (flux_y - south_of(flux_y))
        u2_ref[at, :] = u
        return carry

    lax.fori_loop(0, levels, level, 0)


def finish_body(levels, u2, fx, fn, own_up, own_down, rim_up, rim_down, before, after, rim_before, rim_after,
                out, change_ref, buffer, sems):
    width = own_up.shape[1]
    rows = lax.broadcasted_iota(jnp.int32, (ROWS, width), 0)
    sides = (
        (own_down, rim_down, before, rim_before, 0, 1, 0),
        (own_up, rim_up, after, rim_after, ROWS - 1, ROWS - 2, ROWS - 2),
    )
    copies = []
    for block in range(levels // 8):
        at, below = pl.ds(block * 8, 8), pl.ds(levels + block * 8, 8)
        for own, rim, other, rim_other, row, inner, link in sides:
            face = 0.5 * (rim[at, :] + rim_other[at, :]) * rim[below, :] * rim_other[below, :]
            change = face * (other[at, :] - own[at, :])
            flux = row_of(fx, block, row, width) * (east(change) - change)
            passed = row_of(fn, block, link, width) * change
            change_ref[row] = (change + (flux - west(flux)) - passed
                               + face * (other[below, :] - own[below, :] - 2.0 * change))
            change_ref[inner] = passed
        for k in range(8):
            level = block * 8 + k
            values = unstacked(u2[level_at(level, width), :])
            for row in (0, 1, ROWS - 2, ROWS - 1):
                values = values + jnp.where(rows == row, spread(change_ref[row, k : k + 1, :], values), 0.0)
            buffer[rows_at(level), :] = values
        whole = pl.ds(block * 8 * ROWS, 8 * ROWS)
        copy = pltpu.make_async_copy(buffer.at[whole], out.at[whole], sems.at[block])
        copy.start()
        copies.append(copy)
    for copy in copies:
        copy.wait()


def exchange(to_next, to_previous):
    count = lax.axis_size("tile")
    up = [(i, i + 1) for i in range(count - 1)]
    down = [(i + 1, i) for i in range(count - 1)]
    return lax.ppermute(to_next, "tile", up), lax.ppermute(to_previous, "tile", down)


def body(ct_tracer, ct_surface, kappa, kvert, land, kmt, screen, layer_weight):
    levels, rows, width = ct_tracer.shape
    count = lax.axis_size("tile")
    tall = levels * rows
    tile, field, rim = (rows, width), (tall * width // 128, 128), (2 * levels, width)
    flat = lambda array: array.reshape(tall, width)
    scalars = pl.BlockSpec(memory_space=pltpu.SMEM)
    anywhere = pl.BlockSpec(memory_space=pl.ANY)
    ct_tracer, kappa, kvert, land = (flat(a) for a in (ct_tracer, kappa, kvert, land))

    setup = pl.pallas_call(
        functools.partial(setup_body, levels),
        out_shape=[pltpu.VMEM(field, FLOAT)] + [pltpu.VMEM(tile, FLOAT)] * 8,
        in_specs=[scalars, anywhere] + in_vmem(3),
        out_specs=in_vmem(9),
        scratch_shapes=[pltpu.VMEM((tall, width), jnp.int32), pltpu.SemaphoreType.DMA((4,))],
        name="setup",
        compiler_params=pltpu.CompilerParams(vmem_limit_bytes=LIMIT),
    )
    wet, height, surface, s_fx, s_fn, s_dg, q1, to_next, to_previous = setup(layer_weight, land, kmt, ct_surface, screen)
    before, after = exchange(to_next, to_previous)

    kap, kv, source = held(kappa), held(kvert), held(ct_tracer)
    rim_up, rim_down = kernel(functools.partial(rims_body, levels), [rim, rim], in_vmem(2), "rims", [field])(kap, wet)
    rim_before, rim_after = exchange(rim_up, rim_down)

    b1, b2, sums = kernel(
        functools.partial(basis_body, count), [tile, tile, (8 * count, 128)], in_vmem(9), "basis"
    )(ct_surface, height, surface, s_fx, s_fn, s_dg, q1, before, after)
    sums = lax.all_to_all(sums.reshape(count, 8, 128), "tile", 0, 0, tiled=True).reshape(8 * count, 128)

    fx, fn = kernel(functools.partial(faces_body, levels), [field, field], in_vmem(2), "faces")(kap, wet)
    m0, w = kernel(
        functools.partial(columns_body, levels), [field, field], [scalars] + in_vmem(3), "columns", [field]
    )(layer_weight, source, kv, wet)

    solution, up, down = kernel(
        functools.partial(edges_body, levels, count), [tile, rim, rim], in_vmem(8), "edges"
    )(sums, ct_surface, b1, b2, m0, w, fx, fn)
    row_before, row_after = exchange(up, down)
    (u2,) = kernel(functools.partial(inner_body, levels), [field], in_vmem(5), "inner")(m0, w, solution, fx, fn)

    finish = pl.pallas_call(
        functools.partial(finish_body, levels),
        out_shape=jax.ShapeDtypeStruct((tall, width), FLOAT),
        in_specs=in_vmem(11),
        out_specs=anywhere,
        scratch_shapes=[pltpu.VMEM((rows, 8, width), FLOAT), pltpu.VMEM((tall, width), FLOAT), pltpu.SemaphoreType.DMA((levels // 8,))],
        name="finish",
        compiler_params=pltpu.CompilerParams(vmem_limit_bytes=LIMIT),
    )
    values = finish(u2, fx, fn, up, down, rim_up, rim_down, row_before, row_after, rim_before, rim_after)
    return (values.reshape(levels, rows, width), solution)


def solution(mesh):
    in_specs = (
        P(None, ("grp", "tile"), None),
        P(("grp", "tile"), None),
        P(None, "tile", None),
        P(None, "tile", None),
        P(None, "tile", None),
        P("tile", None),
        P("tile", None),
        P(),
    )
    out_specs = (P(None, ("grp", "tile"), None), P(("grp", "tile"), None))
    return jax.shard_map(body, mesh=mesh, in_specs=in_specs, out_specs=out_specs, check_vma=False)
```

```python
import functools

import jax
import jax.numpy as jnp
from jax import lax
from jax.experimental import pallas as pl
from jax.experimental.pallas import tpu as pltpu
from jax.sharding import PartitionSpec as P

ITERS = 3
ROWS = 8
LOW = 0.05
HIGH = 9.0
MID = 0.5 * (HIGH + LOW)
HALF = 0.5 * (HIGH - LOW)
FLOAT = jnp.float32
RIM = 12
LIMIT = 24 * 1024 * 1024


def east(values):
    return pltpu.roll(values, values.shape[1] - 1, 1)


def west(values):
    return pltpu.roll(values, 1, 1)


def north(values):
    return pltpu.roll(values, values.shape[0] - 1, 0)


def south(values):
    return pltpu.roll(values, 1, 0)


def stacked(values):
    return jnp.concatenate([values[:, i : i + 128] for i in range(0, values.shape[1], 128)], axis=0)


def unstacked(values):
    return jnp.concatenate([values[i : i + ROWS, :] for i in range(0, values.shape[0], ROWS)], axis=1)


def row_of(ref, block, row, width):
    tall = width // 128 * ROWS
    return jnp.concatenate(
        [ref[pl.ds(block * 8 * tall + j * ROWS + row, 8, stride=tall), :] for j in range(width // 128)], axis=1
    )


def level_at(k, width):
    tall = width // 128 * ROWS
    return pl.ds(pl.multiple_of(k * tall, tall), tall)


def rows_at(k):
    return pl.ds(pl.multiple_of(k * ROWS, ROWS), ROWS)


def row_index(values):
    return lax.broadcasted_iota(jnp.int32, values.shape, 0)


def spread(row, like):
    return jnp.broadcast_to(row, like.shape)


def vmem(*shapes):
    return [pltpu.VMEM(shape, FLOAT) for shape in shapes]


def hbm(*shapes):
    return [pltpu.HBM(shape, FLOAT) for shape in shapes]


def in_vmem(count):
    return [pl.BlockSpec(memory_space=pltpu.VMEM)] * count


def in_hbm(count):
    return [pl.BlockSpec(memory_space=pltpu.HBM)] * count


def kernel(body, outs, ins, out_specs, name, scratch=(), cost=1000000):
    return pl.pallas_call(
        body,
        out_shape=outs,
        in_specs=ins,
        out_specs=out_specs,
        scratch_shapes=list(scratch),
        name=name,
        cost_estimate=pl.CostEstimate(flops=cost, bytes_accessed=cost, transcendentals=0),
        compiler_params=pltpu.CompilerParams(vmem_limit_bytes=LIMIT),
    )


def held(array):
    return pltpu.with_memory_space_constraint(array, pltpu.VMEM)


def left(array):
    return pltpu.with_memory_space_constraint(array, pltpu.HBM)


def is_even():
    return lax.rem(lax.axis_index("tile"), 2) == 0


def dealt(even, low, high):
    return jnp.where(even, high, low), jnp.where(even, low, high)


def setup_body(levels, weight, land, kmt_hbm, ct_hbm, screen_hbm, wet_ref, height_ref, surface_ref,
               fx_ref, fn_ref, dg_ref, q1_ref, base_ref, near_ref, far_ref, buffer, kmt, screen, sems):
    chunk = levels // 4
    small = [
        pltpu.make_async_copy(source, target, sems.at[4 + i])
        for i, (source, target) in enumerate(((kmt_hbm, kmt), (ct_hbm, base_ref), (screen_hbm, screen)))
    ]
    copies = []
    for i in range(4):
        whole = pl.ds(i * chunk * ROWS, chunk * ROWS)
        copies.append(pltpu.make_async_copy(land.at[whole], buffer.at[whole], sems.at[i]))
    for copy in small[:1] + copies + small[1:]:
        copy.start()
    total = weight[0]
    for k in range(1, levels):
        total = total + weight[k]
    small[0].wait()
    depth = kmt[...]
    height = jnp.zeros(depth.shape, FLOAT)
    for i, copy in enumerate(copies):
        copy.wait()

        def level(k, height):
            wet = jnp.where(k < depth, buffer[rows_at(k), :], 0).astype(FLOAT)
            wet_ref[level_at(k, depth.shape[1]), :] = stacked(wet)
            return height + weight[k] * wet

        height = lax.fori_loop(i * chunk, (i + 1) * chunk, level, height, unroll=4)
    height = height / total
    surface = jnp.where(0 < depth, buffer[0:ROWS, :], 0).astype(FLOAT)
    height_ref[...] = height
    surface_ref[...] = surface
    small[1].wait()
    small[2].wait()
    base = base_ref[...]
    rows = row_index(base)
    scale = 0.5 / HALF
    fx = scale * (height + east(height)) * surface * east(surface)
    fn = scale * (height + north(height)) * surface * north(surface)
    fn = jnp.where(rows < ROWS - 1, fn, 0.0)
    fs = south(fn)
    fw = west(fx)
    dg = (screen[...] - MID) * (1.0 / HALF) + fx + fw + fn + fs

    def apply(v):
        return dg * v - fx * east(v) - fw * west(v) - fn * north(v) - fs * south(v)

    q1 = apply(base)
    q2 = apply(q1)
    fx_ref[...] = fx
    fn_ref[...] = fn
    dg_ref[...] = dg
    q1_ref[...] = q1
    even = is_even()
    near_ref[7:8, :] = jnp.zeros_like(base[0:1, :])
    far_ref[7:8, :] = jnp.zeros_like(base[0:1, :])
    for place, values in enumerate((base, q1, q2, fx, dg, height, surface)):
        at = slice(place, place + 1)
        near_ref[at, :], far_ref[at, :] = dealt(even, values[0:1, :], values[ROWS - 1 : ROWS, :])


def basis_body(count, ct, height, surface, fx_ref, fn_ref, dg_ref, q1_ref, near, far, basis_ref, sums_ref):
    even = is_even()
    b0 = ct[...]
    rows = row_index(b0)
    first, last = rows == 0, rows == ROWS - 1
    fx, fn, dg = fx_ref[...], fn_ref[...], dg_ref[...]
    fw, fs = west(fx), south(fn)

    def halo(values, row):
        b0_h, q1_h, q2_h, fx_h, dg_h, high_h, wet_h = (values[i : i + 1, :] for i in range(7))
        face = (0.5 / HALF) * (high_h + height[row : row + 1, :]) * wet_h * surface[row : row + 1, :]
        extra = face * (b0_h - ct[row : row + 1, :])
        return b0_h, q1_h + extra, q2_h, fx_h, dg_h, face, extra

    def lift(row):
        return jnp.broadcast_to(row, b0.shape)

    before, after = dealt(even, near[...], far[...])
    sides = (halo(before, 0), halo(after, ROWS - 1))
    face_b, face_a = lift(sides[0][5]), lift(sides[1][5])
    b1 = q1_ref[...] - jnp.where(first, lift(sides[0][6]), 0.0) - jnp.where(last, lift(sides[1][6]), 0.0)
    dg = dg + jnp.where(first, face_b, 0.0) + jnp.where(last, face_a, 0.0)
    fn = jnp.where(last, face_a, fn)
    fs = jnp.where(first, face_b, fs)

    def apply(v, v_before, v_after):
        v_n = jnp.where(last, lift(v_after), north(v))
        v_s = jnp.where(first, lift(v_before), south(v))
        return dg * v - fx * east(v) - fw * west(v) - fn * v_n - fs * v_s

    b2 = 2.0 * apply(b1, sides[0][1], sides[1][1]) - b0

    def outer(side, own):
        b0_h, b1_h, q2_h, fx_h, dg_h, face, extra = side
        b0_h, b1_h, q2_h, fx_h, dg_h, face, extra, own = (lift(v) for v in (b0_h, b1_h, q2_h, fx_h, dg_h, face, extra, own))
        turned = dg_h * extra - fx_h * east(extra) - west(fx_h) * west(extra)
        return (2.0 * (q2_h + turned + face * (b1_h - own)) - b0_h)[0:1, :]

    b2_b = outer(sides[0], b1[0:1, :])
    b2_a = outer(sides[1], b1[ROWS - 1 : ROWS, :])
    next2 = apply(b2, b2_b, b2_a)
    for place, values in enumerate((b0, b1, b2)):
        basis_ref[place * ROWS : (place + 1) * ROWS, :] = values
    tile_rows = lax.broadcasted_iota(jnp.int32, (8, 128), 0)
    packed = jnp.zeros((8, 128), FLOAT)
    for place, (p, q) in enumerate(((b0, b0), (b0, b1), (b1, b1), (b1, b2), (b2, b2), (b2, next2))):
        product = p * q
        folded = product[:, 0:128]
        for j in range(1, product.shape[1] // 128):
            folded = folded + product[:, j * 128 : (j + 1) * 128]
        packed = jnp.where(tile_rows == place, jnp.sum(folded, axis=0, keepdims=True), packed)
    for j in range(count):
        sums_ref[j * 8 : (j + 1) * 8, :] = packed


def quadratic(left, form):
    total = None
    for i in range(3):
        for j in range(3):
            if left[i] is not None and left[j] is not None:
                term = left[i] * left[j] * form[i][j]
                total = term if total is None else total + term
    return total


def plus(p, q):
    return q if p is None else p if q is None else p + q


def times(scale, p):
    return None if p is None else scale * p


def weights(sums):
    s0, s1, s2, s3, s4, s5 = sums
    g02 = 2.0 * s2 - s0
    gram = ((s0, s1, g02), (s1, s2, s3), (g02, s3, s4))
    b11, b12 = 0.5 * (s3 + s1), 0.5 * (s4 + g02)
    shift = ((s1, s2, s3), (s2, b11, b12), (s3, b12, s5))
    form = [[MID * gram[i][j] + HALF * shift[i][j] for j in range(3)] for i in range(3)]
    one = jnp.ones_like(s0)
    x, r, d = [None] * 3, [one, None, None], [one, None, None]
    rr = s0
    for step in range(ITERS):
        alpha = jnp.clip(rr / quadratic(d, form), 1.0 / HIGH, 1.0 / LOW)
        x = [plus(x[i], times(alpha, d[i])) for i in range(3)]
        if step + 1 < ITERS:
            image = [
                plus(times(MID, d[0]), times(0.5 * HALF, d[1])),
                plus(plus(times(MID, d[1]), times(HALF, d[0])), times(0.5 * HALF, d[2])),
                plus(times(MID, d[2]), times(0.5 * HALF, d[1])),
            ]
            r = [plus(r[i], times(-1.0, times(alpha, image[i]))) for i in range(3)]
            new = quadratic(r, gram)
            beta = jnp.clip(new / rr, 0.0, HIGH / LOW)
            d = [plus(r[i], times(beta, d[i])) for i in range(3)]
            rr = new
    return x


def edges_body(levels, count, sums, basis_ref, rim_hbm, out_hbm, s_ref, near_ref, far_ref, rims, sems):
    blocks = levels // 8
    copies = []
    for block in range(blocks):
        whole = pl.ds(block * RIM * 8, RIM * 8)
        copies.append(pltpu.make_async_copy(rim_hbm.at[whole], rims.at[whole], sems.at[block]))
    for copy in copies:
        copy.start()
    total = sums[0:8, :]
    for j in range(1, count):
        total = total + sums[j * 8 : (j + 1) * 8, :]
    total = jnp.sum(total, axis=1, keepdims=True)
    mix = weights([total[i : i + 1, :] for i in range(6)])
    b0, b1, b2 = (basis_ref[i * ROWS : (i + 1) * ROWS, :] for i in range(3))
    s = mix[0] * b0 + mix[1] * b1 + mix[2] * b2
    s_ref[...] = s
    copy_s = pltpu.make_async_copy(s_ref, out_hbm, sems.at[blocks])
    copy_s.start()
    s_rows = {r: spread(s[r : r + 1, :], s) for r in (0, 1, ROWS - 2, ROWS - 1)}
    even = is_even()

    for block, copy in enumerate(copies):
        copy.wait()
        found = []
        for side, row, inner in ((0, 0, 1), (1, ROWS - 1, ROWS - 2)):
            m, gm, w, q, face, link = (
                rims[pl.ds((block * RIM + side * 6 + i) * 8, 8), :] for i in range(6)
            )
            v = s_rows[row] * w
            flux = face * (east(v) - v)
            found.append((m + v, gm + v + (flux - west(flux)) - link * v + s_rows[inner] * q))
        for place in range(2):
            at = pl.ds(place * levels + block * 8, 8)
            near_ref[at, :], far_ref[at, :] = dealt(even, found[0][place], found[1][place])
    copy_s.wait()


def columns_body(levels, weight, source_hbm, kvert_hbm, kappa_hbm, wet, m0_hbm, w_hbm, rim_hbm, near_ref, far_ref,
                 source, kvert, kappa, m0, w, ratio, bricks, rims, in_sems, out_sems):
    width = source.shape[1]
    parts = 4
    chunk = levels // parts
    ins = []
    for i in range(parts):
        whole = pl.ds(i * chunk * ROWS, chunk * ROWS)
        for a, (far, near) in enumerate(((source_hbm, source), (kvert_hbm, kvert), (kappa_hbm, kappa))):
            ins.append(pltpu.make_async_copy(far.at[whole], near.at[whole], in_sems.at[i * 3 + a]))
    for copy in [ins[i * 3 + a] for i in range(parts) for a in (0, 1)] + ins[2::3]:
        copy.start()
    total = weight[0]
    for k in range(1, levels):
        total = total + weight[k]
    shape = (ROWS * width // 128, 128)
    inverse = 1.0 / jnp.full(shape, total, FLOAT)

    def down(k, carry):
        link, m_in, w_in = carry
        at = level_at(k, width)
        here = wet[at, :]
        below = jnp.where(k + 1 < levels, wet[level_at(jnp.minimum(k + 1, levels - 1), width), :], 0.0)
        coupling = stacked(kvert[rows_at(k), :]) * here * below
        over = 1.0 / (1.0 + coupling + link)
        m_here = (stacked(source[rows_at(k), :]) + m_in) * over
        w_here = (here * (weight[k] * inverse) + w_in) * over
        part = coupling * over
        ratio[at, :] = part
        m0[at, :] = m_here
        w[at, :] = w_here
        return coupling - coupling * part, coupling * m_here, coupling * w_here

    zero = jnp.zeros(shape, FLOAT)
    carry = (zero, zero, zero)
    for i in range(parts):
        ins[i * 3].wait()
        ins[i * 3 + 1].wait()
        carry = lax.fori_loop(i * chunk, (i + 1) * chunk, down, carry)

    def up(i, carry):
        at = level_at(levels - 1 - i, width)
        m_below, w_below = carry
        part = ratio[at, :]
        m_here = m0[at, :] + part * m_below
        w_here = w[at, :] + part * w_below
        m0[at, :] = m_here
        w[at, :] = w_here
        return m_here, w_here

    carry = (zero, zero)
    outs = []
    for i in range(parts):
        carry = lax.fori_loop(i * chunk, (i + 1) * chunk, up, carry)
        size = chunk * shape[0]
        whole = pl.ds((parts - 1 - i) * size, size)
        for a, (near, far) in enumerate(((m0, m0_hbm), (w, w_hbm))):
            copy = pltpu.make_async_copy(near.at[whole], far.at[whole], out_sems.at[i * 2 + a])
            copy.start()
            outs.append(copy)
    for i in range(parts):
        ins[i * 3 + 2].wait()

    def brick(k, carry):
        bricks[level_at(k, width), :] = stacked(kappa[rows_at(k), :])
        return carry

    lax.fori_loop(0, levels, brick, 0, unroll=4)
    even = is_even()
    for block in range(levels // 8):
        found = []
        for side, row, inner in ((0, 0, 1), (1, ROWS - 1, ROWS - 2)):
            kap, kap_in = row_of(bricks, block, row, width), row_of(bricks, block, inner, width)
            here, here_in = row_of(wet, block, row, width), row_of(wet, block, inner, width)
            m, w_row = row_of(m0, block, row, width), row_of(w, block, row, width)
            face = 0.5 * (kap + east(kap)) * here * east(here)
            link = 0.5 * (kap + kap_in) * here * here_in
            flux = face * (east(m) - m)
            gm = m + (flux - west(flux)) + link * (row_of(m0, block, inner, width) - m)
            q = link * row_of(w, block, inner, width)
            for i, values in enumerate((m, gm, w_row, q, face, link)):
                rims[pl.ds((block * RIM + side * 6 + i) * 8, 8), :] = values
            found.append((kap, here))
        for place in range(2):
            at = pl.ds(place * levels + block * 8, 8)
            near_ref[at, :], far_ref[at, :] = dealt(even, found[0][place], found[1][place])
        whole = pl.ds(block * RIM * 8, RIM * 8)
        copy = pltpu.make_async_copy(rims.at[whole], rim_hbm.at[whole], out_sems.at[2 * parts + block])
        copy.start()
        outs.append(copy)
    for copy in outs:
        copy.wait()


def inner_body(levels, kmt, s_ref, m0, w, kappa, land, u2_ref):
    s = s_ref[...]
    depth = kmt[...]
    inside = row_index(s) < ROWS - 1

    def face(here, there):
        return jnp.where(jnp.minimum(here, there) > 0.0, here + there, 0.0)

    def level(k):
        at = rows_at(k)
        sea = jnp.where(k < depth, land[at, :], 0) > 0
        half = jnp.where(sea, 0.5 * kappa[at, :], 0.0)
        fx = face(half, east(half))
        fn = jnp.where(inside, face(half, north(half)), 0.0)
        fw, fs = west(fx), south(fn)
        keep = 1.0 - (fx + fw) - (fn + fs)
        brick = level_at(k, s.shape[1])
        u = unstacked(m0[brick, :]) + s * unstacked(w[brick, :])
        for _ in range(2):
            u = keep * u + (fx * east(u) + fw * west(u)) + (fn * north(u) + fs * south(u))
        return u

    def group(i, carry):
        for values, k in [(level(2 * i + j), 2 * i + j) for j in range(2)]:
            u2_ref[rows_at(k), :] = values
        return carry

    lax.fori_loop(0, levels // 2, group, 0)


def finish_body(levels, u2, rims, own_near, own_far, rim_near, rim_far, near, far, rim_other_near, rim_other_far,
                out, change_ref, buffer, sems):
    width = own_near.shape[1]
    tall = width // 128 * ROWS
    rows = lax.broadcasted_iota(jnp.int32, (ROWS, width), 0)
    on_rim = (rows < 2) | (rows >= ROWS - 2)
    even = is_even()
    copies = []
    for block in range(levels // 8):
        at, below = pl.ds(block * 8, 8), pl.ds(levels + block * 8, 8)

        def pairs(a, b):
            return [dealt(even, a[part, :], b[part, :]) for part in (at, below)]

        own, rim = pairs(own_near, own_far), pairs(rim_near, rim_far)
        other, rim_other = pairs(near, far), pairs(rim_other_near, rim_other_far)
        for side, row, inner in ((0, 0, 1), (1, ROWS - 1, ROWS - 2)):
            face = 0.5 * (rim[0][side] + rim_other[0][side]) * rim[1][side] * rim_other[1][side]
            change = face * (other[0][side] - own[0][side])
            along, link = (rims[pl.ds((block * RIM + side * 6 + i) * 8, 8), :] for i in (4, 5))
            flux = along * (east(change) - change)
            passed = link * change
            on_row = (change + (flux - west(flux)) - passed
                      + face * (other[1][side] - own[1][side] - 2.0 * change))
            for j in range(width // 128):
                lanes = slice(j * 128, (j + 1) * 128)
                change_ref[pl.ds(j * ROWS + row, 8, stride=tall), :] = on_row[:, lanes]
                change_ref[pl.ds(j * ROWS + inner, 8, stride=tall), :] = passed[:, lanes]
        for k in range(8):
            level = block * 8 + k
            change = jnp.where(on_rim, unstacked(change_ref[level_at(k, width), :]), 0.0)
            buffer[rows_at(level), :] = u2[rows_at(level), :] + change
        whole = pl.ds(block * 8 * ROWS, 8 * ROWS)
        copy = pltpu.make_async_copy(buffer.at[whole], out.at[whole], sems.at[block])
        copy.start()
        copies.append(copy)
    for copy in copies:
        copy.wait()


def exchange(to_near, to_far):
    count = lax.axis_size("tile")

    def swap(array, start):
        firsts = range(start, count - 1, 2)
        return lax.ppermute(array, "tile", [(i, i + 1) for i in firsts] + [(i + 1, i) for i in firsts])

    from_far = swap(to_far, 1)
    return swap(to_near, 0), from_far


def body(ct_tracer, ct_surface, kappa, kvert, land, kmt, screen, layer_weight):
    levels, rows, width = ct_tracer.shape
    count = lax.axis_size("tile")
    tall = levels * rows
    tile, brick, flat = (rows, width), (tall * width // 128, 128), (tall, width)
    rim, rim_rows = (2 * levels, width), (levels * RIM, width)
    scalars = [pl.BlockSpec(memory_space=pltpu.SMEM)]
    ct_tracer, kappa, kvert, land = (a.reshape(flat) for a in (ct_tracer, kappa, kvert, land))
    semaphores = pltpu.SemaphoreType.DMA

    wet, height, surface, s_fx, s_fn, s_dg, q1, base, to_near, to_far = kernel(
        functools.partial(setup_body, levels), vmem(brick, *[tile] * 9), scalars + in_hbm(4), in_vmem(10), "setup",
        [pltpu.VMEM(flat, jnp.int32), pltpu.VMEM(tile, jnp.int32), pltpu.VMEM(tile, FLOAT), semaphores((7,))],
    )(layer_weight, left(land), left(kmt), left(ct_surface), left(screen))
    near, far = exchange(to_near, to_far)

    fields = [pltpu.VMEM(flat, FLOAT)] * 3 + [pltpu.VMEM(brick, FLOAT)] * 4 + [pltpu.VMEM(rim_rows, FLOAT)]
    m0, w, rims, rim_near, rim_far = kernel(
        functools.partial(columns_body, levels), hbm(brick, brick, rim_rows) + vmem(rim, rim),
        scalars + in_hbm(3) + in_vmem(1), in_hbm(3) + in_vmem(2), "columns",
        fields + [semaphores((12,)), semaphores((8 + levels // 8,))],
    )(layer_weight, left(ct_tracer), left(kvert), left(kappa), wet)

    basis, sums = kernel(
        functools.partial(basis_body, count), vmem((3 * rows, width), (8 * count, 128)), in_vmem(9), in_vmem(2), "basis"
    )(base, height, surface, s_fx, s_fn, s_dg, q1, near, far)
    sums = lax.all_to_all(sums.reshape(count, 8, 128), "tile", 0, 0, tiled=True).reshape(8 * count, 128)
    rim_other_near, rim_other_far = exchange(rim_near, rim_far)

    solution, s, row_near, row_far = kernel(
        functools.partial(edges_body, levels, count), hbm(tile) + vmem(tile, rim, rim),
        in_vmem(2) + in_hbm(1), in_hbm(1) + in_vmem(3), "edges",
        [pltpu.VMEM(rim_rows, FLOAT), semaphores((levels // 8 + 1,))],
    )(sums, basis, left(rims))
    other_near, other_far = exchange(row_near, row_far)
    u2 = kernel(
        functools.partial(inner_body, levels), vmem(flat), in_vmem(6), in_vmem(1), "inner"
    )(held(kmt), s, held(m0), held(w), held(kappa), held(land))[0]

    values = kernel(
        functools.partial(finish_body, levels), hbm(flat), in_vmem(10), in_hbm(1), "finish",
        [pltpu.VMEM((8 * rows * width // 128, 128), FLOAT), pltpu.VMEM(flat, FLOAT), semaphores((levels // 8,))],
    )(u2, held(rims), row_near, row_far, rim_near, rim_far, other_near, other_far, rim_other_near, rim_other_far)[0]
    return (values.reshape(levels, rows, width), solution)


def solution(mesh):
    in_specs = (
        P(None, ("grp", "tile"), None),
        P(("grp", "tile"), None),
        P(None, "tile", None),
        P(None, "tile", None),
        P(None, "tile", None),
        P("tile", None),
        P("tile", None),
        P(),
    )
    out_specs = (P(None, ("grp", "tile"), None), P(("grp", "tile"), None))
    return jax.shard_map(body, mesh=mesh, in_specs=in_specs, out_specs=out_specs, check_vma=False)
```

```python
import functools

import jax
import jax.numpy as jnp
from jax import lax
from jax.experimental import pallas as pl
from jax.experimental.pallas import tpu as pltpu
from jax.sharding import PartitionSpec as P

ITERS = 3
ROWS = 8
LOW = 0.05
HIGH = 9.0
MID = 0.5 * (HIGH + LOW)
HALF = 0.5 * (HIGH - LOW)
FLOAT = jnp.float32
RIM = 8
LINKS = 4
LIMIT = 24 * 1024 * 1024


def east(values):
    return pltpu.roll(values, values.shape[1] - 1, 1)


def west(values):
    return pltpu.roll(values, 1, 1)


def north(values):
    return pltpu.roll(values, values.shape[0] - 1, 0)


def south(values):
    return pltpu.roll(values, 1, 0)


def stacked(values):
    return jnp.concatenate([values[:, i : i + 128] for i in range(0, values.shape[1], 128)], axis=0)


def unstacked(values):
    return jnp.concatenate([values[i : i + ROWS, :] for i in range(0, values.shape[0], ROWS)], axis=1)


def row_of(ref, block, row, width):
    tall = width // 128 * ROWS
    return jnp.concatenate(
        [ref[pl.ds(block * 8 * tall + j * ROWS + row, 8, stride=tall), :] for j in range(width // 128)], axis=1
    )


def level_at(k, width):
    tall = width // 128 * ROWS
    return pl.ds(pl.multiple_of(k * tall, tall), tall)


def rows_at(k):
    return pl.ds(pl.multiple_of(k * ROWS, ROWS), ROWS)


def row_index(values):
    return lax.broadcasted_iota(jnp.int32, values.shape, 0)


def spread(row, like):
    return jnp.broadcast_to(row, like.shape)


def vmem(*shapes):
    return [pltpu.VMEM(shape, FLOAT) for shape in shapes]


def hbm(*shapes):
    return [pltpu.HBM(shape, FLOAT) for shape in shapes]


def in_vmem(count):
    return [pl.BlockSpec(memory_space=pltpu.VMEM)] * count


def in_hbm(count):
    return [pl.BlockSpec(memory_space=pltpu.HBM)] * count


def kernel(body, outs, ins, out_specs, name, scratch=(), cost=1000000):
    return pl.pallas_call(
        body,
        out_shape=outs,
        in_specs=ins,
        out_specs=out_specs,
        scratch_shapes=list(scratch),
        name=name,
        cost_estimate=pl.CostEstimate(flops=cost, bytes_accessed=cost, transcendentals=0),
        compiler_params=pltpu.CompilerParams(vmem_limit_bytes=LIMIT),
    )


def held(array):
    return pltpu.with_memory_space_constraint(array, pltpu.VMEM)


def left(array):
    return pltpu.with_memory_space_constraint(array, pltpu.HBM)


def is_even():
    return lax.rem(lax.axis_index("tile"), 2) == 0


def dealt(even, low, high):
    return jnp.where(even, high, low), jnp.where(even, low, high)


def loads(pairs, sems, first=0):
    copies = [pltpu.make_async_copy(far, near, sems.at[first + i]) for i, (far, near) in enumerate(pairs)]
    for copy in copies:
        copy.start()
    return copies


def in_parts(far, near, parts):
    size = far.shape[0] // parts
    return [(far.at[pl.ds(i * size, size)], near.at[pl.ds(i * size, size)]) for i in range(parts)]


def weight_sum(weight, levels):
    total = weight[0]
    for k in range(1, levels):
        total = total + weight[k]
    return total


def setup_body(levels, weight_hbm, land_hbm, kmt_hbm, ct_hbm, screen_hbm, kappa_hbm, height_ref, surface_ref,
               fx_ref, fn_ref, dg_ref, q1_ref, base_ref, near_ref, far_ref, rim_near_ref, rim_far_ref, links_hbm,
               weight, land, kmt, screen, kappa, wet_bricks, kappa_bricks, links, sems, out_sems):
    chunk = levels // 4
    small = loads(((weight_hbm, weight), (kmt_hbm, kmt)), sems)
    land_copies = loads(in_parts(land_hbm, land, 4), sems, 2)
    small += loads(((ct_hbm, base_ref), (screen_hbm, screen)), sems, 6)
    kappa_copies = loads(in_parts(kappa_hbm, kappa, 4), sems, 8)
    small[0].wait()
    total = weight_sum(weight, levels)
    small[1].wait()
    depth = kmt[...]
    width = depth.shape[1]
    height = jnp.zeros(depth.shape, FLOAT)
    for i, copy in enumerate(land_copies):
        copy.wait()

        def level(k, height):
            wet = jnp.where(k < depth, land[rows_at(k), :], 0).astype(FLOAT)
            wet_bricks[level_at(k, width), :] = stacked(wet)
            return height + weight[k] * wet

        height = lax.fori_loop(i * chunk, (i + 1) * chunk, level, height, unroll=4)
    height = height / total
    surface = jnp.where(0 < depth, land[0:ROWS, :], 0).astype(FLOAT)
    height_ref[...] = height
    surface_ref[...] = surface
    small[2].wait()
    small[3].wait()
    base = base_ref[...]
    rows = row_index(base)
    scale = 0.5 / HALF
    fx = scale * (height + east(height)) * surface * east(surface)
    fn = scale * (height + north(height)) * surface * north(surface)
    fn = jnp.where(rows < ROWS - 1, fn, 0.0)
    fs = south(fn)
    fw = west(fx)
    dg = (screen[...] - MID) * (1.0 / HALF) + fx + fw + fn + fs

    def apply(v):
        return dg * v - fx * east(v) - fw * west(v) - fn * north(v) - fs * south(v)

    q1 = apply(base)
    q2 = apply(q1)
    fx_ref[...] = fx
    fn_ref[...] = fn
    dg_ref[...] = dg
    q1_ref[...] = q1
    even = is_even()
    near_ref[7:8, :] = jnp.zeros_like(base[0:1, :])
    far_ref[7:8, :] = jnp.zeros_like(base[0:1, :])
    for place, values in enumerate((base, q1, q2, fx, dg, height, surface)):
        at = slice(place, place + 1)
        near_ref[at, :], far_ref[at, :] = dealt(even, values[0:1, :], values[ROWS - 1 : ROWS, :])

    for i, copy in enumerate(kappa_copies):
        copy.wait()

        def brick(k, carry):
            kappa_bricks[level_at(k, width), :] = stacked(kappa[rows_at(k), :])
            return carry

        lax.fori_loop(i * chunk, (i + 1) * chunk, brick, 0, unroll=4)
    for block in range(levels // 8):
        found = []
        for side, row, inner in ((0, 0, 1), (1, ROWS - 1, ROWS - 2)):
            kap, kap_in = row_of(kappa_bricks, block, row, width), row_of(kappa_bricks, block, inner, width)
            here, here_in = row_of(wet_bricks, block, row, width), row_of(wet_bricks, block, inner, width)
            at = (block * LINKS + side * 2) * 8
            links[pl.ds(at, 8), :] = 0.5 * (kap + east(kap)) * here * east(here)
            links[pl.ds(at + 8, 8), :] = 0.5 * (kap + kap_in) * here * here_in
            found.append((kap, here))
        for place in range(2):
            at = pl.ds(place * levels + block * 8, 8)
            rim_near_ref[at, :], rim_far_ref[at, :] = dealt(even, found[0][place], found[1][place])
    out = pltpu.make_async_copy(links, links_hbm, out_sems.at[0])
    out.start()
    out.wait()


def basis_body(count, ct, height, surface, fx_ref, fn_ref, dg_ref, q1_ref, near, far, basis_hbm, sums_ref, basis_ref, sems):
    even = is_even()
    b0 = ct[...]
    rows = row_index(b0)
    first, last = rows == 0, rows == ROWS - 1
    fx, fn, dg = fx_ref[...], fn_ref[...], dg_ref[...]
    fw, fs = west(fx), south(fn)

    def halo(values, row):
        b0_h, q1_h, q2_h, fx_h, dg_h, high_h, wet_h = (values[i : i + 1, :] for i in range(7))
        face = (0.5 / HALF) * (high_h + height[row : row + 1, :]) * wet_h * surface[row : row + 1, :]
        extra = face * (b0_h - ct[row : row + 1, :])
        return b0_h, q1_h + extra, q2_h, fx_h, dg_h, face, extra

    def lift(row):
        return jnp.broadcast_to(row, b0.shape)

    before, after = dealt(even, near[...], far[...])
    sides = (halo(before, 0), halo(after, ROWS - 1))
    face_b, face_a = lift(sides[0][5]), lift(sides[1][5])
    b1 = q1_ref[...] - jnp.where(first, lift(sides[0][6]), 0.0) - jnp.where(last, lift(sides[1][6]), 0.0)
    dg = dg + jnp.where(first, face_b, 0.0) + jnp.where(last, face_a, 0.0)
    fn = jnp.where(last, face_a, fn)
    fs = jnp.where(first, face_b, fs)

    def apply(v, v_before, v_after):
        v_n = jnp.where(last, lift(v_after), north(v))
        v_s = jnp.where(first, lift(v_before), south(v))
        return dg * v - fx * east(v) - fw * west(v) - fn * v_n - fs * v_s

    b2 = 2.0 * apply(b1, sides[0][1], sides[1][1]) - b0

    def outer(side, own):
        b0_h, b1_h, q2_h, fx_h, dg_h, face, extra = side
        b0_h, b1_h, q2_h, fx_h, dg_h, face, extra, own = (lift(v) for v in (b0_h, b1_h, q2_h, fx_h, dg_h, face, extra, own))
        turned = dg_h * extra - fx_h * east(extra) - west(fx_h) * west(extra)
        return (2.0 * (q2_h + turned + face * (b1_h - own)) - b0_h)[0:1, :]

    copies = []
    for place, values in enumerate((b0, b1, b2)):
        whole = pl.ds(place * ROWS, ROWS)
        basis_ref[whole, :] = values
        copies += loads([(basis_ref.at[whole], basis_hbm.at[whole])], sems, place)
    b2_b = outer(sides[0], b1[0:1, :])
    b2_a = outer(sides[1], b1[ROWS - 1 : ROWS, :])
    next2 = apply(b2, b2_b, b2_a)
    tile_rows = lax.broadcasted_iota(jnp.int32, (8, 128), 0)
    packed = jnp.zeros((8, 128), FLOAT)
    for place, (p, q) in enumerate(((b0, b0), (b0, b1), (b1, b1), (b1, b2), (b2, b2), (b2, next2))):
        product = p * q
        folded = product[:, 0:128]
        for j in range(1, product.shape[1] // 128):
            folded = folded + product[:, j * 128 : (j + 1) * 128]
        packed = jnp.where(tile_rows == place, jnp.sum(folded, axis=0, keepdims=True), packed)
    for j in range(count):
        sums_ref[j * 8 : (j + 1) * 8, :] = packed
    for copy in copies:
        copy.wait()


def quadratic(left, form):
    total = None
    for i in range(3):
        for j in range(3):
            if left[i] is not None and left[j] is not None:
                term = left[i] * left[j] * form[i][j]
                total = term if total is None else total + term
    return total


def plus(p, q):
    return q if p is None else p if q is None else p + q


def times(scale, p):
    return None if p is None else scale * p


def weights(sums):
    s0, s1, s2, s3, s4, s5 = sums
    g02 = 2.0 * s2 - s0
    gram = ((s0, s1, g02), (s1, s2, s3), (g02, s3, s4))
    b11, b12 = 0.5 * (s3 + s1), 0.5 * (s4 + g02)
    shift = ((s1, s2, s3), (s2, b11, b12), (s3, b12, s5))
    form = [[MID * gram[i][j] + HALF * shift[i][j] for j in range(3)] for i in range(3)]
    one = jnp.ones_like(s0)
    x, r, d = [None] * 3, [one, None, None], [one, None, None]
    rr = s0
    for step in range(ITERS):
        alpha = jnp.clip(rr / quadratic(d, form), 1.0 / HIGH, 1.0 / LOW)
        x = [plus(x[i], times(alpha, d[i])) for i in range(3)]
        if step + 1 < ITERS:
            image = [
                plus(times(MID, d[0]), times(0.5 * HALF, d[1])),
                plus(plus(times(MID, d[1]), times(HALF, d[0])), times(0.5 * HALF, d[2])),
                plus(times(MID, d[2]), times(0.5 * HALF, d[1])),
            ]
            r = [plus(r[i], times(-1.0, times(alpha, image[i]))) for i in range(3)]
            new = quadratic(r, gram)
            beta = jnp.clip(new / rr, 0.0, HIGH / LOW)
            d = [plus(r[i], times(beta, d[i])) for i in range(3)]
            rr = new
    return x


def edges_body(levels, count, sums, basis_hbm, rim_hbm, links_hbm, out_hbm, s_ref, near_ref, far_ref,
               basis_ref, rims, links, sems):
    blocks = levels // 8
    basis_copy = loads([(basis_hbm, basis_ref)], sems)[0]
    both = [pair for pairs in zip(in_parts(rim_hbm, rims, blocks), in_parts(links_hbm, links, blocks)) for pair in pairs]
    copies = loads(both, sems, 1)
    total = sums[0:8, :]
    for j in range(1, count):
        total = total + sums[j * 8 : (j + 1) * 8, :]
    total = jnp.sum(total, axis=1, keepdims=True)
    mix = weights([total[i : i + 1, :] for i in range(6)])
    basis_copy.wait()
    b0, b1, b2 = (basis_ref[i * ROWS : (i + 1) * ROWS, :] for i in range(3))
    s = mix[0] * b0 + mix[1] * b1 + mix[2] * b2
    s_ref[...] = s
    copy_s = loads([(s_ref, out_hbm)], sems, 2 * blocks + 1)[0]
    s_rows = {r: spread(s[r : r + 1, :], s) for r in (0, 1, ROWS - 2, ROWS - 1)}
    even = is_even()

    for block in range(blocks):
        copies[2 * block].wait()
        copies[2 * block + 1].wait()
        found = []
        for side, row, inner in ((0, 0, 1), (1, ROWS - 1, ROWS - 2)):
            m, gm, w, q = (rims[pl.ds((block * RIM + side * 4 + i) * 8, 8), :] for i in range(4))
            face, link = (links[pl.ds((block * LINKS + side * 2 + i) * 8, 8), :] for i in range(2))
            v = s_rows[row] * w
            flux = face * (east(v) - v)
            found.append((m + v, gm + v + (flux - west(flux)) - link * v + s_rows[inner] * q))
        for place in range(2):
            at = pl.ds(place * levels + block * 8, 8)
            near_ref[at, :], far_ref[at, :] = dealt(even, found[0][place], found[1][place])
    copy_s.wait()


def columns_body(levels, weight_hbm, kmt_hbm, source_hbm, kvert_hbm, land_hbm, links_hbm, m0_hbm, w_hbm, rim_hbm,
                 weight, kmt, source, kvert, land, links, m0, w, ratio, rims, in_sems, out_sems):
    width = source.shape[1]
    parts = 4
    chunk = levels // parts
    small = loads(((weight_hbm, weight), (kmt_hbm, kmt)), in_sems)
    parted = [in_parts(far, near, parts) for far, near in ((land_hbm, land), (kvert_hbm, kvert), (source_hbm, source))]
    big = loads([pairs[i] for i in range(parts) for pairs in parted], in_sems, 2)
    links_copy = loads([(links_hbm, links)], in_sems, 2 + 3 * parts)[0]
    small[0].wait()
    total = weight_sum(weight, levels)
    shape = (ROWS * width // 128, 128)
    inverse = 1.0 / jnp.full(shape, total, FLOAT)
    small[1].wait()
    depth = stacked(kmt[...])

    def sea(k):
        return jnp.where(k < depth, stacked(land[rows_at(k), :]), 0).astype(FLOAT)

    def down(k, carry):
        here, link, m_in, w_in = carry
        at = level_at(k, width)
        below = jnp.where(k + 1 < levels, sea(jnp.minimum(k + 1, levels - 1)), 0.0)
        coupling = stacked(kvert[rows_at(k), :]) * here * below
        over = 1.0 / (1.0 + coupling + link)
        m_here = (stacked(source[rows_at(k), :]) + m_in) * over
        w_here = (here * (weight[k] * inverse) + w_in) * over
        part = coupling * over
        ratio[at, :] = part
        m0[at, :] = m_here
        w[at, :] = w_here
        return below, coupling - coupling * part, coupling * m_here, coupling * w_here

    zero = jnp.zeros(shape, FLOAT)
    big[0].wait()
    carry = (sea(0), zero, zero, zero)
    for i in range(parts):
        big[3 * i + 1].wait()
        big[3 * i + 2].wait()
        if i + 1 < parts:
            big[3 * i + 3].wait()
        carry = lax.fori_loop(i * chunk, (i + 1) * chunk, down, carry)

    def up(i, carry):
        at = level_at(levels - 1 - i, width)
        m_below, w_below = carry
        part = ratio[at, :]
        m_here = m0[at, :] + part * m_below
        w_here = w[at, :] + part * w_below
        m0[at, :] = m_here
        w[at, :] = w_here
        return m_here, w_here

    carry = (zero, zero)
    outs = []
    for i in range(parts):
        carry = lax.fori_loop(i * chunk, (i + 1) * chunk, up, carry)
        size = chunk * shape[0]
        whole = pl.ds((parts - 1 - i) * size, size)
        for a, (near, far) in enumerate(((m0, m0_hbm), (w, w_hbm))):
            copy = pltpu.make_async_copy(near.at[whole], far.at[whole], out_sems.at[i * 2 + a])
            copy.start()
            outs.append(copy)
    links_copy.wait()
    for block in range(levels // 8):
        for side, row, inner in ((0, 0, 1), (1, ROWS - 1, ROWS - 2)):
            m, w_row = row_of(m0, block, row, width), row_of(w, block, row, width)
            face, link = (links[pl.ds((block * LINKS + side * 2 + i) * 8, 8), :] for i in range(2))
            flux = face * (east(m) - m)
            gm = m + (flux - west(flux)) + link * (row_of(m0, block, inner, width) - m)
            q = link * row_of(w, block, inner, width)
            for i, values in enumerate((m, gm, w_row, q)):
                rims[pl.ds((block * RIM + side * 4 + i) * 8, 8), :] = values
        whole = pl.ds(block * RIM * 8, RIM * 8)
        outs += loads([(rims.at[whole], rim_hbm.at[whole])], out_sems, 2 * parts + block)
    for copy in outs:
        copy.wait()


def inner_body(levels, s_ref, kmt_hbm, m0_hbm, w_hbm, kappa_hbm, land_hbm, u2_ref, kmt, m0, w, kappa, land, sems):
    parts = 4
    kmt_copy = loads([(kmt_hbm, kmt)], sems)[0]
    pairs = ((kappa_hbm, kappa), (land_hbm, land), (m0_hbm, m0), (w_hbm, w))
    parted = [in_parts(far, near, parts) for far, near in pairs]
    copies = loads([pairs[i] for i in range(parts) for pairs in parted], sems, 1)
    s = s_ref[...]
    kmt_copy.wait()
    depth = kmt[...]
    inside = row_index(s) < ROWS - 1

    def face(here, there):
        return jnp.where(jnp.minimum(here, there) > 0.0, here + there, 0.0)

    def level(k):
        at = rows_at(k)
        sea = jnp.where(k < depth, land[at, :], 0) > 0
        half = jnp.where(sea, 0.5 * kappa[at, :], 0.0)
        fx = face(half, east(half))
        fn = jnp.where(inside, face(half, north(half)), 0.0)
        fw, fs = west(fx), south(fn)
        keep = 1.0 - (fx + fw) - (fn + fs)
        brick = level_at(k, s.shape[1])
        u = unstacked(m0[brick, :]) + s * unstacked(w[brick, :])
        for _ in range(2):
            u = keep * u + (fx * east(u) + fw * west(u)) + (fn * north(u) + fs * south(u))
        return u

    def group(i, carry):
        for values, k in [(level(2 * i + j), 2 * i + j) for j in range(2)]:
            u2_ref[rows_at(k), :] = values
        return carry

    chunk = levels // 2 // parts
    for i in range(parts):
        for copy in copies[4 * i : 4 * i + 4]:
            copy.wait()
        lax.fori_loop(i * chunk, (i + 1) * chunk, group, 0)


def finish_body(levels, u2, links, own_near, own_far, rim_near, rim_far, near, far, rim_other_near, rim_other_far,
                out, change_ref, buffer, sems):
    width = own_near.shape[1]
    tall = width // 128 * ROWS
    rows = lax.broadcasted_iota(jnp.int32, (ROWS, width), 0)
    on_rim = (rows < 2) | (rows >= ROWS - 2)
    even = is_even()
    copies = []
    for block in range(levels // 8):
        at, below = pl.ds(block * 8, 8), pl.ds(levels + block * 8, 8)

        def pairs(a, b):
            return [dealt(even, a[part, :], b[part, :]) for part in (at, below)]

        own, rim = pairs(own_near, own_far), pairs(rim_near, rim_far)
        other, rim_other = pairs(near, far), pairs(rim_other_near, rim_other_far)
        for side, row, inner in ((0, 0, 1), (1, ROWS - 1, ROWS - 2)):
            face = 0.5 * (rim[0][side] + rim_other[0][side]) * rim[1][side] * rim_other[1][side]
            change = face * (other[0][side] - own[0][side])
            along, link = (links[pl.ds((block * LINKS + side * 2 + i) * 8, 8), :] for i in range(2))
            flux = along * (east(change) - change)
            passed = link * change
            on_row = (change + (flux - west(flux)) - passed
                      + face * (other[1][side] - own[1][side] - 2.0 * change))
            for j in range(width // 128):
                lanes = slice(j * 128, (j + 1) * 128)
                change_ref[pl.ds(j * ROWS + row, 8, stride=tall), :] = on_row[:, lanes]
                change_ref[pl.ds(j * ROWS + inner, 8, stride=tall), :] = passed[:, lanes]
        for k in range(8):
            level = block * 8 + k
            change = jnp.where(on_rim, unstacked(change_ref[level_at(k, width), :]), 0.0)
            buffer[rows_at(level), :] = u2[rows_at(level), :] + change
        whole = pl.ds(block * 8 * ROWS, 8 * ROWS)
        copy = pltpu.make_async_copy(buffer.at[whole], out.at[whole], sems.at[block])
        copy.start()
        copies.append(copy)
    for copy in copies:
        copy.wait()


def exchange(to_near, to_far):
    count = lax.axis_size("tile")

    def swap(array, start):
        firsts = range(start, count - 1, 2)
        return lax.ppermute(array, "tile", [(i, i + 1) for i in firsts] + [(i + 1, i) for i in firsts])

    from_far = swap(to_far, 1)
    return swap(to_near, 0), from_far


def body(ct_tracer, ct_surface, kappa, kvert, land, kmt, screen, layer_weight):
    levels, rows, width = ct_tracer.shape
    count = lax.axis_size("tile")
    tall = levels * rows
    tile, brick, flat = (rows, width), (tall * width // 128, 128), (tall, width)
    rim, rim_rows, link_rows = (2 * levels, width), (levels * RIM, width), (levels * LINKS, width)
    scalars, whole = pltpu.SMEM((levels,), FLOAT), pltpu.VMEM(flat, FLOAT)
    ints, tile_ints = pltpu.VMEM(flat, jnp.int32), pltpu.VMEM(tile, jnp.int32)
    bricks, tiles = pltpu.VMEM(brick, FLOAT), pltpu.VMEM(tile, FLOAT)
    ct_tracer, kappa, kvert, land = (left(a.reshape(flat)) for a in (ct_tracer, kappa, kvert, land))
    kmt, layer_weight = left(kmt), left(layer_weight)
    semaphores = pltpu.SemaphoreType.DMA

    height, surface, s_fx, s_fn, s_dg, q1, base, to_near, to_far, rim_near, rim_far, links = kernel(
        functools.partial(setup_body, levels), vmem(*[tile] * 9, rim, rim) + hbm(link_rows), in_hbm(6),
        in_vmem(11) + in_hbm(1), "setup",
        [scalars, ints, tile_ints, tiles, whole, bricks, bricks, pltpu.VMEM(link_rows, FLOAT), semaphores((12,)),
         semaphores((1,))],
    )(layer_weight, land, kmt, left(ct_surface), left(screen), kappa)
    near, far = exchange(to_near, to_far)
    rim_other_near, rim_other_far = exchange(rim_near, rim_far)

    basis, sums = kernel(
        functools.partial(basis_body, count), hbm((3 * rows, width)) + vmem((8 * count, 128)), in_vmem(9),
        in_hbm(1) + in_vmem(1), "basis", [pltpu.VMEM((3 * rows, width), FLOAT), semaphores((3,))],
    )(base, height, surface, s_fx, s_fn, s_dg, q1, near, far)
    sums = lax.all_to_all(sums.reshape(count, 8, 128), "tile", 0, 0, tiled=True).reshape(8 * count, 128)

    m0, w, rims = kernel(
        functools.partial(columns_body, levels), hbm(brick, brick, rim_rows), in_hbm(6), in_hbm(3), "columns",
        [scalars, tile_ints, whole, whole, ints, pltpu.VMEM(link_rows, FLOAT), bricks, bricks, bricks,
         pltpu.VMEM(rim_rows, FLOAT), semaphores((15,)), semaphores((8 + levels // 8,))],
    )(layer_weight, kmt, ct_tracer, kvert, land, left(links))

    solution, s, row_near, row_far = kernel(
        functools.partial(edges_body, levels, count), hbm(tile) + vmem(tile, rim, rim),
        in_vmem(1) + in_hbm(3), in_hbm(1) + in_vmem(3), "edges",
        [pltpu.VMEM((3 * rows, width), FLOAT), pltpu.VMEM(rim_rows, FLOAT), pltpu.VMEM(link_rows, FLOAT),
         semaphores((levels // 4 + 2,))],
    )(sums, left(basis), left(rims), left(links))
    other_near, other_far = exchange(row_near, row_far)
    u2 = kernel(
        functools.partial(inner_body, levels), vmem(flat), in_vmem(1) + in_hbm(5), in_vmem(1), "inner",
        [tile_ints, bricks, bricks, whole, ints, semaphores((17,))],
    )(s, kmt, left(m0), left(w), kappa, land)[0]

    values = kernel(
        functools.partial(finish_body, levels), hbm(flat), in_vmem(10), in_hbm(1), "finish",
        [pltpu.VMEM((8 * rows * width // 128, 128), FLOAT), whole, semaphores((levels // 8,))],
    )(u2, held(links), row_near, row_far, rim_near, rim_far, other_near, other_far, rim_other_near, rim_other_far)[0]
    return (values.reshape(levels, rows, width), solution)


def solution(mesh):
    in_specs = (
        P(None, ("grp", "tile"), None),
        P(("grp", "tile"), None),
        P(None, "tile", None),
        P(None, "tile", None),
        P(None, "tile", None),
        P("tile", None),
        P("tile", None),
        P(),
    )
    out_specs = (P(None, ("grp", "tile"), None), P(("grp", "tile"), None))
    return jax.shard_map(body, mesh=mesh, in_specs=in_specs, out_specs=out_specs, check_vma=False)
```

```python
import functools

import jax
import jax.numpy as jnp
from jax import lax
from jax.experimental import pallas as pl
from jax.experimental.pallas import tpu as pltpu
from jax.sharding import PartitionSpec as P

ITERS = 3
ROWS = 8
LOW = 0.05
HIGH = 9.0
MID = 0.5 * (HIGH + LOW)
HALF = 0.5 * (HIGH - LOW)
FLOAT = jnp.float32
RIM = 8
LINKS = 4
LIMIT = 24 * 1024 * 1024


def east(values):
    return pltpu.roll(values, values.shape[1] - 1, 1)


def west(values):
    return pltpu.roll(values, 1, 1)


def north(values):
    return pltpu.roll(values, values.shape[0] - 1, 0)


def south(values):
    return pltpu.roll(values, 1, 0)


def stacked(values):
    return jnp.concatenate([values[:, i : i + 128] for i in range(0, values.shape[1], 128)], axis=0)


def unstacked(values):
    return jnp.concatenate([values[i : i + ROWS, :] for i in range(0, values.shape[0], ROWS)], axis=1)


def row_of(ref, block, row, width):
    tall = width // 128 * ROWS
    return jnp.concatenate(
        [ref[pl.ds(block * 8 * tall + j * ROWS + row, 8, stride=tall), :] for j in range(width // 128)], axis=1
    )


def level_at(k, width):
    tall = width // 128 * ROWS
    return pl.ds(pl.multiple_of(k * tall, tall), tall)


def rows_at(k):
    return pl.ds(pl.multiple_of(k * ROWS, ROWS), ROWS)


def row_index(values):
    return lax.broadcasted_iota(jnp.int32, values.shape, 0)


def spread(row, like):
    return jnp.broadcast_to(row, like.shape)


def vmem(*shapes):
    return [pltpu.VMEM(shape, FLOAT) for shape in shapes]


def hbm(*shapes):
    return [pltpu.HBM(shape, FLOAT) for shape in shapes]


def in_vmem(count):
    return [pl.BlockSpec(memory_space=pltpu.VMEM)] * count


def in_hbm(count):
    return [pl.BlockSpec(memory_space=pltpu.HBM)] * count


def kernel(body, outs, ins, out_specs, name, scratch=(), cost=1):
    return pl.pallas_call(
        body,
        out_shape=outs,
        in_specs=ins,
        out_specs=out_specs,
        scratch_shapes=list(scratch),
        name=name,
        cost_estimate=pl.CostEstimate(flops=cost, bytes_accessed=cost, transcendentals=0),
        compiler_params=pltpu.CompilerParams(vmem_limit_bytes=LIMIT),
    )


def held(array):
    return pltpu.with_memory_space_constraint(array, pltpu.VMEM)


def left(array):
    return pltpu.with_memory_space_constraint(array, pltpu.HBM)


def is_even():
    return lax.rem(lax.axis_index("tile"), 2) == 0


def dealt(even, low, high):
    return jnp.where(even, high, low), jnp.where(even, low, high)


def loads(pairs, sems, first=0):
    copies = [pltpu.make_async_copy(far, near, sems.at[first + i]) for i, (far, near) in enumerate(pairs)]
    for copy in copies:
        copy.start()
    return copies


def in_parts(far, near, parts):
    size = far.shape[0] // parts
    return [(far.at[pl.ds(i * size, size)], near.at[pl.ds(i * size, size)]) for i in range(parts)]


def weight_sum(weight, levels):
    total = weight[0]
    for k in range(1, levels):
        total = total + weight[k]
    return total


def setup_body(levels, weight_hbm, land_hbm, kmt_hbm, ct_hbm, screen_hbm, kappa_hbm, height_ref, surface_ref,
               fx_ref, fn_ref, dg_ref, q1_ref, base_ref, near_ref, far_ref, rim_near_ref, rim_far_ref, links_hbm,
               weight, land, kmt, screen, kappa, wet_bricks, kappa_bricks, links, sems, out_sems):
    chunk = levels // 4
    small = loads(((weight_hbm, weight), (kmt_hbm, kmt)), sems)
    land_copies = loads(in_parts(land_hbm, land, 4), sems, 2)
    small += loads(((ct_hbm, base_ref), (screen_hbm, screen)), sems, 6)
    kappa_copies = loads(in_parts(kappa_hbm, kappa, 4), sems, 8)
    small[0].wait()
    total = weight_sum(weight, levels)
    small[1].wait()
    depth = kmt[...]
    width = depth.shape[1]
    height = jnp.zeros(depth.shape, FLOAT)
    for i, copy in enumerate(land_copies):
        copy.wait()

        def level(k, height):
            wet = jnp.where(k < depth, land[rows_at(k), :], 0).astype(FLOAT)
            wet_bricks[level_at(k, width), :] = stacked(wet)
            return height + weight[k] * wet

        height = lax.fori_loop(i * chunk, (i + 1) * chunk, level, height, unroll=4)
    height = height / total
    surface = jnp.where(0 < depth, land[0:ROWS, :], 0).astype(FLOAT)
    height_ref[...] = height
    surface_ref[...] = surface
    small[2].wait()
    small[3].wait()
    base = base_ref[...]
    rows = row_index(base)
    scale = 0.5 / HALF
    fx = scale * (height + east(height)) * surface * east(surface)
    fn = scale * (height + north(height)) * surface * north(surface)
    fn = jnp.where(rows < ROWS - 1, fn, 0.0)
    fs = south(fn)
    fw = west(fx)
    dg = (screen[...] - MID) * (1.0 / HALF) + fx + fw + fn + fs

    def apply(v):
        return dg * v - fx * east(v) - fw * west(v) - fn * north(v) - fs * south(v)

    q1 = apply(base)
    q2 = apply(q1)
    fx_ref[...] = fx
    fn_ref[...] = fn
    dg_ref[...] = dg
    q1_ref[...] = q1
    even = is_even()
    near_ref[7:8, :] = jnp.zeros_like(base[0:1, :])
    far_ref[7:8, :] = jnp.zeros_like(base[0:1, :])
    for place, values in enumerate((base, q1, q2, fx, dg, height, surface)):
        at = slice(place, place + 1)
        near_ref[at, :], far_ref[at, :] = dealt(even, values[0:1, :], values[ROWS - 1 : ROWS, :])

    for i, copy in enumerate(kappa_copies):
        copy.wait()

        def brick(k, carry):
            kappa_bricks[level_at(k, width), :] = stacked(kappa[rows_at(k), :])
            return carry

        lax.fori_loop(i * chunk, (i + 1) * chunk, brick, 0, unroll=4)
    for block in range(levels // 8):
        found = []
        for side, row, inner in ((0, 0, 1), (1, ROWS - 1, ROWS - 2)):
            kap, kap_in = row_of(kappa_bricks, block, row, width), row_of(kappa_bricks, block, inner, width)
            here, here_in = row_of(wet_bricks, block, row, width), row_of(wet_bricks, block, inner, width)
            at = (block * LINKS + side * 2) * 8
            links[pl.ds(at, 8), :] = 0.5 * (kap + east(kap)) * here * east(here)
            links[pl.ds(at + 8, 8), :] = 0.5 * (kap + kap_in) * here * here_in
            found.append((kap, here))
        for place in range(2):
            at = pl.ds(place * levels + block * 8, 8)
            rim_near_ref[at, :], rim_far_ref[at, :] = dealt(even, found[0][place], found[1][place])
    out = pltpu.make_async_copy(links, links_hbm, out_sems.at[0])
    out.start()
    out.wait()


def basis_body(count, ct, height, surface, fx_ref, fn_ref, dg_ref, q1_ref, near, far, basis_ref, sums_ref):
    even = is_even()
    b0 = ct[...]
    rows = row_index(b0)
    first, last = rows == 0, rows == ROWS - 1
    fx, fn, dg = fx_ref[...], fn_ref[...], dg_ref[...]
    fw, fs = west(fx), south(fn)

    def halo(values, row):
        b0_h, q1_h, q2_h, fx_h, dg_h, high_h, wet_h = (values[i : i + 1, :] for i in range(7))
        face = (0.5 / HALF) * (high_h + height[row : row + 1, :]) * wet_h * surface[row : row + 1, :]
        extra = face * (b0_h - ct[row : row + 1, :])
        return b0_h, q1_h + extra, q2_h, fx_h, dg_h, face, extra

    def lift(row):
        return jnp.broadcast_to(row, b0.shape)

    before, after = dealt(even, near[...], far[...])
    sides = (halo(before, 0), halo(after, ROWS - 1))
    face_b, face_a = lift(sides[0][5]), lift(sides[1][5])
    b1 = q1_ref[...] - jnp.where(first, lift(sides[0][6]), 0.0) - jnp.where(last, lift(sides[1][6]), 0.0)
    dg = dg + jnp.where(first, face_b, 0.0) + jnp.where(last, face_a, 0.0)
    fn = jnp.where(last, face_a, fn)
    fs = jnp.where(first, face_b, fs)

    def apply(v, v_before, v_after):
        v_n = jnp.where(last, lift(v_after), north(v))
        v_s = jnp.where(first, lift(v_before), south(v))
        return dg * v - fx * east(v) - fw * west(v) - fn * v_n - fs * v_s

    b2 = 2.0 * apply(b1, sides[0][1], sides[1][1]) - b0

    def outer(side, own):
        b0_h, b1_h, q2_h, fx_h, dg_h, face, extra = side
        b0_h, b1_h, q2_h, fx_h, dg_h, face, extra, own = (lift(v) for v in (b0_h, b1_h, q2_h, fx_h, dg_h, face, extra, own))
        turned = dg_h * extra - fx_h * east(extra) - west(fx_h) * west(extra)
        return (2.0 * (q2_h + turned + face * (b1_h - own)) - b0_h)[0:1, :]

    for place, values in enumerate((b0, b1, b2)):
        basis_ref[pl.ds(place * ROWS, ROWS), :] = values
    b2_b = outer(sides[0], b1[0:1, :])
    b2_a = outer(sides[1], b1[ROWS - 1 : ROWS, :])
    next2 = apply(b2, b2_b, b2_a)
    tile_rows = lax.broadcasted_iota(jnp.int32, (8, 128), 0)
    packed = jnp.zeros((8, 128), FLOAT)
    for place, (p, q) in enumerate(((b0, b0), (b0, b1), (b1, b1), (b1, b2), (b2, b2), (b2, next2))):
        product = p * q
        folded = product[:, 0:128]
        for j in range(1, product.shape[1] // 128):
            folded = folded + product[:, j * 128 : (j + 1) * 128]
        packed = jnp.where(tile_rows == place, jnp.sum(folded, axis=0, keepdims=True), packed)
    for j in range(count):
        sums_ref[j * 8 : (j + 1) * 8, :] = packed


def quadratic(left, form):
    total = None
    for i in range(3):
        for j in range(3):
            if left[i] is not None and left[j] is not None:
                term = left[i] * left[j] * form[i][j]
                total = term if total is None else total + term
    return total


def plus(p, q):
    return q if p is None else p if q is None else p + q


def times(scale, p):
    return None if p is None else scale * p


def weights(sums):
    s0, s1, s2, s3, s4, s5 = sums
    g02 = 2.0 * s2 - s0
    gram = ((s0, s1, g02), (s1, s2, s3), (g02, s3, s4))
    b11, b12 = 0.5 * (s3 + s1), 0.5 * (s4 + g02)
    shift = ((s1, s2, s3), (s2, b11, b12), (s3, b12, s5))
    form = [[MID * gram[i][j] + HALF * shift[i][j] for j in range(3)] for i in range(3)]
    one = jnp.ones_like(s0)
    x, r, d = [None] * 3, [one, None, None], [one, None, None]
    rr = s0
    for step in range(ITERS):
        alpha = jnp.clip(rr / quadratic(d, form), 1.0 / HIGH, 1.0 / LOW)
        x = [plus(x[i], times(alpha, d[i])) for i in range(3)]
        if step + 1 < ITERS:
            image = [
                plus(times(MID, d[0]), times(0.5 * HALF, d[1])),
                plus(plus(times(MID, d[1]), times(HALF, d[0])), times(0.5 * HALF, d[2])),
                plus(times(MID, d[2]), times(0.5 * HALF, d[1])),
            ]
            r = [plus(r[i], times(-1.0, times(alpha, image[i]))) for i in range(3)]
            new = quadratic(r, gram)
            beta = jnp.clip(new / rr, 0.0, HIGH / LOW)
            d = [plus(r[i], times(beta, d[i])) for i in range(3)]
            rr = new
    return x


def edges_body(levels, count, sums, basis_ref, rim_hbm, links_hbm, out_hbm, s_ref, near_ref, far_ref,
               rims, links, sems):
    blocks = levels // 8
    both = [pair for pairs in zip(in_parts(rim_hbm, rims, blocks), in_parts(links_hbm, links, blocks)) for pair in pairs]
    copies = loads(both, sems)
    total = sums[0:8, :]
    for j in range(1, count):
        total = total + sums[j * 8 : (j + 1) * 8, :]
    total = jnp.sum(total, axis=1, keepdims=True)
    mix = weights([total[i : i + 1, :] for i in range(6)])
    b0, b1, b2 = (basis_ref[i * ROWS : (i + 1) * ROWS, :] for i in range(3))
    s = mix[0] * b0 + mix[1] * b1 + mix[2] * b2
    s_ref[...] = s
    copy_s = loads([(s_ref, out_hbm)], sems, 2 * blocks)[0]
    s_rows = {r: spread(s[r : r + 1, :], s) for r in (0, 1, ROWS - 2, ROWS - 1)}
    even = is_even()

    for block in range(blocks):
        copies[2 * block].wait()
        copies[2 * block + 1].wait()
        found = []
        for side, row, inner in ((0, 0, 1), (1, ROWS - 1, ROWS - 2)):
            m, gm, w, q = (rims[pl.ds((block * RIM + side * 4 + i) * 8, 8), :] for i in range(4))
            face, link = (links[pl.ds((block * LINKS + side * 2 + i) * 8, 8), :] for i in range(2))
            v = s_rows[row] * w
            flux = face * (east(v) - v)
            found.append((m + v, gm + v + (flux - west(flux)) - link * v + s_rows[inner] * q))
        for place in range(2):
            at = pl.ds(place * levels + block * 8, 8)
            near_ref[at, :], far_ref[at, :] = dealt(even, found[0][place], found[1][place])
    copy_s.wait()


def columns_body(levels, weight_hbm, kmt_hbm, source_hbm, kvert_hbm, land_hbm, links_hbm, m0_hbm, w_hbm, rim_hbm,
                 weight, kmt, source, kvert, land, links, m0, w, ratio, rims, in_sems, out_sems):
    width = source.shape[1]
    parts = 4
    chunk = levels // parts
    small = loads(((weight_hbm, weight), (kmt_hbm, kmt)), in_sems)
    parted = [in_parts(far, near, parts) for far, near in ((land_hbm, land), (kvert_hbm, kvert), (source_hbm, source))]
    big = loads([pairs[i] for i in range(parts) for pairs in parted], in_sems, 2)
    links_copy = loads([(links_hbm, links)], in_sems, 2 + 3 * parts)[0]
    small[0].wait()
    total = weight_sum(weight, levels)
    shape = (ROWS * width // 128, 128)
    inverse = 1.0 / jnp.full(shape, total, FLOAT)
    small[1].wait()
    depth = stacked(kmt[...])

    def sea(k):
        return jnp.where(k < depth, stacked(land[rows_at(k), :]), 0).astype(FLOAT)

    def down(k, carry):
        here, link, m_in, w_in = carry
        at = level_at(k, width)
        below = jnp.where(k + 1 < levels, sea(jnp.minimum(k + 1, levels - 1)), 0.0)
        coupling = stacked(kvert[rows_at(k), :]) * here * below
        over = 1.0 / (1.0 + coupling + link)
        m_here = (stacked(source[rows_at(k), :]) + m_in) * over
        w_here = (here * (weight[k] * inverse) + w_in) * over
        part = coupling * over
        ratio[at, :] = part
        m0[at, :] = m_here
        w[at, :] = w_here
        return below, coupling - coupling * part, coupling * m_here, coupling * w_here

    zero = jnp.zeros(shape, FLOAT)
    big[0].wait()
    carry = (sea(0), zero, zero, zero)
    for i in range(parts):
        big[3 * i + 1].wait()
        big[3 * i + 2].wait()
        if i + 1 < parts:
            big[3 * i + 3].wait()
        carry = lax.fori_loop(i * chunk, (i + 1) * chunk, down, carry)

    def up(i, carry):
        at = level_at(levels - 1 - i, width)
        m_below, w_below = carry
        part = ratio[at, :]
        m_here = m0[at, :] + part * m_below
        w_here = w[at, :] + part * w_below
        m0[at, :] = m_here
        w[at, :] = w_here
        return m_here, w_here

    carry = (zero, zero)
    outs = []
    for i in range(parts):
        carry = lax.fori_loop(i * chunk, (i + 1) * chunk, up, carry)
        size = chunk * shape[0]
        whole = pl.ds((parts - 1 - i) * size, size)
        for a, (near, far) in enumerate(((m0, m0_hbm), (w, w_hbm))):
            copy = pltpu.make_async_copy(near.at[whole], far.at[whole], out_sems.at[i * 2 + a])
            copy.start()
            outs.append(copy)
    links_copy.wait()
    for block in range(levels // 8):
        for side, row, inner in ((0, 0, 1), (1, ROWS - 1, ROWS - 2)):
            m, w_row = row_of(m0, block, row, width), row_of(w, block, row, width)
            face, link = (links[pl.ds((block * LINKS + side * 2 + i) * 8, 8), :] for i in range(2))
            flux = face * (east(m) - m)
            gm = m + (flux - west(flux)) + link * (row_of(m0, block, inner, width) - m)
            q = link * row_of(w, block, inner, width)
            for i, values in enumerate((m, gm, w_row, q)):
                rims[pl.ds((block * RIM + side * 4 + i) * 8, 8), :] = values
        whole = pl.ds(block * RIM * 8, RIM * 8)
        outs += loads([(rims.at[whole], rim_hbm.at[whole])], out_sems, 2 * parts + block)
    for copy in outs:
        copy.wait()


def inner_body(levels, s_ref, kmt_hbm, m0_hbm, w_hbm, kappa_hbm, land_hbm, u2_ref, kmt, m0, w, kappa, land, sems):
    parts = 4
    kmt_copy = loads([(kmt_hbm, kmt)], sems)[0]
    pairs = ((kappa_hbm, kappa), (land_hbm, land), (m0_hbm, m0), (w_hbm, w))
    parted = [in_parts(far, near, parts) for far, near in pairs]
    copies = loads([pairs[i] for i in range(parts) for pairs in parted], sems, 1)
    s = s_ref[...]
    kmt_copy.wait()
    depth = kmt[...]
    inside = row_index(s) < ROWS - 1

    def face(here, there):
        return jnp.where(jnp.minimum(here, there) > 0.0, here + there, 0.0)

    def level(k):
        at = rows_at(k)
        sea = jnp.where(k < depth, land[at, :], 0) > 0
        half = jnp.where(sea, 0.5 * kappa[at, :], 0.0)
        fx = face(half, east(half))
        fn = jnp.where(inside, face(half, north(half)), 0.0)
        fw, fs = west(fx), south(fn)
        keep = 1.0 - (fx + fw) - (fn + fs)
        brick = level_at(k, s.shape[1])
        u = unstacked(m0[brick, :]) + s * unstacked(w[brick, :])
        for _ in range(2):
            u = keep * u + (fx * east(u) + fw * west(u)) + (fn * north(u) + fs * south(u))
        return u

    def group(i, carry):
        for values, k in [(level(2 * i + j), 2 * i + j) for j in range(2)]:
            u2_ref[rows_at(k), :] = values
        return carry

    chunk = levels // 2 // parts
    for i in range(parts):
        for copy in copies[4 * i : 4 * i + 4]:
            copy.wait()
        lax.fori_loop(i * chunk, (i + 1) * chunk, group, 0)


def finish_body(levels, u2, links, own_near, own_far, rim_near, rim_far, near, far, rim_other_near, rim_other_far,
                out, change_ref, buffer, sems):
    width = own_near.shape[1]
    tall = width // 128 * ROWS
    rows = lax.broadcasted_iota(jnp.int32, (ROWS, width), 0)
    on_rim = (rows < 2) | (rows >= ROWS - 2)
    even = is_even()
    copies = []
    for block in range(levels // 8):
        at, below = pl.ds(block * 8, 8), pl.ds(levels + block * 8, 8)

        def pairs(a, b):
            return [dealt(even, a[part, :], b[part, :]) for part in (at, below)]

        own, rim = pairs(own_near, own_far), pairs(rim_near, rim_far)
        other, rim_other = pairs(near, far), pairs(rim_other_near, rim_other_far)
        for side, row, inner in ((0, 0, 1), (1, ROWS - 1, ROWS - 2)):
            face = 0.5 * (rim[0][side] + rim_other[0][side]) * rim[1][side] * rim_other[1][side]
            change = face * (other[0][side] - own[0][side])
            along, link = (links[pl.ds((block * LINKS + side * 2 + i) * 8, 8), :] for i in range(2))
            flux = along * (east(change) - change)
            passed = link * change
            on_row = (change + (flux - west(flux)) - passed
                      + face * (other[1][side] - own[1][side] - 2.0 * change))
            for j in range(width // 128):
                lanes = slice(j * 128, (j + 1) * 128)
                change_ref[pl.ds(j * ROWS + row, 8, stride=tall), :] = on_row[:, lanes]
                change_ref[pl.ds(j * ROWS + inner, 8, stride=tall), :] = passed[:, lanes]
        for k in range(8):
            level = block * 8 + k
            change = jnp.where(on_rim, unstacked(change_ref[level_at(k, width), :]), 0.0)
            buffer[rows_at(level), :] = u2[rows_at(level), :] + change
        whole = pl.ds(block * 8 * ROWS, 8 * ROWS)
        copy = pltpu.make_async_copy(buffer.at[whole], out.at[whole], sems.at[block])
        copy.start()
        copies.append(copy)
    for copy in copies:
        copy.wait()


def exchange(to_near, to_far):
    count = lax.axis_size("tile")

    def swap(array, start):
        firsts = range(start, count - 1, 2)
        return lax.ppermute(array, "tile", [(i, i + 1) for i in firsts] + [(i + 1, i) for i in firsts])

    from_far = swap(to_far, 1)
    return swap(to_near, 0), from_far


def body(ct_tracer, ct_surface, kappa, kvert, land, kmt, screen, layer_weight):
    levels, rows, width = ct_tracer.shape
    count = lax.axis_size("tile")
    tall = levels * rows
    tile, brick, flat = (rows, width), (tall * width // 128, 128), (tall, width)
    rim, rim_rows, link_rows = (2 * levels, width), (levels * RIM, width), (levels * LINKS, width)
    scalars, whole = pltpu.SMEM((levels,), FLOAT), pltpu.VMEM(flat, FLOAT)
    ints, tile_ints = pltpu.VMEM(flat, jnp.int32), pltpu.VMEM(tile, jnp.int32)
    bricks, tiles = pltpu.VMEM(brick, FLOAT), pltpu.VMEM(tile, FLOAT)
    ct_tracer, kappa, kvert, land = (left(a.reshape(flat)) for a in (ct_tracer, kappa, kvert, land))
    kmt, layer_weight = left(kmt), left(layer_weight)
    semaphores = pltpu.SemaphoreType.DMA

    height, surface, s_fx, s_fn, s_dg, q1, base, to_near, to_far, rim_near, rim_far, links = kernel(
        functools.partial(setup_body, levels), vmem(*[tile] * 9, rim, rim) + hbm(link_rows), in_hbm(6),
        in_vmem(11) + in_hbm(1), "setup",
        [scalars, ints, tile_ints, tiles, whole, bricks, bricks, pltpu.VMEM(link_rows, FLOAT), semaphores((12,)),
         semaphores((1,))],
    )(layer_weight, land, kmt, left(ct_surface), left(screen), kappa)
    near, far = exchange(to_near, to_far)
    rim_other_near, rim_other_far = exchange(rim_near, rim_far)

    basis, sums = kernel(
        functools.partial(basis_body, count), vmem((3 * rows, width), (8 * count, 128)), in_vmem(9), in_vmem(2), "basis"
    )(base, height, surface, s_fx, s_fn, s_dg, q1, near, far)
    sums = lax.all_to_all(sums.reshape(count, 8, 128), "tile", 0, 0, tiled=True).reshape(8 * count, 128)

    m0, w, rims = kernel(
        functools.partial(columns_body, levels), hbm(brick, brick, rim_rows), in_hbm(6), in_hbm(3), "columns",
        [scalars, tile_ints, whole, whole, ints, pltpu.VMEM(link_rows, FLOAT), bricks, bricks, bricks,
         pltpu.VMEM(rim_rows, FLOAT), semaphores((15,)), semaphores((8 + levels // 8,))],
    )(layer_weight, kmt, ct_tracer, kvert, land, left(links))

    solution, s, row_near, row_far = kernel(
        functools.partial(edges_body, levels, count), hbm(tile) + vmem(tile, rim, rim),
        in_vmem(2) + in_hbm(2), in_hbm(1) + in_vmem(3), "edges",
        [pltpu.VMEM(rim_rows, FLOAT), pltpu.VMEM(link_rows, FLOAT),
         semaphores((levels // 4 + 1,))],
    )(sums, basis, left(rims), left(links))
    other_near, other_far = exchange(row_near, row_far)
    u2 = kernel(
        functools.partial(inner_body, levels), vmem(flat), in_vmem(1) + in_hbm(5), in_vmem(1), "inner",
        [tile_ints, bricks, bricks, whole, ints, semaphores((17,))],
    )(s, kmt, left(m0), left(w), kappa, land)[0]

    values = kernel(
        functools.partial(finish_body, levels), hbm(flat), in_vmem(10), in_hbm(1), "finish",
        [pltpu.VMEM((8 * rows * width // 128, 128), FLOAT), whole, semaphores((levels // 8,))],
    )(u2, held(links), row_near, row_far, rim_near, rim_far, other_near, other_far, rim_other_near, rim_other_far)[0]
    return (values.reshape(levels, rows, width), solution)


def solution(mesh):
    in_specs = (
        P(None, ("grp", "tile"), None),
        P(("grp", "tile"), None),
        P(None, "tile", None),
        P(None, "tile", None),
        P(None, "tile", None),
        P("tile", None),
        P("tile", None),
        P(),
    )
    out_specs = (P(None, ("grp", "tile"), None), P(("grp", "tile"), None))
    return jax.shard_map(body, mesh=mesh, in_specs=in_specs, out_specs=out_specs, check_vma=False)
```

```python
import functools

import jax
import jax.numpy as jnp
from jax import lax
from jax.experimental import pallas as pl
from jax.experimental.pallas import tpu as pltpu
from jax.sharding import PartitionSpec as P

ITERS = 3
ROWS = 8
LOW = 0.05
HIGH = 9.0
MID = 0.5 * (HIGH + LOW)
HALF = 0.5 * (HIGH - LOW)
FLOAT = jnp.float32
RIM = 8
LINKS = 4
LIMIT = 24 * 1024 * 1024


def east(values):
    return pltpu.roll(values, values.shape[1] - 1, 1)


def west(values):
    return pltpu.roll(values, 1, 1)


def north(values):
    return pltpu.roll(values, values.shape[0] - 1, 0)


def south(values):
    return pltpu.roll(values, 1, 0)


def stacked(values):
    return jnp.concatenate([values[:, i : i + 128] for i in range(0, values.shape[1], 128)], axis=0)


def unstacked(values):
    return jnp.concatenate([values[i : i + ROWS, :] for i in range(0, values.shape[0], ROWS)], axis=1)


def row_of(ref, block, row, width):
    tall = width // 128 * ROWS
    return jnp.concatenate(
        [ref[pl.ds(block * 8 * tall + j * ROWS + row, 8, stride=tall), :] for j in range(width // 128)], axis=1
    )


def level_at(k, width):
    tall = width // 128 * ROWS
    return pl.ds(pl.multiple_of(k * tall, tall), tall)


def rows_at(k):
    return pl.ds(pl.multiple_of(k * ROWS, ROWS), ROWS)


def row_index(values):
    return lax.broadcasted_iota(jnp.int32, values.shape, 0)


def spread(row, like):
    return jnp.broadcast_to(row, like.shape)


def vmem(*shapes):
    return [pltpu.VMEM(shape, FLOAT) for shape in shapes]


def hbm(*shapes):
    return [pltpu.HBM(shape, FLOAT) for shape in shapes]


def in_vmem(count):
    return [pl.BlockSpec(memory_space=pltpu.VMEM)] * count


def in_hbm(count):
    return [pl.BlockSpec(memory_space=pltpu.HBM)] * count


def kernel(body, outs, ins, out_specs, name, scratch=(), cost=1):
    return pl.pallas_call(
        body,
        out_shape=outs,
        in_specs=ins,
        out_specs=out_specs,
        scratch_shapes=list(scratch),
        name=name,
        cost_estimate=pl.CostEstimate(flops=cost, bytes_accessed=cost, transcendentals=0),
        compiler_params=pltpu.CompilerParams(vmem_limit_bytes=LIMIT),
    )


def held(array):
    return pltpu.with_memory_space_constraint(array, pltpu.VMEM)


def left(array):
    return pltpu.with_memory_space_constraint(array, pltpu.HBM)


def is_even():
    return lax.rem(lax.axis_index("tile"), 2) == 0


def dealt(even, low, high):
    return jnp.where(even, high, low), jnp.where(even, low, high)


def loads(pairs, sems, first=0):
    copies = [pltpu.make_async_copy(far, near, sems.at[first + i]) for i, (far, near) in enumerate(pairs)]
    for copy in copies:
        copy.start()
    return copies


def in_parts(far, near, parts):
    size = far.shape[0] // parts
    return [(far.at[pl.ds(i * size, size)], near.at[pl.ds(i * size, size)]) for i in range(parts)]


def weight_sum(weight, levels):
    total = weight[0]
    for k in range(1, levels):
        total = total + weight[k]
    return total


def setup_body(levels, weight_hbm, land_hbm, kmt_hbm, ct_hbm, screen_hbm, kappa_hbm, height_ref, surface_ref,
               fx_ref, fn_ref, dg_ref, q1_ref, base_ref, near_ref, far_ref, rim_near_ref, rim_far_ref, links_hbm,
               weight, land, kmt, screen, kappa, wet_bricks, kappa_bricks, links, sems, out_sems):
    chunk = levels // 4
    small = loads(((weight_hbm, weight), (kmt_hbm, kmt)), sems)
    land_copies = loads(in_parts(land_hbm, land, 4), sems, 2)
    small += loads(((ct_hbm, base_ref), (screen_hbm, screen)), sems, 6)
    kappa_copies = loads(in_parts(kappa_hbm, kappa, 4), sems, 8)
    small[0].wait()
    total = weight_sum(weight, levels)
    small[1].wait()
    depth = kmt[...]
    width = depth.shape[1]
    height = jnp.zeros(depth.shape, FLOAT)
    for i, copy in enumerate(land_copies):
        copy.wait()

        def level(k, height):
            wet = jnp.where(k < depth, land[rows_at(k), :], 0).astype(FLOAT)
            wet_bricks[level_at(k, width), :] = stacked(wet)
            return height + weight[k] * wet

        height = lax.fori_loop(i * chunk, (i + 1) * chunk, level, height, unroll=4)
    height = height / total
    surface = jnp.where(0 < depth, land[0:ROWS, :], 0).astype(FLOAT)
    height_ref[...] = height
    surface_ref[...] = surface
    small[2].wait()
    small[3].wait()
    base = base_ref[...]
    rows = row_index(base)
    scale = 0.5 / HALF
    fx = scale * (height + east(height)) * surface * east(surface)
    fn = scale * (height + north(height)) * surface * north(surface)
    fn = jnp.where(rows < ROWS - 1, fn, 0.0)
    fs = south(fn)
    fw = west(fx)
    dg = (screen[...] - MID) * (1.0 / HALF) + fx + fw + fn + fs

    def apply(v):
        return dg * v - fx * east(v) - fw * west(v) - fn * north(v) - fs * south(v)

    q1 = apply(base)
    q2 = apply(q1)
    fx_ref[...] = fx
    fn_ref[...] = fn
    dg_ref[...] = dg
    q1_ref[...] = q1
    even = is_even()
    near_ref[7:8, :] = jnp.zeros_like(base[0:1, :])
    far_ref[7:8, :] = jnp.zeros_like(base[0:1, :])
    for place, values in enumerate((base, q1, q2, fx, dg, height, surface)):
        at = slice(place, place + 1)
        near_ref[at, :], far_ref[at, :] = dealt(even, values[0:1, :], values[ROWS - 1 : ROWS, :])

    for i, copy in enumerate(kappa_copies):
        copy.wait()

        def brick(k, carry):
            kappa_bricks[level_at(k, width), :] = stacked(kappa[rows_at(k), :])
            return carry

        lax.fori_loop(i * chunk, (i + 1) * chunk, brick, 0, unroll=4)
    for block in range(levels // 8):
        found = []
        for side, row, inner in ((0, 0, 1), (1, ROWS - 1, ROWS - 2)):
            kap, kap_in = row_of(kappa_bricks, block, row, width), row_of(kappa_bricks, block, inner, width)
            here, here_in = row_of(wet_bricks, block, row, width), row_of(wet_bricks, block, inner, width)
            at = (block * LINKS + side * 2) * 8
            links[pl.ds(at, 8), :] = 0.5 * (kap + east(kap)) * here * east(here)
            links[pl.ds(at + 8, 8), :] = 0.5 * (kap + kap_in) * here * here_in
            found.append((kap, here))
        for place in range(2):
            at = pl.ds(place * levels + block * 8, 8)
            rim_near_ref[at, :], rim_far_ref[at, :] = dealt(even, found[0][place], found[1][place])
    out = pltpu.make_async_copy(links, links_hbm, out_sems.at[0])
    out.start()
    out.wait()


def basis_body(ct, height, surface, fx_ref, fn_ref, dg_ref, q1_ref, near, far, basis_ref, sums_ref):
    even = is_even()
    b0 = ct[...]
    rows = row_index(b0)
    first, last = rows == 0, rows == ROWS - 1
    fx, fn, dg = fx_ref[...], fn_ref[...], dg_ref[...]
    fw, fs = west(fx), south(fn)

    def halo(values, row):
        b0_h, q1_h, q2_h, fx_h, dg_h, high_h, wet_h = (values[i : i + 1, :] for i in range(7))
        face = (0.5 / HALF) * (high_h + height[row : row + 1, :]) * wet_h * surface[row : row + 1, :]
        extra = face * (b0_h - ct[row : row + 1, :])
        return b0_h, q1_h + extra, q2_h, fx_h, dg_h, face, extra

    def lift(row):
        return jnp.broadcast_to(row, b0.shape)

    before, after = dealt(even, near[...], far[...])
    sides = (halo(before, 0), halo(after, ROWS - 1))
    face_b, face_a = lift(sides[0][5]), lift(sides[1][5])
    b1 = q1_ref[...] - jnp.where(first, lift(sides[0][6]), 0.0) - jnp.where(last, lift(sides[1][6]), 0.0)
    dg = dg + jnp.where(first, face_b, 0.0) + jnp.where(last, face_a, 0.0)
    fn = jnp.where(last, face_a, fn)
    fs = jnp.where(first, face_b, fs)

    def apply(v, v_before, v_after):
        v_n = jnp.where(last, lift(v_after), north(v))
        v_s = jnp.where(first, lift(v_before), south(v))
        return dg * v - fx * east(v) - fw * west(v) - fn * v_n - fs * v_s

    b2 = 2.0 * apply(b1, sides[0][1], sides[1][1]) - b0

    def outer(side, own):
        b0_h, b1_h, q2_h, fx_h, dg_h, face, extra = side
        b0_h, b1_h, q2_h, fx_h, dg_h, face, extra, own = (lift(v) for v in (b0_h, b1_h, q2_h, fx_h, dg_h, face, extra, own))
        turned = dg_h * extra - fx_h * east(extra) - west(fx_h) * west(extra)
        return (2.0 * (q2_h + turned + face * (b1_h - own)) - b0_h)[0:1, :]

    for place, values in enumerate((b0, b1, b2)):
        basis_ref[pl.ds(place * ROWS, ROWS), :] = values
    b2_b = outer(sides[0], b1[0:1, :])
    b2_a = outer(sides[1], b1[ROWS - 1 : ROWS, :])
    next2 = apply(b2, b2_b, b2_a)
    tile_rows = lax.broadcasted_iota(jnp.int32, (8, 128), 0)
    packed = jnp.zeros((8, 128), FLOAT)
    for place, (p, q) in enumerate(((b0, b0), (b0, b1), (b1, b1), (b1, b2), (b2, b2), (b2, next2))):
        product = p * q
        folded = product[:, 0:128]
        for j in range(1, product.shape[1] // 128):
            folded = folded + product[:, j * 128 : (j + 1) * 128]
        packed = jnp.where(tile_rows == place, jnp.sum(folded, axis=0, keepdims=True), packed)
    sums_ref[...] = packed


def quadratic(left, form):
    total = None
    for i in range(3):
        for j in range(3):
            if left[i] is not None and left[j] is not None:
                term = left[i] * left[j] * form[i][j]
                total = term if total is None else total + term
    return total


def plus(p, q):
    return q if p is None else p if q is None else p + q


def times(scale, p):
    return None if p is None else scale * p


def weights(sums):
    s0, s1, s2, s3, s4, s5 = sums
    g02 = 2.0 * s2 - s0
    gram = ((s0, s1, g02), (s1, s2, s3), (g02, s3, s4))
    b11, b12 = 0.5 * (s3 + s1), 0.5 * (s4 + g02)
    shift = ((s1, s2, s3), (s2, b11, b12), (s3, b12, s5))
    form = [[MID * gram[i][j] + HALF * shift[i][j] for j in range(3)] for i in range(3)]
    one = jnp.ones_like(s0)
    x, r, d = [None] * 3, [one, None, None], [one, None, None]
    rr = s0
    for step in range(ITERS):
        alpha = jnp.clip(rr / quadratic(d, form), 1.0 / HIGH, 1.0 / LOW)
        x = [plus(x[i], times(alpha, d[i])) for i in range(3)]
        if step + 1 < ITERS:
            image = [
                plus(times(MID, d[0]), times(0.5 * HALF, d[1])),
                plus(plus(times(MID, d[1]), times(HALF, d[0])), times(0.5 * HALF, d[2])),
                plus(times(MID, d[2]), times(0.5 * HALF, d[1])),
            ]
            r = [plus(r[i], times(-1.0, times(alpha, image[i]))) for i in range(3)]
            new = quadratic(r, gram)
            beta = jnp.clip(new / rr, 0.0, HIGH / LOW)
            d = [plus(r[i], times(beta, d[i])) for i in range(3)]
            rr = new
    return x


def edges_body(levels, count, sums, basis_ref, rim_near, rim_far, rim_other_near, rim_other_far, rim_hbm, links_hbm,
               out_hbm, s_ref, near_ref, far_ref, faces_ref,
               rims, links, sems):
    blocks = levels // 8
    both = [pair for pairs in zip(in_parts(rim_hbm, rims, blocks), in_parts(links_hbm, links, blocks)) for pair in pairs]
    copies = loads(both, sems)
    total = sums[0:8, :]
    for j in range(1, count):
        total = total + sums[j * 8 : (j + 1) * 8, :]
    total = jnp.sum(total, axis=1, keepdims=True)
    mix = weights([total[i : i + 1, :] for i in range(6)])
    b0, b1, b2 = (basis_ref[i * ROWS : (i + 1) * ROWS, :] for i in range(3))
    s = mix[0] * b0 + mix[1] * b1 + mix[2] * b2
    s_ref[...] = s
    copy_s = loads([(s_ref, out_hbm)], sems, 2 * blocks)[0]
    s_rows = {r: spread(s[r : r + 1, :], s) for r in (0, 1, ROWS - 2, ROWS - 1)}
    even = is_even()

    for block in range(blocks):
        at, below = pl.ds(block * 8, 8), pl.ds(levels + block * 8, 8)
        kap, wet, kap_other, wet_other = (
            dealt(even, near[part, :], far[part, :])
            for near, far in ((rim_near, rim_far), (rim_other_near, rim_other_far)) for part in (at, below)
        )
        for side in range(2):
            faces_ref[pl.ds(side * levels + block * 8, 8), :] = (
                0.5 * (kap[side] + kap_other[side]) * wet[side] * wet_other[side]
            )
        copies[2 * block].wait()
        copies[2 * block + 1].wait()
        found = []
        for side, row, inner in ((0, 0, 1), (1, ROWS - 1, ROWS - 2)):
            m, gm, w, q = (rims[pl.ds((block * RIM + side * 4 + i) * 8, 8), :] for i in range(4))
            face, link = (links[pl.ds((block * LINKS + side * 2 + i) * 8, 8), :] for i in range(2))
            v = s_rows[row] * w
            flux = face * (east(v) - v)
            found.append((m + v, gm + v + (flux - west(flux)) - link * v + s_rows[inner] * q))
        for place in range(2):
            at = pl.ds(place * levels + block * 8, 8)
            near_ref[at, :], far_ref[at, :] = dealt(even, found[0][place], found[1][place])
    copy_s.wait()


def inverse_of(values):
    guess = pl.reciprocal(values, approx=True)
    guess = guess * (2.0 - values * guess)
    return guess * (2.0 - values * guess)


def columns_body(levels, weight_hbm, kmt_hbm, source_hbm, kvert_hbm, land_hbm, links_hbm, m0_hbm, w_hbm, rim_hbm,
                 weight, kmt, source, kvert, land, links, m0, w, ratio, rims, in_sems, out_sems):
    width = source.shape[1]
    parts = 4
    chunk = levels // parts
    small = loads(((weight_hbm, weight), (kmt_hbm, kmt)), in_sems)
    parted = [in_parts(far, near, parts) for far, near in ((land_hbm, land), (kvert_hbm, kvert), (source_hbm, source))]
    big = loads([pairs[i] for i in range(parts) for pairs in parted], in_sems, 2)
    links_copy = loads([(links_hbm, links)], in_sems, 2 + 3 * parts)[0]
    small[0].wait()
    total = weight_sum(weight, levels)
    shape = (ROWS * width // 128, 128)
    inverse = 1.0 / jnp.full(shape, total, FLOAT)
    small[1].wait()
    depth = stacked(kmt[...])

    def sea(k):
        return jnp.where(k < depth, stacked(land[rows_at(k), :]), 0).astype(FLOAT)

    def down(k, carry):
        here, link, m_in, w_in = carry
        at = level_at(k, width)
        below = jnp.where(k + 1 < levels, sea(jnp.minimum(k + 1, levels - 1)), 0.0)
        coupling = stacked(kvert[rows_at(k), :]) * here * below
        over = inverse_of(1.0 + coupling + link)
        m_here = (stacked(source[rows_at(k), :]) + m_in) * over
        w_here = (here * (weight[k] * inverse) + w_in) * over
        part = coupling * over
        ratio[at, :] = part
        m0[at, :] = m_here
        w[at, :] = w_here
        return below, coupling - coupling * part, coupling * m_here, coupling * w_here

    zero = jnp.zeros(shape, FLOAT)
    big[0].wait()
    carry = (sea(0), zero, zero, zero)
    for i in range(parts):
        big[3 * i + 1].wait()
        big[3 * i + 2].wait()
        if i + 1 < parts:
            big[3 * i + 3].wait()
        carry = lax.fori_loop(i * chunk, (i + 1) * chunk, down, carry, unroll=4)

    def up(i, carry):
        at = level_at(levels - 1 - i, width)
        m_below, w_below = carry
        part = ratio[at, :]
        m_here = m0[at, :] + part * m_below
        w_here = w[at, :] + part * w_below
        m0[at, :] = m_here
        w[at, :] = w_here
        return m_here, w_here

    carry = (zero, zero)
    outs = []
    for i in range(parts):
        carry = lax.fori_loop(i * chunk, (i + 1) * chunk, up, carry, unroll=4)
        size = chunk * shape[0]
        whole = pl.ds((parts - 1 - i) * size, size)
        for a, (near, far) in enumerate(((m0, m0_hbm), (w, w_hbm))):
            copy = pltpu.make_async_copy(near.at[whole], far.at[whole], out_sems.at[i * 2 + a])
            copy.start()
            outs.append(copy)
    links_copy.wait()
    for block in range(levels // 8):
        for side, row, inner in ((0, 0, 1), (1, ROWS - 1, ROWS - 2)):
            m, w_row = row_of(m0, block, row, width), row_of(w, block, row, width)
            face, link = (links[pl.ds((block * LINKS + side * 2 + i) * 8, 8), :] for i in range(2))
            flux = face * (east(m) - m)
            gm = m + (flux - west(flux)) + link * (row_of(m0, block, inner, width) - m)
            q = link * row_of(w, block, inner, width)
            for i, values in enumerate((m, gm, w_row, q)):
                rims[pl.ds((block * RIM + side * 4 + i) * 8, 8), :] = values
        whole = pl.ds(block * RIM * 8, RIM * 8)
        outs += loads([(rims.at[whole], rim_hbm.at[whole])], out_sems, 2 * parts + block)
    for copy in outs:
        copy.wait()


def inner_body(levels, s_ref, kmt_hbm, m0_hbm, w_hbm, kappa_hbm, land_hbm, u2_ref, kmt, m0, w, kappa, land, sems):
    parts = 4
    kmt_copy = loads([(kmt_hbm, kmt)], sems)[0]
    pairs = ((kappa_hbm, kappa), (land_hbm, land), (m0_hbm, m0), (w_hbm, w))
    parted = [in_parts(far, near, parts) for far, near in pairs]
    copies = loads([pairs[i] for i in range(parts) for pairs in parted], sems, 1)
    s = s_ref[...]
    kmt_copy.wait()
    depth = kmt[...]
    inside = row_index(s) < ROWS - 1

    def face(here, there):
        return jnp.where(jnp.minimum(here, there) > 0.0, here + there, 0.0)

    def level(k):
        at = rows_at(k)
        sea = jnp.where(k < depth, land[at, :], 0) > 0
        half = jnp.where(sea, 0.5 * kappa[at, :], 0.0)
        fx = face(half, east(half))
        fn = jnp.where(inside, face(half, north(half)), 0.0)
        fw, fs = west(fx), south(fn)
        keep = 1.0 - (fx + fw) - (fn + fs)
        brick = level_at(k, s.shape[1])
        u = unstacked(m0[brick, :]) + s * unstacked(w[brick, :])
        for _ in range(2):
            u = keep * u + (fx * east(u) + fw * west(u)) + (fn * north(u) + fs * south(u))
        return u

    def group(i, carry):
        for values, k in [(level(2 * i + j), 2 * i + j) for j in range(2)]:
            u2_ref[rows_at(k), :] = values
        return carry

    chunk = levels // 2 // parts
    for i in range(parts):
        for copy in copies[4 * i : 4 * i + 4]:
            copy.wait()
        lax.fori_loop(i * chunk, (i + 1) * chunk, group, 0)


def finish_body(levels, u2, links, own_near, own_far, near, far, faces,
                out, change_ref, buffer, sems):
    width = own_near.shape[1]
    tall = width // 128 * ROWS
    rows = lax.broadcasted_iota(jnp.int32, (ROWS, width), 0)
    on_rim = (rows < 2) | (rows >= ROWS - 2)
    even = is_even()
    copies = []
    for block in range(levels // 8):
        at, below = pl.ds(block * 8, 8), pl.ds(levels + block * 8, 8)

        def pairs(a, b):
            return [dealt(even, a[part, :], b[part, :]) for part in (at, below)]

        own, other = pairs(own_near, own_far), pairs(near, far)
        for side, row, inner in ((0, 0, 1), (1, ROWS - 1, ROWS - 2)):
            face = faces[pl.ds(side * levels + block * 8, 8), :]
            change = face * (other[0][side] - own[0][side])
            along, link = (links[pl.ds((block * LINKS + side * 2 + i) * 8, 8), :] for i in range(2))
            flux = along * (east(change) - change)
            passed = link * change
            on_row = (change + (flux - west(flux)) - passed
                      + face * (other[1][side] - own[1][side] - 2.0 * change))
            for j in range(width // 128):
                lanes = slice(j * 128, (j + 1) * 128)
                change_ref[pl.ds(j * ROWS + row, 8, stride=tall), :] = on_row[:, lanes]
                change_ref[pl.ds(j * ROWS + inner, 8, stride=tall), :] = passed[:, lanes]
        for k in range(8):
            level = block * 8 + k
            change = jnp.where(on_rim, unstacked(change_ref[level_at(k, width), :]), 0.0)
            buffer[rows_at(level), :] = u2[rows_at(level), :] + change
        whole = pl.ds(block * 8 * ROWS, 8 * ROWS)
        copy = pltpu.make_async_copy(buffer.at[whole], out.at[whole], sems.at[block])
        copy.start()
        copies.append(copy)
    for copy in copies:
        copy.wait()


def exchange(to_near, to_far):
    count = lax.axis_size("tile")

    def swap(array, start):
        firsts = range(start, count - 1, 2)
        return lax.ppermute(array, "tile", [(i, i + 1) for i in firsts] + [(i + 1, i) for i in firsts])

    from_far = swap(to_far, 1)
    return swap(to_near, 0), from_far


def body(ct_tracer, ct_surface, kappa, kvert, land, kmt, screen, layer_weight):
    levels, rows, width = ct_tracer.shape
    count = lax.axis_size("tile")
    tall = levels * rows
    tile, brick, flat = (rows, width), (tall * width // 128, 128), (tall, width)
    rim, rim_rows, link_rows = (2 * levels, width), (levels * RIM, width), (levels * LINKS, width)
    scalars, whole = pltpu.SMEM((levels,), FLOAT), pltpu.VMEM(flat, FLOAT)
    ints, tile_ints = pltpu.VMEM(flat, jnp.int32), pltpu.VMEM(tile, jnp.int32)
    bricks, tiles = pltpu.VMEM(brick, FLOAT), pltpu.VMEM(tile, FLOAT)
    ct_tracer, kappa, kvert, land = (left(a.reshape(flat)) for a in (ct_tracer, kappa, kvert, land))
    kmt, layer_weight = left(kmt), left(layer_weight)
    semaphores = pltpu.SemaphoreType.DMA

    height, surface, s_fx, s_fn, s_dg, q1, base, to_near, to_far, rim_near, rim_far, links = kernel(
        functools.partial(setup_body, levels), vmem(*[tile] * 9, rim, rim) + hbm(link_rows), in_hbm(6),
        in_vmem(11) + in_hbm(1), "setup",
        [scalars, ints, tile_ints, tiles, whole, bricks, bricks, pltpu.VMEM(link_rows, FLOAT), semaphores((12,)),
         semaphores((1,))],
    )(layer_weight, land, kmt, left(ct_surface), left(screen), kappa)
    near, far = exchange(to_near, to_far)
    rim_other_near, rim_other_far = exchange(rim_near, rim_far)

    basis, sums = kernel(
        basis_body, vmem((3 * rows, width), (8, 128)), in_vmem(9), in_vmem(2), "basis"
    )(base, height, surface, s_fx, s_fn, s_dg, q1, near, far)
    sums = lax.all_gather(sums, "tile", axis=0, tiled=True)

    m0, w, rims = kernel(
        functools.partial(columns_body, levels), hbm(brick, brick, rim_rows), in_hbm(6), in_hbm(3), "columns",
        [scalars, tile_ints, whole, whole, ints, pltpu.VMEM(link_rows, FLOAT), bricks, bricks, bricks,
         pltpu.VMEM(rim_rows, FLOAT), semaphores((15,)), semaphores((8 + levels // 8,))],
    )(layer_weight, kmt, ct_tracer, kvert, land, left(links))

    solution, s, row_near, row_far, faces = kernel(
        functools.partial(edges_body, levels, count), hbm(tile) + vmem(tile, rim, rim, rim),
        in_vmem(6) + in_hbm(2), in_hbm(1) + in_vmem(4), "edges",
        [pltpu.VMEM(rim_rows, FLOAT), pltpu.VMEM(link_rows, FLOAT),
         semaphores((levels // 4 + 1,))],
    )(sums, basis, rim_near, rim_far, rim_other_near, rim_other_far, left(rims), left(links))
    other_near, other_far = exchange(row_near, row_far)
    u2 = kernel(
        functools.partial(inner_body, levels), vmem(flat), in_vmem(1) + in_hbm(5), in_vmem(1), "inner",
        [tile_ints, bricks, bricks, whole, ints, semaphores((17,))],
    )(s, kmt, left(m0), left(w), kappa, land)[0]

    values = kernel(
        functools.partial(finish_body, levels), hbm(flat), in_vmem(7), in_hbm(1), "finish",
        [pltpu.VMEM((8 * rows * width // 128, 128), FLOAT), whole, semaphores((levels // 8,))],
    )(u2, held(links), row_near, row_far, other_near, other_far, faces)[0]
    return (values.reshape(levels, rows, width), solution)


def solution(mesh):
    in_specs = (
        P(None, ("grp", "tile"), None),
        P(("grp", "tile"), None),
        P(None, "tile", None),
        P(None, "tile", None),
        P(None, "tile", None),
        P("tile", None),
        P("tile", None),
        P(),
    )
    out_specs = (P(None, ("grp", "tile"), None), P(("grp", "tile"), None))
    return jax.shard_map(body, mesh=mesh, in_specs=in_specs, out_specs=out_specs, check_vma=False)
```

```python
import functools

import jax
import jax.numpy as jnp
from jax import lax
from jax.experimental import pallas as pl
from jax.experimental.pallas import tpu as pltpu
from jax.sharding import PartitionSpec as P

ITERS = 3
ROWS = 8
LOW = 0.05
HIGH = 9.0
MID = 0.5 * (HIGH + LOW)
HALF = 0.5 * (HIGH - LOW)
FLOAT = jnp.float32
LINKS = 4
LIMIT = 24 * 1024 * 1024


def east(values):
    return pltpu.roll(values, values.shape[1] - 1, 1)


def west(values):
    return pltpu.roll(values, 1, 1)


def north(values):
    return pltpu.roll(values, values.shape[0] - 1, 0)


def south(values):
    return pltpu.roll(values, 1, 0)


def stacked(values):
    return jnp.concatenate([values[:, i : i + 128] for i in range(0, values.shape[1], 128)], axis=0)


def unstacked(values):
    return jnp.concatenate([values[i : i + ROWS, :] for i in range(0, values.shape[0], ROWS)], axis=1)


def row_of(ref, block, row, width):
    tall = width // 128 * ROWS
    return jnp.concatenate(
        [ref[pl.ds(block * 8 * tall + j * ROWS + row, 8, stride=tall), :] for j in range(width // 128)], axis=1
    )


def level_at(k, width):
    tall = width // 128 * ROWS
    return pl.ds(pl.multiple_of(k * tall, tall), tall)


def rows_at(k):
    return pl.ds(pl.multiple_of(k * ROWS, ROWS), ROWS)


def row_index(values):
    return lax.broadcasted_iota(jnp.int32, values.shape, 0)


def spread(row, like):
    return jnp.broadcast_to(row, like.shape)


def vmem(*shapes):
    return [pltpu.VMEM(shape, FLOAT) for shape in shapes]


def hbm(*shapes):
    return [pltpu.HBM(shape, FLOAT) for shape in shapes]


def in_vmem(count):
    return [pl.BlockSpec(memory_space=pltpu.VMEM)] * count


def in_hbm(count):
    return [pl.BlockSpec(memory_space=pltpu.HBM)] * count


def kernel(body, outs, ins, out_specs, name, scratch=(), cost=1):
    return pl.pallas_call(
        body,
        out_shape=outs,
        in_specs=ins,
        out_specs=out_specs,
        scratch_shapes=list(scratch),
        name=name,
        cost_estimate=pl.CostEstimate(flops=cost, bytes_accessed=cost, transcendentals=0),
        compiler_params=pltpu.CompilerParams(vmem_limit_bytes=LIMIT),
    )


def held(array):
    return pltpu.with_memory_space_constraint(array, pltpu.VMEM)


def left(array):
    return pltpu.with_memory_space_constraint(array, pltpu.HBM)


def is_even():
    return lax.rem(lax.axis_index("tile"), 2) == 0


def dealt(even, low, high):
    return jnp.where(even, high, low), jnp.where(even, low, high)


def loads(pairs, sems, first=0):
    copies = [pltpu.make_async_copy(far, near, sems.at[first + i]) for i, (far, near) in enumerate(pairs)]
    for copy in copies:
        copy.start()
    return copies


def in_parts(far, near, parts):
    size = far.shape[0] // parts
    return [(far.at[pl.ds(i * size, size)], near.at[pl.ds(i * size, size)]) for i in range(parts)]


def weight_sum(weight, levels):
    total = weight[0]
    for k in range(1, levels):
        total = total + weight[k]
    return total


def setup_body(levels, weight_hbm, land_hbm, kmt_hbm, ct_hbm, screen_hbm, height_ref, surface_ref,
               fx_ref, fn_ref, dg_ref, q1_ref, base_ref, near_ref, far_ref, wet_bricks,
               weight, land, kmt, screen, sems):
    chunk = levels // 4
    small = loads(((weight_hbm, weight), (kmt_hbm, kmt)), sems)
    land_copies = loads(in_parts(land_hbm, land, 4), sems, 2)
    small += loads(((ct_hbm, base_ref), (screen_hbm, screen)), sems, 6)
    small[0].wait()
    total = weight_sum(weight, levels)
    small[1].wait()
    depth = kmt[...]
    width = depth.shape[1]
    height = jnp.zeros(depth.shape, FLOAT)
    for i, copy in enumerate(land_copies):
        copy.wait()

        def level(k, height):
            wet = jnp.where(k < depth, land[rows_at(k), :], 0).astype(FLOAT)
            wet_bricks[level_at(k, width), :] = stacked(wet)
            return height + weight[k] * wet

        height = lax.fori_loop(i * chunk, (i + 1) * chunk, level, height, unroll=4)
    height = height / total
    surface = jnp.where(0 < depth, land[0:ROWS, :], 0).astype(FLOAT)
    height_ref[...] = height
    surface_ref[...] = surface
    small[2].wait()
    small[3].wait()
    base = base_ref[...]
    rows = row_index(base)
    scale = 0.5 / HALF
    fx = scale * (height + east(height)) * surface * east(surface)
    fn = scale * (height + north(height)) * surface * north(surface)
    fn = jnp.where(rows < ROWS - 1, fn, 0.0)
    fs = south(fn)
    fw = west(fx)
    dg = (screen[...] - MID) * (1.0 / HALF) + fx + fw + fn + fs

    def apply(v):
        return dg * v - fx * east(v) - fw * west(v) - fn * north(v) - fs * south(v)

    q1 = apply(base)
    q2 = apply(q1)
    fx_ref[...] = fx
    fn_ref[...] = fn
    dg_ref[...] = dg
    q1_ref[...] = q1
    even = is_even()
    near_ref[7:8, :] = jnp.zeros_like(base[0:1, :])
    far_ref[7:8, :] = jnp.zeros_like(base[0:1, :])
    for place, values in enumerate((base, q1, q2, fx, dg, height, surface)):
        at = slice(place, place + 1)
        near_ref[at, :], far_ref[at, :] = dealt(even, values[0:1, :], values[ROWS - 1 : ROWS, :])


def rims_body(levels, kappa_hbm, wet_bricks, near_ref, far_ref, links_hbm, kappa, kappa_bricks, links, sems):
    chunk = levels // 4
    width = kappa.shape[1]
    for i, copy in enumerate(loads(in_parts(kappa_hbm, kappa, 4), sems)):
        copy.wait()

        def brick(k, carry):
            kappa_bricks[level_at(k, width), :] = stacked(kappa[rows_at(k), :])
            return carry

        lax.fori_loop(i * chunk, (i + 1) * chunk, brick, 0, unroll=4)
    even = is_even()
    outs = []
    for block in range(levels // 8):
        found = []
        for side, row, inner in ((0, 0, 1), (1, ROWS - 1, ROWS - 2)):
            kap, kap_in = row_of(kappa_bricks, block, row, width), row_of(kappa_bricks, block, inner, width)
            here, here_in = row_of(wet_bricks, block, row, width), row_of(wet_bricks, block, inner, width)
            at = (block * LINKS + side * 2) * 8
            links[pl.ds(at, 8), :] = 0.5 * (kap + east(kap)) * here * east(here)
            links[pl.ds(at + 8, 8), :] = 0.5 * (kap + kap_in) * here * here_in
            found.append((kap, here))
        for place in range(2):
            at = pl.ds(place * levels + block * 8, 8)
            near_ref[at, :], far_ref[at, :] = dealt(even, found[0][place], found[1][place])
        whole = pl.ds(block * LINKS * 8, LINKS * 8)
        outs += loads([(links.at[whole], links_hbm.at[whole])], sems, 4 + block)
    for copy in outs:
        copy.wait()


def basis_body(count, ct, height, surface, fx_ref, fn_ref, dg_ref, q1_ref, near, far, links_hbm, basis_ref, sums_ref):
    even = is_even()
    b0 = ct[...]
    rows = row_index(b0)
    first, last = rows == 0, rows == ROWS - 1
    fx, fn, dg = fx_ref[...], fn_ref[...], dg_ref[...]
    fw, fs = west(fx), south(fn)

    def halo(values, row):
        b0_h, q1_h, q2_h, fx_h, dg_h, high_h, wet_h = (values[i : i + 1, :] for i in range(7))
        face = (0.5 / HALF) * (high_h + height[row : row + 1, :]) * wet_h * surface[row : row + 1, :]
        extra = face * (b0_h - ct[row : row + 1, :])
        return b0_h, q1_h + extra, q2_h, fx_h, dg_h, face, extra

    def lift(row):
        return jnp.broadcast_to(row, b0.shape)

    before, after = dealt(even, near[...], far[...])
    sides = (halo(before, 0), halo(after, ROWS - 1))
    face_b, face_a = lift(sides[0][5]), lift(sides[1][5])
    b1 = q1_ref[...] - jnp.where(first, lift(sides[0][6]), 0.0) - jnp.where(last, lift(sides[1][6]), 0.0)
    dg = dg + jnp.where(first, face_b, 0.0) + jnp.where(last, face_a, 0.0)
    fn = jnp.where(last, face_a, fn)
    fs = jnp.where(first, face_b, fs)

    def apply(v, v_before, v_after):
        v_n = jnp.where(last, lift(v_after), north(v))
        v_s = jnp.where(first, lift(v_before), south(v))
        return dg * v - fx * east(v) - fw * west(v) - fn * v_n - fs * v_s

    b2 = 2.0 * apply(b1, sides[0][1], sides[1][1]) - b0

    def outer(side, own):
        b0_h, b1_h, q2_h, fx_h, dg_h, face, extra = side
        b0_h, b1_h, q2_h, fx_h, dg_h, face, extra, own = (lift(v) for v in (b0_h, b1_h, q2_h, fx_h, dg_h, face, extra, own))
        turned = dg_h * extra - fx_h * east(extra) - west(fx_h) * west(extra)
        return (2.0 * (q2_h + turned + face * (b1_h - own)) - b0_h)[0:1, :]

    for place, values in enumerate((b0, b1, b2)):
        basis_ref[pl.ds(place * ROWS, ROWS), :] = values
    b2_b = outer(sides[0], b1[0:1, :])
    b2_a = outer(sides[1], b1[ROWS - 1 : ROWS, :])
    next2 = apply(b2, b2_b, b2_a)
    tile_rows = lax.broadcasted_iota(jnp.int32, (8, 128), 0)
    packed = jnp.zeros((8, 128), FLOAT)
    for place, (p, q) in enumerate(((b0, b0), (b0, b1), (b1, b1), (b1, b2), (b2, b2), (b2, next2))):
        product = p * q
        folded = product[:, 0:128]
        for j in range(1, product.shape[1] // 128):
            folded = folded + product[:, j * 128 : (j + 1) * 128]
        packed = jnp.where(tile_rows == place, jnp.sum(folded, axis=0, keepdims=True), packed)
    for j in range(count):
        sums_ref[j * 8 : (j + 1) * 8, :] = packed


def quadratic(left, form):
    total = None
    for i in range(3):
        for j in range(3):
            if left[i] is not None and left[j] is not None:
                term = left[i] * left[j] * form[i][j]
                total = term if total is None else total + term
    return total


def plus(p, q):
    return q if p is None else p if q is None else p + q


def times(scale, p):
    return None if p is None else scale * p


def weights(sums):
    s0, s1, s2, s3, s4, s5 = sums
    g02 = 2.0 * s2 - s0
    gram = ((s0, s1, g02), (s1, s2, s3), (g02, s3, s4))
    b11, b12 = 0.5 * (s3 + s1), 0.5 * (s4 + g02)
    shift = ((s1, s2, s3), (s2, b11, b12), (s3, b12, s5))
    form = [[MID * gram[i][j] + HALF * shift[i][j] for j in range(3)] for i in range(3)]
    one = jnp.ones_like(s0)
    x, r, d = [None] * 3, [one, None, None], [one, None, None]
    rr = s0
    for step in range(ITERS):
        alpha = jnp.clip(rr / quadratic(d, form), 1.0 / HIGH, 1.0 / LOW)
        x = [plus(x[i], times(alpha, d[i])) for i in range(3)]
        if step + 1 < ITERS:
            image = [
                plus(times(MID, d[0]), times(0.5 * HALF, d[1])),
                plus(plus(times(MID, d[1]), times(HALF, d[0])), times(0.5 * HALF, d[2])),
                plus(times(MID, d[2]), times(0.5 * HALF, d[1])),
            ]
            r = [plus(r[i], times(-1.0, times(alpha, image[i]))) for i in range(3)]
            new = quadratic(r, gram)
            beta = jnp.clip(new / rr, 0.0, HIGH / LOW)
            d = [plus(r[i], times(beta, d[i])) for i in range(3)]
            rr = new
    return x


def inverse_of(values):
    guess = pl.reciprocal(values, approx=True)
    guess = guess * (2.0 - values * guess)
    return guess * (2.0 - values * guess)


def columns_body(levels, count, sums, basis_ref, weight_hbm, kmt_hbm, source_hbm, kvert_hbm, land_hbm, links_hbm,
                 out_hbm, u, near_ref, far_ref, weight, kmt, source, kvert, land, links, s_ref, ratio, sems, out_sems):
    width = source.shape[1]
    parts = 4
    chunk = levels // parts
    small = loads(((weight_hbm, weight), (kmt_hbm, kmt)), sems)
    parted = [in_parts(far, near, parts) for far, near in ((land_hbm, land), (kvert_hbm, kvert), (source_hbm, source))]
    big = loads([pairs[i] for i in range(parts) for pairs in parted], sems, 2)
    links_copy = loads([(links_hbm, links)], sems, 2 + 3 * parts)[0]

    tile_sums = sums[0:8, :]
    for j in range(1, count):
        tile_sums = tile_sums + sums[j * 8 : (j + 1) * 8, :]
    tile_sums = jnp.sum(tile_sums, axis=1, keepdims=True)
    mix = weights([tile_sums[i : i + 1, :] for i in range(6)])
    b0, b1, b2 = (basis_ref[i * ROWS : (i + 1) * ROWS, :] for i in range(3))
    s = mix[0] * b0 + mix[1] * b1 + mix[2] * b2
    s_ref[...] = s
    outs = loads([(s_ref, out_hbm)], out_sems)

    small[0].wait()
    scaled = stacked(s) / jnp.full((ROWS * width // 128, 128), weight_sum(weight, levels), FLOAT)
    small[1].wait()
    depth = stacked(kmt[...])

    def sea(k):
        return jnp.where(k < depth, stacked(land[rows_at(k), :]), 0).astype(FLOAT)

    def down(k, carry):
        here, link, passed = carry
        at = level_at(k, width)
        below = jnp.where(k + 1 < levels, sea(jnp.minimum(k + 1, levels - 1)), 0.0)
        coupling = stacked(kvert[rows_at(k), :]) * here * below
        over = inverse_of(1.0 + coupling + link)
        value = (stacked(source[rows_at(k), :]) + here * (weight[k] * scaled) + passed) * over
        part = coupling * over
        ratio[at, :] = part
        u[at, :] = value
        return below, coupling - coupling * part, coupling * value

    zero = jnp.zeros(scaled.shape, FLOAT)
    big[0].wait()
    carry = (sea(0), zero, zero)
    for i in range(parts):
        big[3 * i + 1].wait()
        big[3 * i + 2].wait()
        if i + 1 < parts:
            big[3 * i + 3].wait()
        carry = lax.fori_loop(i * chunk, (i + 1) * chunk, down, carry, unroll=4)

    def up(i, below):
        at = level_at(levels - 1 - i, width)
        value = u[at, :] + ratio[at, :] * below
        u[at, :] = value
        return value

    lax.fori_loop(0, levels, up, zero, unroll=4)
    links_copy.wait()
    even = is_even()
    for block in range(levels // 8):
        found = []
        for side, row, inner in ((0, 0, 1), (1, ROWS - 1, ROWS - 2)):
            value, value_in = row_of(u, block, row, width), row_of(u, block, inner, width)
            face, link = (links[pl.ds((block * LINKS + side * 2 + i) * 8, 8), :] for i in range(2))
            flux = face * (east(value) - value)
            found.append((value, value + (flux - west(flux)) + link * (value_in - value)))
        for place in range(2):
            at = pl.ds(place * levels + block * 8, 8)
            near_ref[at, :], far_ref[at, :] = dealt(even, found[0][place], found[1][place])
    for copy in outs:
        copy.wait()


def inner_body(levels, u0, kmt_hbm, kappa_hbm, land_hbm, u2_ref, kmt, kappa, land, sems):
    parts = 4
    kmt_copy = loads([(kmt_hbm, kmt)], sems)[0]
    pairs = ((kappa_hbm, kappa), (land_hbm, land))
    parted = [in_parts(far, near, parts) for far, near in pairs]
    copies = loads([pairs[i] for i in range(parts) for pairs in parted], sems, 1)
    kmt_copy.wait()
    depth = kmt[...]
    width = depth.shape[1]
    inside = row_index(depth) < ROWS - 1

    def face(here, there):
        return jnp.where(jnp.minimum(here, there) > 0.0, here + there, 0.0)

    def level(k):
        at = rows_at(k)
        sea = jnp.where(k < depth, land[at, :], 0) > 0
        half = jnp.where(sea, 0.5 * kappa[at, :], 0.0)
        fx = face(half, east(half))
        fn = jnp.where(inside, face(half, north(half)), 0.0)
        fw, fs = west(fx), south(fn)
        keep = 1.0 - (fx + fw) - (fn + fs)
        u = unstacked(u0[level_at(k, width), :])
        for _ in range(2):
            u = keep * u + (fx * east(u) + fw * west(u)) + (fn * north(u) + fs * south(u))
        return u

    def group(i, carry):
        for values, k in [(level(2 * i + j), 2 * i + j) for j in range(2)]:
            u2_ref[rows_at(k), :] = values
        return carry

    chunk = levels // 2 // parts
    for i in range(parts):
        for copy in copies[2 * i : 2 * i + 2]:
            copy.wait()
        lax.fori_loop(i * chunk, (i + 1) * chunk, group, 0)


def finish_body(levels, u2, links, own_near, own_far, rim_near, rim_far, near, far, rim_other_near, rim_other_far,
                out, change_ref, buffer, sems):
    width = own_near.shape[1]
    tall = width // 128 * ROWS
    rows = lax.broadcasted_iota(jnp.int32, (ROWS, width), 0)
    on_rim = (rows < 2) | (rows >= ROWS - 2)
    even = is_even()
    copies = []
    for block in range(levels // 8):
        at, below = pl.ds(block * 8, 8), pl.ds(levels + block * 8, 8)

        def pairs(a, b):
            return [dealt(even, a[part, :], b[part, :]) for part in (at, below)]

        own, rim = pairs(own_near, own_far), pairs(rim_near, rim_far)
        other, rim_other = pairs(near, far), pairs(rim_other_near, rim_other_far)
        for side, row, inner in ((0, 0, 1), (1, ROWS - 1, ROWS - 2)):
            face = 0.5 * (rim[0][side] + rim_other[0][side]) * rim[1][side] * rim_other[1][side]
            change = face * (other[0][side] - own[0][side])
            along, link = (links[pl.ds((block * LINKS + side * 2 + i) * 8, 8), :] for i in range(2))
            flux = along * (east(change) - change)
            passed = link * change
            on_row = (change + (flux - west(flux)) - passed
                      + face * (other[1][side] - own[1][side] - 2.0 * change))
            for j in range(width // 128):
                lanes = slice(j * 128, (j + 1) * 128)
                change_ref[pl.ds(j * ROWS + row, 8, stride=tall), :] = on_row[:, lanes]
                change_ref[pl.ds(j * ROWS + inner, 8, stride=tall), :] = passed[:, lanes]
        for k in range(8):
            level = block * 8 + k
            change = jnp.where(on_rim, unstacked(change_ref[level_at(k, width), :]), 0.0)
            buffer[rows_at(level), :] = u2[rows_at(level), :] + change
        whole = pl.ds(block * 8 * ROWS, 8 * ROWS)
        copy = pltpu.make_async_copy(buffer.at[whole], out.at[whole], sems.at[block])
        copy.start()
        copies.append(copy)
    for copy in copies:
        copy.wait()


def exchange(to_near, to_far):
    count = lax.axis_size("tile")

    def swap(array, start):
        firsts = range(start, count - 1, 2)
        return lax.ppermute(array, "tile", [(i, i + 1) for i in firsts] + [(i + 1, i) for i in firsts])

    from_far = swap(to_far, 1)
    return swap(to_near, 0), from_far


def body(ct_tracer, ct_surface, kappa, kvert, land, kmt, screen, layer_weight):
    levels, rows, width = ct_tracer.shape
    count = lax.axis_size("tile")
    tall = levels * rows
    tile, brick, flat = (rows, width), (tall * width // 128, 128), (tall, width)
    rim, link_rows = (2 * levels, width), (levels * LINKS, width)
    scalars, whole = pltpu.SMEM((levels,), FLOAT), pltpu.VMEM(flat, FLOAT)
    ints, tile_ints = pltpu.VMEM(flat, jnp.int32), pltpu.VMEM(tile, jnp.int32)
    bricks, tiles = pltpu.VMEM(brick, FLOAT), pltpu.VMEM(tile, FLOAT)
    ct_tracer, kappa, kvert, land = (left(a.reshape(flat)) for a in (ct_tracer, kappa, kvert, land))
    kmt, layer_weight = left(kmt), left(layer_weight)
    semaphores = pltpu.SemaphoreType.DMA

    height, surface, s_fx, s_fn, s_dg, q1, base, to_near, to_far, wet = kernel(
        functools.partial(setup_body, levels), vmem(*[tile] * 9, brick), in_hbm(5), in_vmem(10), "setup",
        [scalars, ints, tile_ints, tiles, semaphores((8,))],
    )(layer_weight, land, kmt, left(ct_surface), left(screen))
    near, far = exchange(to_near, to_far)

    rim_near, rim_far, links = kernel(
        functools.partial(rims_body, levels), vmem(rim, rim) + hbm(link_rows), in_hbm(1) + in_vmem(1),
        in_vmem(2) + in_hbm(1), "rims", [whole, bricks, pltpu.VMEM(link_rows, FLOAT), semaphores((4 + levels // 8,))],
    )(kappa, wet)
    links = left(links)
    rim_other_near, rim_other_far = exchange(rim_near, rim_far)

    basis, sums = kernel(
        functools.partial(basis_body, count), vmem((3 * rows, width), (8 * count, 128)), in_vmem(9) + in_hbm(1),
        in_vmem(2), "basis"
    )(base, height, surface, s_fx, s_fn, s_dg, q1, near, far, links)
    sums = lax.all_to_all(sums.reshape(count, 8, 128), "tile", 0, 0, tiled=True).reshape(8 * count, 128)

    solution, u0, row_near, row_far = kernel(
        functools.partial(columns_body, levels, count), hbm(tile) + vmem(brick, rim, rim), in_vmem(2) + in_hbm(6),
        in_hbm(1) + in_vmem(3), "columns",
        [scalars, tile_ints, whole, whole, ints, pltpu.VMEM(link_rows, FLOAT), tiles, bricks, semaphores((15,)),
         semaphores((1,))],
    )(sums, basis, layer_weight, kmt, ct_tracer, kvert, land, links)
    other_near, other_far = exchange(row_near, row_far)
    u2 = kernel(
        functools.partial(inner_body, levels), vmem(flat), in_vmem(1) + in_hbm(3), in_vmem(1), "inner",
        [tile_ints, whole, ints, semaphores((9,))],
    )(u0, kmt, kappa, land)[0]

    values = kernel(
        functools.partial(finish_body, levels), hbm(flat), in_vmem(10), in_hbm(1), "finish",
        [pltpu.VMEM((8 * rows * width // 128, 128), FLOAT), whole, semaphores((levels // 8,))],
    )(u2, held(links), row_near, row_far, rim_near, rim_far, other_near, other_far, rim_other_near, rim_other_far)[0]
    return (values.reshape(levels, rows, width), solution)


def solution(mesh):
    in_specs = (
        P(None, ("grp", "tile"), None),
        P(("grp", "tile"), None),
        P(None, "tile", None),
        P(None, "tile", None),
        P(None, "tile", None),
        P("tile", None),
        P("tile", None),
        P(),
    )
    out_specs = (P(None, ("grp", "tile"), None), P(("grp", "tile"), None))
    return jax.shard_map(body, mesh=mesh, in_specs=in_specs, out_specs=out_specs, check_vma=False)
```

```python
import functools

import jax
import jax.numpy as jnp
from jax import lax
from jax.experimental import pallas as pl
from jax.experimental.pallas import tpu as pltpu
from jax.sharding import PartitionSpec as P

ITERS = 3
ROWS = 8
LOW = 0.05
HIGH = 9.0
MID = 0.5 * (HIGH + LOW)
HALF = 0.5 * (HIGH - LOW)
FLOAT = jnp.float32
LINKS = 4
LIMIT = 24 * 1024 * 1024


def east(values):
    return pltpu.roll(values, values.shape[1] - 1, 1)


def west(values):
    return pltpu.roll(values, 1, 1)


def north(values):
    return pltpu.roll(values, values.shape[0] - 1, 0)


def south(values):
    return pltpu.roll(values, 1, 0)


def stacked(values):
    return jnp.concatenate([values[:, i : i + 128] for i in range(0, values.shape[1], 128)], axis=0)


def unstacked(values):
    return jnp.concatenate([values[i : i + ROWS, :] for i in range(0, values.shape[0], ROWS)], axis=1)


def row_of(ref, block, row, width):
    tall = width // 128 * ROWS
    return jnp.concatenate(
        [ref[pl.ds(block * 8 * tall + j * ROWS + row, 8, stride=tall), :] for j in range(width // 128)], axis=1
    )


def level_at(k, width):
    tall = width // 128 * ROWS
    return pl.ds(pl.multiple_of(k * tall, tall), tall)


def rows_at(k):
    return pl.ds(pl.multiple_of(k * ROWS, ROWS), ROWS)


def row_index(values):
    return lax.broadcasted_iota(jnp.int32, values.shape, 0)


def spread(row, like):
    return jnp.broadcast_to(row, like.shape)


def vmem(*shapes):
    return [pltpu.VMEM(shape, FLOAT) for shape in shapes]


def hbm(*shapes):
    return [pltpu.HBM(shape, FLOAT) for shape in shapes]


def in_vmem(count):
    return [pl.BlockSpec(memory_space=pltpu.VMEM)] * count


def in_hbm(count):
    return [pl.BlockSpec(memory_space=pltpu.HBM)] * count


def kernel(body, outs, ins, out_specs, name, scratch=(), cost=1, aliases={}):
    return pl.pallas_call(
        body,
        out_shape=outs,
        in_specs=ins,
        out_specs=out_specs,
        scratch_shapes=list(scratch),
        name=name,
        input_output_aliases=aliases,
        cost_estimate=pl.CostEstimate(flops=cost, bytes_accessed=cost, transcendentals=0),
        compiler_params=pltpu.CompilerParams(vmem_limit_bytes=LIMIT),
    )


def held(array):
    return pltpu.with_memory_space_constraint(array, pltpu.VMEM)


def left(array):
    return pltpu.with_memory_space_constraint(array, pltpu.HBM)


def is_even():
    return lax.rem(lax.axis_index("tile"), 2) == 0


def dealt(even, low, high):
    return jnp.where(even, high, low), jnp.where(even, low, high)


def loads(pairs, sems, first=0):
    copies = [pltpu.make_async_copy(far, near, sems.at[first + i]) for i, (far, near) in enumerate(pairs)]
    for copy in copies:
        copy.start()
    return copies


def in_parts(far, near, parts):
    size = far.shape[0] // parts
    return [(far.at[pl.ds(i * size, size)], near.at[pl.ds(i * size, size)]) for i in range(parts)]


def weight_sum(weight, levels):
    total = weight[0]
    for k in range(1, levels):
        total = total + weight[k]
    return total


def setup_body(levels, weight_hbm, land_hbm, kmt_hbm, ct_hbm, screen_hbm, height_ref, surface_ref,
               fx_ref, fn_ref, dg_ref, q1_ref, base_ref, near_ref, far_ref, wet_bricks,
               weight, land, kmt, screen, sems):
    chunk = levels // 4
    small = loads(((weight_hbm, weight), (kmt_hbm, kmt)), sems)
    land_copies = loads(in_parts(land_hbm, land, 4), sems, 2)
    small += loads(((ct_hbm, base_ref), (screen_hbm, screen)), sems, 6)
    small[0].wait()
    total = weight_sum(weight, levels)
    small[1].wait()
    depth = kmt[...]
    width = depth.shape[1]
    height = jnp.zeros(depth.shape, FLOAT)
    for i, copy in enumerate(land_copies):
        copy.wait()

        def level(k, height):
            wet = jnp.where(k < depth, land[rows_at(k), :], 0).astype(FLOAT)
            wet_bricks[level_at(k, width), :] = stacked(wet)
            return height + weight[k] * wet

        height = lax.fori_loop(i * chunk, (i + 1) * chunk, level, height, unroll=4)
    height = height / total
    surface = jnp.where(0 < depth, land[0:ROWS, :], 0).astype(FLOAT)
    height_ref[...] = height
    surface_ref[...] = surface
    small[2].wait()
    small[3].wait()
    base = base_ref[...]
    rows = row_index(base)
    scale = 0.5 / HALF
    fx = scale * (height + east(height)) * surface * east(surface)
    fn = scale * (height + north(height)) * surface * north(surface)
    fn = jnp.where(rows < ROWS - 1, fn, 0.0)
    fs = south(fn)
    fw = west(fx)
    dg = (screen[...] - MID) * (1.0 / HALF) + fx + fw + fn + fs

    def apply(v):
        return dg * v - fx * east(v) - fw * west(v) - fn * north(v) - fs * south(v)

    q1 = apply(base)
    q2 = apply(q1)
    fx_ref[...] = fx
    fn_ref[...] = fn
    dg_ref[...] = dg
    q1_ref[...] = q1
    even = is_even()
    near_ref[7:8, :] = jnp.zeros_like(base[0:1, :])
    far_ref[7:8, :] = jnp.zeros_like(base[0:1, :])
    for place, values in enumerate((base, q1, q2, fx, dg, height, surface)):
        at = slice(place, place + 1)
        near_ref[at, :], far_ref[at, :] = dealt(even, values[0:1, :], values[ROWS - 1 : ROWS, :])


def rims_body(levels, kappa_hbm, wet_bricks, near_ref, far_ref, links_hbm, kappa, kappa_bricks, links, sems):
    chunk = levels // 4
    width = kappa.shape[1]
    for i, copy in enumerate(loads(in_parts(kappa_hbm, kappa, 4), sems)):
        copy.wait()

        def brick(k, carry):
            kappa_bricks[level_at(k, width), :] = stacked(kappa[rows_at(k), :])
            return carry

        lax.fori_loop(i * chunk, (i + 1) * chunk, brick, 0, unroll=4)
    even = is_even()
    outs = []
    for block in range(levels // 8):
        found = []
        for side, row, inner in ((0, 0, 1), (1, ROWS - 1, ROWS - 2)):
            kap, kap_in = row_of(kappa_bricks, block, row, width), row_of(kappa_bricks, block, inner, width)
            here, here_in = row_of(wet_bricks, block, row, width), row_of(wet_bricks, block, inner, width)
            at = (block * LINKS + side * 2) * 8
            links[pl.ds(at, 8), :] = 0.5 * (kap + east(kap)) * here * east(here)
            links[pl.ds(at + 8, 8), :] = 0.5 * (kap + kap_in) * here * here_in
            found.append((kap, here))
        for place in range(2):
            at = pl.ds(place * levels + block * 8, 8)
            near_ref[at, :], far_ref[at, :] = dealt(even, found[0][place], found[1][place])
        whole = pl.ds(block * LINKS * 8, LINKS * 8)
        outs += loads([(links.at[whole], links_hbm.at[whole])], sems, 4 + block)
    for copy in outs:
        copy.wait()


def basis_body(ct, height, surface, fx_ref, fn_ref, dg_ref, q1_ref, near, far, links_hbm, basis_ref, sums_ref):
    even = is_even()
    b0 = ct[...]
    rows = row_index(b0)
    first, last = rows == 0, rows == ROWS - 1
    fx, fn, dg = fx_ref[...], fn_ref[...], dg_ref[...]
    fw, fs = west(fx), south(fn)

    def halo(values, row):
        b0_h, q1_h, q2_h, fx_h, dg_h, high_h, wet_h = (values[i : i + 1, :] for i in range(7))
        face = (0.5 / HALF) * (high_h + height[row : row + 1, :]) * wet_h * surface[row : row + 1, :]
        extra = face * (b0_h - ct[row : row + 1, :])
        return b0_h, q1_h + extra, q2_h, fx_h, dg_h, face, extra

    def lift(row):
        return jnp.broadcast_to(row, b0.shape)

    before, after = dealt(even, near[...], far[...])
    sides = (halo(before, 0), halo(after, ROWS - 1))
    face_b, face_a = lift(sides[0][5]), lift(sides[1][5])
    b1 = q1_ref[...] - jnp.where(first, lift(sides[0][6]), 0.0) - jnp.where(last, lift(sides[1][6]), 0.0)
    dg = dg + jnp.where(first, face_b, 0.0) + jnp.where(last, face_a, 0.0)
    fn = jnp.where(last, face_a, fn)
    fs = jnp.where(first, face_b, fs)

    def apply(v, v_before, v_after):
        v_n = jnp.where(last, lift(v_after), north(v))
        v_s = jnp.where(first, lift(v_before), south(v))
        return dg * v - fx * east(v) - fw * west(v) - fn * v_n - fs * v_s

    b2 = 2.0 * apply(b1, sides[0][1], sides[1][1]) - b0

    def outer(side, own):
        b0_h, b1_h, q2_h, fx_h, dg_h, face, extra = side
        b0_h, b1_h, q2_h, fx_h, dg_h, face, extra, own = (lift(v) for v in (b0_h, b1_h, q2_h, fx_h, dg_h, face, extra, own))
        turned = dg_h * extra - fx_h * east(extra) - west(fx_h) * west(extra)
        return (2.0 * (q2_h + turned + face * (b1_h - own)) - b0_h)[0:1, :]

    for place, values in enumerate((b0, b1, b2)):
        basis_ref[pl.ds(place * ROWS, ROWS), :] = values
    b2_b = outer(sides[0], b1[0:1, :])
    b2_a = outer(sides[1], b1[ROWS - 1 : ROWS, :])
    next2 = apply(b2, b2_b, b2_a)
    lanes = lax.broadcasted_iota(jnp.int32, (1, 128), 1)
    packed = jnp.zeros((1, 128), FLOAT)
    for place, (p, q) in enumerate(((b0, b0), (b0, b1), (b1, b1), (b1, b2), (b2, b2), (b2, next2))):
        product = p * q
        folded = product[:, 0:128]
        for j in range(1, product.shape[1] // 128):
            folded = folded + product[:, j * 128 : (j + 1) * 128]
        total = jnp.sum(jnp.sum(folded, axis=0, keepdims=True), axis=1, keepdims=True)
        packed = jnp.where(lanes == place, total, packed)
    sums_ref[...] = jnp.broadcast_to(packed, sums_ref.shape)


def quadratic(left, form):
    total = None
    for i in range(3):
        for j in range(3):
            if left[i] is not None and left[j] is not None:
                term = left[i] * left[j] * form[i][j]
                total = term if total is None else total + term
    return total


def plus(p, q):
    return q if p is None else p if q is None else p + q


def times(scale, p):
    return None if p is None else scale * p


def weights(sums):
    s0, s1, s2, s3, s4, s5 = sums
    g02 = 2.0 * s2 - s0
    gram = ((s0, s1, g02), (s1, s2, s3), (g02, s3, s4))
    b11, b12 = 0.5 * (s3 + s1), 0.5 * (s4 + g02)
    shift = ((s1, s2, s3), (s2, b11, b12), (s3, b12, s5))
    form = [[MID * gram[i][j] + HALF * shift[i][j] for j in range(3)] for i in range(3)]
    one = jnp.ones_like(s0)
    x, r, d = [None] * 3, [one, None, None], [one, None, None]
    rr = s0
    for step in range(ITERS):
        alpha = jnp.clip(rr / quadratic(d, form), 1.0 / HIGH, 1.0 / LOW)
        x = [plus(x[i], times(alpha, d[i])) for i in range(3)]
        if step + 1 < ITERS:
            image = [
                plus(times(MID, d[0]), times(0.5 * HALF, d[1])),
                plus(plus(times(MID, d[1]), times(HALF, d[0])), times(0.5 * HALF, d[2])),
                plus(times(MID, d[2]), times(0.5 * HALF, d[1])),
            ]
            r = [plus(r[i], times(-1.0, times(alpha, image[i]))) for i in range(3)]
            new = quadratic(r, gram)
            beta = jnp.clip(new / rr, 0.0, HIGH / LOW)
            d = [plus(r[i], times(beta, d[i])) for i in range(3)]
            rr = new
    return x


def inverse_of(values):
    guess = pl.reciprocal(values, approx=True)
    guess = guess * (2.0 - values * guess)
    return guess * (2.0 - values * guess)


def send_rows(u, links, near_ref, far_ref, width):
    even = is_even()
    levels = near_ref.shape[0] // 2
    for block in range(levels // 8):
        found = []
        for side, row, inner in ((0, 0, 1), (1, ROWS - 1, ROWS - 2)):
            value, value_in = row_of(u, block, row, width), row_of(u, block, inner, width)
            face, link = (links[pl.ds((block * LINKS + side * 2 + i) * 8, 8), :] for i in range(2))
            flux = face * (east(value) - value)
            found.append((value, value + (flux - west(flux)) + link * (value_in - value)))
        for place in range(2):
            at = pl.ds(place * levels + block * 8, 8)
            near_ref[at, :], far_ref[at, :] = dealt(even, found[0][place], found[1][place])


def columns_body(levels, sums, basis_ref, weight_hbm, kmt_hbm, source_hbm, kvert_hbm, land_hbm, links_hbm,
                 out_hbm, high, ratio, low, links_high, near_ref, far_ref,
                 weight, kmt, source, kvert, land, links_low, s_ref, ratio_low, sems, out_sems):
    width = source.shape[1]
    parts = 4
    chunk = levels // parts
    half = levels // 2
    small = loads(((weight_hbm, weight), (kmt_hbm, kmt)), sems)
    parted = [in_parts(far, near, parts) for far, near in ((land_hbm, land), (kvert_hbm, kvert), (source_hbm, source))]
    big = loads([pairs[i] for i in range(parts) for pairs in parted], sems, 2)
    top, bottom = (pl.ds(i * half * LINKS, half * LINKS) for i in range(2))
    links_copies = loads([(links_hbm.at[bottom], links_low), (links_hbm.at[top], links_high)], sems, 2 + 3 * parts)

    total = jnp.sum(sums[...], axis=0, keepdims=True)
    mix = weights([total[:, i : i + 1] for i in range(6)])
    b0, b1, b2 = (basis_ref[i * ROWS : (i + 1) * ROWS, :] for i in range(3))
    s = mix[0] * b0 + mix[1] * b1 + mix[2] * b2
    s_ref[...] = s
    outs = loads([(s_ref, out_hbm)], out_sems)

    small[0].wait()
    scaled = stacked(s) / jnp.full((ROWS * width // 128, 128), weight_sum(weight, levels), FLOAT)
    small[1].wait()
    depth = stacked(kmt[...])

    def sea(k):
        return jnp.where(k < depth, stacked(land[rows_at(k), :]), 0).astype(FLOAT)

    def down(values, parts_of, first, k, carry):
        here, link, passed = carry
        at = level_at(k - first, width)
        below = jnp.where(k + 1 < levels, sea(jnp.minimum(k + 1, levels - 1)), 0.0)
        coupling = stacked(kvert[rows_at(k), :]) * here * below
        over = inverse_of(1.0 + coupling + link)
        value = (stacked(source[rows_at(k), :]) + here * (weight[k] * scaled) + passed) * over
        part = coupling * over
        parts_of[at, :] = part
        values[at, :] = value
        return below, coupling - coupling * part, coupling * value

    zero = jnp.zeros(scaled.shape, FLOAT)
    big[0].wait()
    carry = (sea(0), zero, zero)
    for i in range(parts):
        big[3 * i + 1].wait()
        big[3 * i + 2].wait()
        if i + 1 < parts:
            big[3 * i + 3].wait()
        step = functools.partial(down, high, ratio, 0) if 2 * i < parts else functools.partial(down, low, ratio_low, half)
        carry = lax.fori_loop(i * chunk, (i + 1) * chunk, step, carry, unroll=4)
    ascend(low, low, ratio_low, zero, width)
    for copy in links_copies:
        copy.wait()
    send_rows(low, links_low, near_ref, far_ref, width)
    for copy in outs:
        copy.wait()


def ascend(target, source, ratio, below, width):
    levels = target.shape[0] * 128 // (ROWS * width)

    def up(i, below):
        at = level_at(levels - 1 - i, width)
        value = source[at, :] + ratio[at, :] * below
        target[at, :] = value
        return value

    lax.fori_loop(0, levels, up, below, unroll=4)


def upper_body(high, ratio, low, links, u, near_ref, far_ref):
    width = near_ref.shape[1]
    ascend(u, high, ratio, low[level_at(0, width), :], width)
    send_rows(u, links, near_ref, far_ref, width)


def inner_body(levels, high, low, kmt_hbm, kappa_hbm, land_hbm, u2_ref,
               kmt, kappa, land, fx_ref, fw_ref, fn_ref, fs_ref, keep_ref, u1_ref, sems):
    parts = 4
    half = levels // 2
    kmt_copy = loads([(kmt_hbm, kmt)], sems)[0]
    pairs = ((kappa_hbm, kappa), (land_hbm, land))
    parted = [in_parts(far, near, parts) for far, near in pairs]
    copies = loads([pairs[i] for i in range(parts) for pairs in parted], sems, 1)
    kmt_copy.wait()
    depth = kmt[...]
    width = depth.shape[1]
    inside = row_index(depth) < ROWS - 1

    def face(here, there):
        return jnp.where(jnp.minimum(here, there) > 0.0, here + there, 0.0)

    def coefficients(k, carry):
        at = rows_at(k)
        sea = jnp.where(k < depth, land[at, :], 0) > 0
        halved = jnp.where(sea, 0.5 * kappa[at, :], 0.0)
        fx = face(halved, east(halved))
        fn = jnp.where(inside, face(halved, north(halved)), 0.0)
        fw, fs = west(fx), south(fn)
        for ref, values in ((fx_ref, fx), (fw_ref, fw), (fn_ref, fn), (fs_ref, fs)):
            ref[at, :] = values
        keep_ref[at, :] = 1.0 - (fx + fw) - (fn + fs)
        return carry

    chunk = levels // parts
    for i in range(parts):
        for copy in copies[2 * i : 2 * i + 2]:
            copy.wait()
        lax.fori_loop(i * chunk, (i + 1) * chunk, coefficients, 0, unroll=2)

    def spread_out(u, at):
        return (keep_ref[at, :] * u + (fx_ref[at, :] * east(u) + fw_ref[at, :] * west(u))
                + (fn_ref[at, :] * north(u) + fs_ref[at, :] * south(u)))

    for first, part in ((0, high), (half, low)):

        def once(k, carry):
            at = rows_at(k + first)
            u1_ref[at, :] = spread_out(unstacked(part[level_at(k, width), :]), at)
            return carry

        lax.fori_loop(0, half, once, 0, unroll=2)

    def twice(k, carry):
        at = rows_at(k)
        u2_ref[at, :] = spread_out(u1_ref[at, :], at)
        return carry

    lax.fori_loop(0, levels, twice, 0, unroll=2)


def finish_body(levels, first, last, skipped, u2, links, own_near, own_far, near, far, rim_near, rim_far, rim_other_near, rim_other_far,
                *refs):
    out, change_ref, buffer, sems = refs[-4:]
    width = own_near.shape[1]
    tall = width // 128 * ROWS
    count = last - first
    rows = lax.broadcasted_iota(jnp.int32, (ROWS, width), 0)
    on_rim = (rows < 2) | (rows >= ROWS - 2)
    even = is_even()
    copies = []
    for block in range(count // 8):
        at, below = pl.ds(block * 8, 8), pl.ds(count + block * 8, 8)

        def pairs(a, b):
            return [dealt(even, a[part, :], b[part, :]) for part in (at, below)]

        own, other = pairs(own_near, own_far), pairs(near, far)
        kap, wet, kap_other, wet_other = (
            dealt(even, a[pl.ds(part * levels + first + block * 8, 8), :], b[pl.ds(part * levels + first + block * 8, 8), :])
            for a, b in ((rim_near, rim_far), (rim_other_near, rim_other_far)) for part in range(2)
        )
        for side, row, inner in ((0, 0, 1), (1, ROWS - 1, ROWS - 2)):
            face = 0.5 * (kap[side] + kap_other[side]) * wet[side] * wet_other[side]
            change = face * (other[0][side] - own[0][side])
            along, link = (
                links[pl.ds(((skipped + block) * LINKS + side * 2 + i) * 8, 8), :] for i in range(2)
            )
            flux = along * (east(change) - change)
            passed = link * change
            on_row = (change + (flux - west(flux)) - passed
                      + face * (other[1][side] - own[1][side] - 2.0 * change))
            for j in range(width // 128):
                lanes = slice(j * 128, (j + 1) * 128)
                change_ref[pl.ds(j * ROWS + row, 8, stride=tall), :] = on_row[:, lanes]
                change_ref[pl.ds(j * ROWS + inner, 8, stride=tall), :] = passed[:, lanes]
        for k in range(8):
            here = block * 8 + k
            change = jnp.where(on_rim, unstacked(change_ref[level_at(k, width), :]), 0.0)
            buffer[rows_at(here), :] = u2[rows_at(first + here), :] + change
        whole = pl.ds(block * 8 * ROWS, 8 * ROWS)
        target = pl.ds((first + block * 8) * ROWS, 8 * ROWS)
        copies += loads([(buffer.at[whole], out.at[target])], sems, block)
    for copy in copies:
        copy.wait()


def exchange(to_near, to_far):
    count = lax.axis_size("tile")

    def swap(array, start):
        firsts = range(start, count - 1, 2)
        return lax.ppermute(array, "tile", [(i, i + 1) for i in firsts] + [(i + 1, i) for i in firsts])

    from_far = swap(to_far, 1)
    return swap(to_near, 0), from_far


def body(ct_tracer, ct_surface, kappa, kvert, land, kmt, screen, layer_weight):
    levels, rows, width = ct_tracer.shape
    count = lax.axis_size("tile")
    tall = levels * rows
    tile, brick, flat = (rows, width), (tall * width // 128, 128), (tall, width)
    rim, link_rows = (2 * levels, width), (levels * LINKS, width)
    scalars, whole = pltpu.SMEM((levels,), FLOAT), pltpu.VMEM(flat, FLOAT)
    ints, tile_ints = pltpu.VMEM(flat, jnp.int32), pltpu.VMEM(tile, jnp.int32)
    bricks, tiles = pltpu.VMEM(brick, FLOAT), pltpu.VMEM(tile, FLOAT)
    ct_tracer, kappa, kvert, land = (left(a.reshape(flat)) for a in (ct_tracer, kappa, kvert, land))
    kmt, layer_weight = left(kmt), left(layer_weight)
    semaphores = pltpu.SemaphoreType.DMA

    height, surface, s_fx, s_fn, s_dg, q1, base, to_near, to_far, wet = kernel(
        functools.partial(setup_body, levels), vmem(*[tile] * 9, brick), in_hbm(5), in_vmem(10), "setup",
        [scalars, ints, tile_ints, tiles, semaphores((8,))],
    )(layer_weight, land, kmt, left(ct_surface), left(screen))
    near, far = exchange(to_near, to_far)

    rim_near, rim_far, links = kernel(
        functools.partial(rims_body, levels), vmem(rim, rim) + hbm(link_rows), in_hbm(1) + in_vmem(1),
        in_vmem(2) + in_hbm(1), "rims", [whole, bricks, pltpu.VMEM(link_rows, FLOAT), semaphores((4 + levels // 8,))],
    )(kappa, wet)
    links_left = left(links)
    rim_other_near, rim_other_far = exchange(rim_near, rim_far)

    basis, sums = kernel(
        basis_body, vmem((3 * rows, width), (count, 128)), in_vmem(9) + in_hbm(1),
        in_vmem(2), "basis"
    )(base, height, surface, s_fx, s_fn, s_dg, q1, near, far, links_left)
    sums = lax.all_to_all(sums.reshape(count, 1, 128), "tile", 0, 0, tiled=True).reshape(count, 128)

    rims = (rim_near, rim_far, rim_other_near, rim_other_far)
    half = levels // 2
    halved = lambda shape: (shape[0] // 2, shape[1])
    half_bricks, half_links = halved(brick), halved(link_rows)
    solution, carried, ratio, low, links_high, low_near, low_far = kernel(
        functools.partial(columns_body, levels),
        hbm(tile) + vmem(half_bricks, half_bricks, half_bricks, half_links, halved(rim), halved(rim)),
        in_vmem(2) + in_hbm(6), in_hbm(1) + in_vmem(6), "columns",
        [scalars, tile_ints, whole, whole, ints, pltpu.VMEM(half_links, FLOAT), tiles, pltpu.VMEM(half_bricks, FLOAT),
         semaphores((16,)), semaphores((1,))],
    )(sums, basis, layer_weight, kmt, ct_tracer, kvert, land, links_left)
    low_other_near, low_other_far = exchange(low_near, low_far)
    high, high_near, high_far = kernel(
        upper_body, vmem(half_bricks, halved(rim), halved(rim)), in_vmem(4), in_vmem(3), "upper_columns"
    )(carried, ratio, low, links_high)
    high_other_near, high_other_far = exchange(high_near, high_far)
    u2 = kernel(
        functools.partial(inner_body, levels), vmem(flat), in_vmem(2) + in_hbm(3), in_vmem(1), "inner",
        [tile_ints, whole, ints] + [whole] * 6 + [semaphores((9,))],
    )(high, low, kmt, kappa, land)[0]

    scratch = [
        pltpu.VMEM((8 * rows * width // 128, 128), FLOAT), pltpu.VMEM(halved(flat), FLOAT), semaphores((half // 8,))
    ]
    deep = kernel(
        functools.partial(finish_body, levels, half, levels, half // 8), hbm(flat), in_vmem(10), in_hbm(1), "finish_low", scratch,
    )(u2, held(links), low_near, low_far, low_other_near, low_other_far, *rims)[0]
    values = kernel(
        functools.partial(finish_body, levels, 0, half, 0), hbm(flat), in_vmem(10) + in_hbm(1), in_hbm(1), "finish_high",
        scratch, aliases={10: 0},
    )(u2, links_high, high_near, high_far, high_other_near, high_other_far, *rims, left(deep))[0]
    return (values.reshape(levels, rows, width), solution)


def solution(mesh):
    in_specs = (
        P(None, ("grp", "tile"), None),
        P(("grp", "tile"), None),
        P(None, "tile", None),
        P(None, "tile", None),
        P(None, "tile", None),
        P("tile", None),
        P("tile", None),
        P(),
    )
    out_specs = (P(None, ("grp", "tile"), None), P(("grp", "tile"), None))
    return jax.shard_map(body, mesh=mesh, in_specs=in_specs, out_specs=out_specs, check_vma=False)
```

```python
import functools

import jax
import jax.numpy as jnp
from jax import lax
from jax.experimental import pallas as pl
from jax.experimental.pallas import tpu as pltpu
from jax.sharding import PartitionSpec as P

ITERS = 3
ROWS = 8
LOW = 0.05
HIGH = 9.0
MID = 0.5 * (HIGH + LOW)
HALF = 0.5 * (HIGH - LOW)
FLOAT = jnp.float32
LINKS = 4
LIMIT = 24 * 1024 * 1024


def east(values):
    return pltpu.roll(values, values.shape[1] - 1, 1)


def west(values):
    return pltpu.roll(values, 1, 1)


def north(values):
    return pltpu.roll(values, values.shape[0] - 1, 0)


def south(values):
    return pltpu.roll(values, 1, 0)


def stacked(values):
    return jnp.concatenate([values[:, i : i + 128] for i in range(0, values.shape[1], 128)], axis=0)


def unstacked(values):
    return jnp.concatenate([values[i : i + ROWS, :] for i in range(0, values.shape[0], ROWS)], axis=1)


def padded(shape):
    return (shape[0] + 2 * ROWS, shape[1])


def clear_pads(ref):
    zero = jnp.zeros((ROWS, ref.shape[1]), FLOAT)
    ref[0:ROWS, :] = zero
    ref[ref.shape[0] - ROWS :, :] = zero


def within(ref):
    return ref.at[pl.ds(ROWS, ref.shape[0] - 2 * ROWS)]


def lane_index(values):
    return lax.broadcasted_iota(jnp.int32, values.shape, 1)


def east_of(values):
    turned = pltpu.roll(values, 127, 1)
    further = jnp.concatenate([turned[ROWS:, :], turned[:ROWS, :]], axis=0)
    return jnp.where(lane_index(values) == 127, further, turned)


def west_of(values):
    turned = pltpu.roll(values, 1, 1)
    further = jnp.concatenate([turned[-ROWS:, :], turned[:-ROWS, :]], axis=0)
    return jnp.where(lane_index(values) == 0, further, turned)


def row_of(ref, block, row, width):
    tall = width // 128 * ROWS
    return jnp.concatenate(
        [ref[pl.ds(block * 8 * tall + j * ROWS + row, 8, stride=tall), :] for j in range(width // 128)], axis=1
    )


def level_at(k, width):
    tall = width // 128 * ROWS
    return pl.ds(pl.multiple_of(k * tall, tall), tall)


def rows_at(k):
    return pl.ds(pl.multiple_of(k * ROWS, ROWS), ROWS)


def row_index(values):
    return lax.broadcasted_iota(jnp.int32, values.shape, 0)


def spread(row, like):
    return jnp.broadcast_to(row, like.shape)


def vmem(*shapes):
    return [pltpu.VMEM(shape, FLOAT) for shape in shapes]


def hbm(*shapes):
    return [pltpu.HBM(shape, FLOAT) for shape in shapes]


def in_vmem(count):
    return [pl.BlockSpec(memory_space=pltpu.VMEM)] * count


def in_hbm(count):
    return [pl.BlockSpec(memory_space=pltpu.HBM)] * count


def kernel(body, outs, ins, out_specs, name, scratch=(), cost=1, aliases={}):
    return pl.pallas_call(
        body,
        out_shape=outs,
        in_specs=ins,
        out_specs=out_specs,
        scratch_shapes=list(scratch),
        name=name,
        input_output_aliases=aliases,
        cost_estimate=pl.CostEstimate(flops=cost, bytes_accessed=cost, transcendentals=0),
        compiler_params=pltpu.CompilerParams(vmem_limit_bytes=LIMIT),
    )


def held(array):
    return pltpu.with_memory_space_constraint(array, pltpu.VMEM)


def left(array):
    return pltpu.with_memory_space_constraint(array, pltpu.HBM)


def is_even():
    return lax.rem(lax.axis_index("tile"), 2) == 0


def dealt(even, low, high):
    return jnp.where(even, high, low), jnp.where(even, low, high)


def loads(pairs, sems, first=0):
    copies = [pltpu.make_async_copy(far, near, sems.at[first + i]) for i, (far, near) in enumerate(pairs)]
    for copy in copies:
        copy.start()
    return copies


def in_parts(far, near, parts):
    size = far.shape[0] // parts
    return [(far.at[pl.ds(i * size, size)], near.at[pl.ds(i * size, size)]) for i in range(parts)]


def weight_sum(weight, levels):
    total = weight[0]
    for k in range(1, levels):
        total = total + weight[k]
    return total


def setup_body(levels, weight_hbm, land_hbm, kmt_hbm, ct_hbm, screen_hbm, height_ref, surface_ref,
               fx_ref, fn_ref, dg_ref, q1_ref, base_ref, near_ref, far_ref, wet_bricks,
               weight, land, kmt, screen, sems):
    chunk = levels // 4
    small = loads(((weight_hbm, weight), (kmt_hbm, kmt)), sems)
    land_copies = loads(in_parts(land_hbm, land, 4), sems, 2)
    small += loads(((ct_hbm, base_ref), (screen_hbm, screen)), sems, 6)
    small[0].wait()
    total = weight_sum(weight, levels)
    small[1].wait()
    depth = kmt[...]
    width = depth.shape[1]
    height = jnp.zeros(depth.shape, FLOAT)
    for i, copy in enumerate(land_copies):
        copy.wait()

        def level(k, height):
            wet = jnp.where(k < depth, land[rows_at(k), :], 0).astype(FLOAT)
            wet_bricks[level_at(k, width), :] = stacked(wet)
            return height + weight[k] * wet

        height = lax.fori_loop(i * chunk, (i + 1) * chunk, level, height, unroll=4)
    height = height / total
    surface = jnp.where(0 < depth, land[0:ROWS, :], 0).astype(FLOAT)
    height_ref[...] = height
    surface_ref[...] = surface
    small[2].wait()
    small[3].wait()
    base = base_ref[...]
    rows = row_index(base)
    scale = 0.5 / HALF
    fx = scale * (height + east(height)) * surface * east(surface)
    fn = scale * (height + north(height)) * surface * north(surface)
    fn = jnp.where(rows < ROWS - 1, fn, 0.0)
    fs = south(fn)
    fw = west(fx)
    dg = (screen[...] - MID) * (1.0 / HALF) + fx + fw + fn + fs

    def apply(v):
        return dg * v - fx * east(v) - fw * west(v) - fn * north(v) - fs * south(v)

    q1 = apply(base)
    q2 = apply(q1)
    fx_ref[...] = fx
    fn_ref[...] = fn
    dg_ref[...] = dg
    q1_ref[...] = q1
    even = is_even()
    near_ref[7:8, :] = jnp.zeros_like(base[0:1, :])
    far_ref[7:8, :] = jnp.zeros_like(base[0:1, :])
    for place, values in enumerate((base, q1, q2, fx, dg, height, surface)):
        at = slice(place, place + 1)
        near_ref[at, :], far_ref[at, :] = dealt(even, values[0:1, :], values[ROWS - 1 : ROWS, :])


def rims_body(levels, kappa_hbm, wet_bricks, near_ref, far_ref, links_hbm, kappa, kappa_bricks, links, sems):
    chunk = levels // 4
    width = kappa.shape[1]
    for i, copy in enumerate(loads(in_parts(kappa_hbm, kappa, 4), sems)):
        copy.wait()

        def brick(k, carry):
            kappa_bricks[level_at(k, width), :] = stacked(kappa[rows_at(k), :])
            return carry

        lax.fori_loop(i * chunk, (i + 1) * chunk, brick, 0, unroll=4)
    even = is_even()
    outs = []
    for block in range(levels // 8):
        found = []
        for side, row, inner in ((0, 0, 1), (1, ROWS - 1, ROWS - 2)):
            kap, kap_in = row_of(kappa_bricks, block, row, width), row_of(kappa_bricks, block, inner, width)
            here, here_in = row_of(wet_bricks, block, row, width), row_of(wet_bricks, block, inner, width)
            at = (block * LINKS + side * 2) * 8
            links[pl.ds(at, 8), :] = 0.5 * (kap + east(kap)) * here * east(here)
            links[pl.ds(at + 8, 8), :] = 0.5 * (kap + kap_in) * here * here_in
            found.append((kap, here))
        for place in range(2):
            at = pl.ds(place * levels + block * 8, 8)
            near_ref[at, :], far_ref[at, :] = dealt(even, found[0][place], found[1][place])
        whole = pl.ds(block * LINKS * 8, LINKS * 8)
        outs += loads([(links.at[whole], links_hbm.at[whole])], sems, 4 + block)
    for copy in outs:
        copy.wait()


def basis_body(ct, height, surface, fx_ref, fn_ref, dg_ref, q1_ref, near, far, links_hbm, basis_ref, sums_ref):
    even = is_even()
    b0 = ct[...]
    rows = row_index(b0)
    first, last = rows == 0, rows == ROWS - 1
    fx, fn, dg = fx_ref[...], fn_ref[...], dg_ref[...]
    fw, fs = west(fx), south(fn)

    def halo(values, row):
        b0_h, q1_h, q2_h, fx_h, dg_h, high_h, wet_h = (values[i : i + 1, :] for i in range(7))
        face = (0.5 / HALF) * (high_h + height[row : row + 1, :]) * wet_h * surface[row : row + 1, :]
        extra = face * (b0_h - ct[row : row + 1, :])
        return b0_h, q1_h + extra, q2_h, fx_h, dg_h, face, extra

    def lift(row):
        return jnp.broadcast_to(row, b0.shape)

    before, after = dealt(even, near[...], far[...])
    sides = (halo(before, 0), halo(after, ROWS - 1))
    face_b, face_a = lift(sides[0][5]), lift(sides[1][5])
    b1 = q1_ref[...] - jnp.where(first, lift(sides[0][6]), 0.0) - jnp.where(last, lift(sides[1][6]), 0.0)
    dg = dg + jnp.where(first, face_b, 0.0) + jnp.where(last, face_a, 0.0)
    fn = jnp.where(last, face_a, fn)
    fs = jnp.where(first, face_b, fs)

    def apply(v, v_before, v_after):
        v_n = jnp.where(last, lift(v_after), north(v))
        v_s = jnp.where(first, lift(v_before), south(v))
        return dg * v - fx * east(v) - fw * west(v) - fn * v_n - fs * v_s

    b2 = 2.0 * apply(b1, sides[0][1], sides[1][1]) - b0

    def outer(side, own):
        b0_h, b1_h, q2_h, fx_h, dg_h, face, extra = side
        b0_h, b1_h, q2_h, fx_h, dg_h, face, extra, own = (lift(v) for v in (b0_h, b1_h, q2_h, fx_h, dg_h, face, extra, own))
        turned = dg_h * extra - fx_h * east(extra) - west(fx_h) * west(extra)
        return (2.0 * (q2_h + turned + face * (b1_h - own)) - b0_h)[0:1, :]

    for place, values in enumerate((b0, b1, b2)):
        basis_ref[pl.ds(place * ROWS, ROWS), :] = values
    b2_b = outer(sides[0], b1[0:1, :])
    b2_a = outer(sides[1], b1[ROWS - 1 : ROWS, :])
    next2 = apply(b2, b2_b, b2_a)
    lanes = lax.broadcasted_iota(jnp.int32, (1, 128), 1)
    packed = jnp.zeros((1, 128), FLOAT)
    for place, (p, q) in enumerate(((b0, b0), (b0, b1), (b1, b1), (b1, b2), (b2, b2), (b2, next2))):
        product = p * q
        folded = product[:, 0:128]
        for j in range(1, product.shape[1] // 128):
            folded = folded + product[:, j * 128 : (j + 1) * 128]
        total = jnp.sum(jnp.sum(folded, axis=0, keepdims=True), axis=1, keepdims=True)
        packed = jnp.where(lanes == place, total, packed)
    sums_ref[...] = jnp.broadcast_to(packed, sums_ref.shape)


def quadratic(left, form):
    total = None
    for i in range(3):
        for j in range(3):
            if left[i] is not None and left[j] is not None:
                term = left[i] * left[j] * form[i][j]
                total = term if total is None else total + term
    return total


def plus(p, q):
    return q if p is None else p if q is None else p + q


def times(scale, p):
    return None if p is None else scale * p


def weights(sums):
    s0, s1, s2, s3, s4, s5 = sums
    g02 = 2.0 * s2 - s0
    gram = ((s0, s1, g02), (s1, s2, s3), (g02, s3, s4))
    b11, b12 = 0.5 * (s3 + s1), 0.5 * (s4 + g02)
    shift = ((s1, s2, s3), (s2, b11, b12), (s3, b12, s5))
    form = [[MID * gram[i][j] + HALF * shift[i][j] for j in range(3)] for i in range(3)]
    one = jnp.ones_like(s0)
    x, r, d = [None] * 3, [one, None, None], [one, None, None]
    rr = s0
    for step in range(ITERS):
        alpha = jnp.clip(rr / quadratic(d, form), 1.0 / HIGH, 1.0 / LOW)
        x = [plus(x[i], times(alpha, d[i])) for i in range(3)]
        if step + 1 < ITERS:
            image = [
                plus(times(MID, d[0]), times(0.5 * HALF, d[1])),
                plus(plus(times(MID, d[1]), times(HALF, d[0])), times(0.5 * HALF, d[2])),
                plus(times(MID, d[2]), times(0.5 * HALF, d[1])),
            ]
            r = [plus(r[i], times(-1.0, times(alpha, image[i]))) for i in range(3)]
            new = quadratic(r, gram)
            beta = jnp.clip(new / rr, 0.0, HIGH / LOW)
            d = [plus(r[i], times(beta, d[i])) for i in range(3)]
            rr = new
    return x


def inverse_of(values):
    guess = pl.reciprocal(values, approx=True)
    guess = guess * (2.0 - values * guess)
    return guess * (2.0 - values * guess)


def send_rows(u, links, near_ref, far_ref, width):
    even = is_even()
    levels = near_ref.shape[0] // 2
    for block in range(levels // 8):
        found = []
        for side, row, inner in ((0, 0, 1), (1, ROWS - 1, ROWS - 2)):
            value, value_in = row_of(u, block, row, width), row_of(u, block, inner, width)
            face, link = (links[pl.ds((block * LINKS + side * 2 + i) * 8, 8), :] for i in range(2))
            flux = face * (east(value) - value)
            found.append((value, value + (flux - west(flux)) + link * (value_in - value)))
        for place in range(2):
            at = pl.ds(place * levels + block * 8, 8)
            near_ref[at, :], far_ref[at, :] = dealt(even, found[0][place], found[1][place])


def columns_body(levels, sums, basis_ref, weight_hbm, kmt_hbm, source_hbm, kvert_hbm, land_hbm, links_hbm,
                 out_hbm, high, ratio, low_ref, links_high, near_ref, far_ref,
                 weight, kmt, source, kvert, land, links_low, s_ref, ratio_low, sems, out_sems):
    width = source.shape[1]
    parts = 4
    chunk = levels // parts
    half = levels // 2
    low = within(low_ref)
    clear_pads(low_ref)
    small = loads(((weight_hbm, weight), (kmt_hbm, kmt)), sems)
    parted = [in_parts(far, near, parts) for far, near in ((land_hbm, land), (kvert_hbm, kvert), (source_hbm, source))]
    big = loads([pairs[i] for i in range(parts) for pairs in parted], sems, 2)
    top, bottom = (pl.ds(i * half * LINKS, half * LINKS) for i in range(2))
    links_copies = loads([(links_hbm.at[bottom], links_low), (links_hbm.at[top], links_high)], sems, 2 + 3 * parts)

    total = jnp.sum(sums[...], axis=0, keepdims=True)
    mix = weights([total[:, i : i + 1] for i in range(6)])
    b0, b1, b2 = (basis_ref[i * ROWS : (i + 1) * ROWS, :] for i in range(3))
    s = mix[0] * b0 + mix[1] * b1 + mix[2] * b2
    s_ref[...] = s
    outs = loads([(s_ref, out_hbm)], out_sems)

    small[0].wait()
    scaled = stacked(s) / jnp.full((ROWS * width // 128, 128), weight_sum(weight, levels), FLOAT)
    small[1].wait()
    depth = stacked(kmt[...])

    def sea(k):
        return jnp.where(k < depth, stacked(land[rows_at(k), :]), 0).astype(FLOAT)

    def down(values, parts_of, first, k, carry):
        here, link, passed = carry
        at = level_at(k - first, width)
        below = jnp.where(k + 1 < levels, sea(jnp.minimum(k + 1, levels - 1)), 0.0)
        coupling = stacked(kvert[rows_at(k), :]) * here * below
        over = inverse_of(1.0 + coupling + link)
        value = (stacked(source[rows_at(k), :]) + here * (weight[k] * scaled) + passed) * over
        part = coupling * over
        parts_of[at, :] = part
        values[at, :] = value
        return below, coupling - coupling * part, coupling * value

    zero = jnp.zeros(scaled.shape, FLOAT)
    big[0].wait()
    carry = (sea(0), zero, zero)
    for i in range(parts):
        big[3 * i + 1].wait()
        big[3 * i + 2].wait()
        if i + 1 < parts:
            big[3 * i + 3].wait()
        step = functools.partial(down, high, ratio, 0) if 2 * i < parts else functools.partial(down, low, ratio_low, half)
        carry = lax.fori_loop(i * chunk, (i + 1) * chunk, step, carry, unroll=4)
    ascend(low, low, ratio_low, zero, width)
    for copy in links_copies:
        copy.wait()
    send_rows(low, links_low, near_ref, far_ref, width)
    for copy in outs:
        copy.wait()


def ascend(target, source, ratio, below, width):
    levels = target.shape[0] * 128 // (ROWS * width)

    def up(i, below):
        at = level_at(levels - 1 - i, width)
        value = source[at, :] + ratio[at, :] * below
        target[at, :] = value
        return value

    lax.fori_loop(0, levels, up, below, unroll=4)


def upper_body(high, ratio, low, links, u_ref, near_ref, far_ref):
    width = near_ref.shape[1]
    low, u = within(low), within(u_ref)
    clear_pads(u_ref)
    ascend(u, high, ratio, low[level_at(0, width), :], width)
    send_rows(u, links, near_ref, far_ref, width)


def inner_body(levels, high, low, kmt_hbm, kappa_hbm, land_hbm, u2_ref,
               kmt, kappa, land, halves_ref, fn_ref, u1_ref, sems):
    parts = 4
    half = levels // 2
    kmt_copy = loads([(kmt_hbm, kmt)], sems)[0]
    pairs = ((kappa_hbm, kappa), (land_hbm, land))
    parted = [in_parts(far, near, parts) for far, near in pairs]
    copies = loads([pairs[i] for i in range(parts) for pairs in parted], sems, 1)
    width = u2_ref.shape[1]
    tall = width // 128 * ROWS
    zero = jnp.zeros((ROWS, 128), FLOAT)
    for ref in (halves_ref, fn_ref, u1_ref):
        ref[0:ROWS, :] = zero
        for k in range(levels + 1):
            ref[pl.ds(ROWS + k * tall, ROWS), :] = zero
    kmt_copy.wait()
    depth = stacked(kmt[...])
    inside = lax.rem(row_index(depth), ROWS) < ROWS - 1

    def face(here, there):
        return jnp.where(jnp.minimum(here, there) > 0.0, here + there, 0.0)

    def shifted(ref, k):
        start = ROWS + k * tall
        return ref[pl.ds(start + 1, tall), :], ref[pl.ds(start - 1, tall), :]

    def level(source, first, k, carry):
        at = pl.ds(pl.multiple_of(ROWS + k * tall, ROWS), tall)
        sea = jnp.where(k < depth, stacked(land[rows_at(k), :]), 0) > 0
        halved = jnp.where(sea, 0.5 * stacked(kappa[rows_at(k), :]), 0.0)
        halves_ref[at, :] = halved
        fx = face(halved, east_of(halved))
        fn = jnp.where(inside, face(halved, shifted(halves_ref, k)[0]), 0.0)
        fn_ref[at, :] = fn
        fw, fs = west_of(fx), shifted(fn_ref, k)[1]
        keep = 1.0 - (fx + fw) - (fn + fs)
        u = source[pl.ds(pl.multiple_of(ROWS + (k - first) * tall, ROWS), tall), :]
        north, south = shifted(source, k - first)
        u = keep * u + (fx * east_of(u) + fw * west_of(u)) + (fn * north + fs * south)
        u1_ref[at, :] = u
        north, south = shifted(u1_ref, k)
        u = keep * u + (fx * east_of(u) + fw * west_of(u)) + (fn * north + fs * south)
        u2_ref[rows_at(k), :] = unstacked(u)
        return carry

    chunk = levels // parts
    for i in range(parts):
        for copy in copies[2 * i : 2 * i + 2]:
            copy.wait()
        source, first = (high, 0) if 2 * i < parts else (low, half)
        lax.fori_loop(i * chunk, (i + 1) * chunk, functools.partial(level, source, first), 0, unroll=2)


def finish_body(levels, first, last, skipped, u2, links, own_near, own_far, near, far, rim_near, rim_far, rim_other_near, rim_other_far,
                *refs):
    out, change_ref, buffer, sems = refs[-4:]
    width = own_near.shape[1]
    tall = width // 128 * ROWS
    count = last - first
    rows = lax.broadcasted_iota(jnp.int32, (ROWS, width), 0)
    on_rim = (rows < 2) | (rows >= ROWS - 2)
    even = is_even()
    copies = []
    for block in range(count // 8):
        at, below = pl.ds(block * 8, 8), pl.ds(count + block * 8, 8)

        def pairs(a, b):
            return [dealt(even, a[part, :], b[part, :]) for part in (at, below)]

        own, other = pairs(own_near, own_far), pairs(near, far)
        kap, wet, kap_other, wet_other = (
            dealt(even, a[pl.ds(part * levels + first + block * 8, 8), :], b[pl.ds(part * levels + first + block * 8, 8), :])
            for a, b in ((rim_near, rim_far), (rim_other_near, rim_other_far)) for part in range(2)
        )
        for side, row, inner in ((0, 0, 1), (1, ROWS - 1, ROWS - 2)):
            face = 0.5 * (kap[side] + kap_other[side]) * wet[side] * wet_other[side]
            change = face * (other[0][side] - own[0][side])
            along, link = (
                links[pl.ds(((skipped + block) * LINKS + side * 2 + i) * 8, 8), :] for i in range(2)
            )
            flux = along * (east(change) - change)
            passed = link * change
            on_row = (change + (flux - west(flux)) - passed
                      + face * (other[1][side] - own[1][side] - 2.0 * change))
            for j in range(width // 128):
                lanes = slice(j * 128, (j + 1) * 128)
                change_ref[pl.ds(j * ROWS + row, 8, stride=tall), :] = on_row[:, lanes]
                change_ref[pl.ds(j * ROWS + inner, 8, stride=tall), :] = passed[:, lanes]
        for k in range(8):
            here = block * 8 + k
            change = jnp.where(on_rim, unstacked(change_ref[level_at(k, width), :]), 0.0)
            buffer[rows_at(here), :] = u2[rows_at(first + here), :] + change
        whole = pl.ds(block * 8 * ROWS, 8 * ROWS)
        target = pl.ds((first + block * 8) * ROWS, 8 * ROWS)
        copies += loads([(buffer.at[whole], out.at[target])], sems, block)
    for copy in copies:
        copy.wait()


def exchange(to_near, to_far):
    count = lax.axis_size("tile")

    def swap(array, start):
        firsts = range(start, count - 1, 2)
        return lax.ppermute(array, "tile", [(i, i + 1) for i in firsts] + [(i + 1, i) for i in firsts])

    from_far = swap(to_far, 1)
    return swap(to_near, 0), from_far


def body(ct_tracer, ct_surface, kappa, kvert, land, kmt, screen, layer_weight):
    levels, rows, width = ct_tracer.shape
    count = lax.axis_size("tile")
    tall = levels * rows
    tile, brick, flat = (rows, width), (tall * width // 128, 128), (tall, width)
    rim, link_rows = (2 * levels, width), (levels * LINKS, width)
    scalars, whole = pltpu.SMEM((levels,), FLOAT), pltpu.VMEM(flat, FLOAT)
    ints, tile_ints = pltpu.VMEM(flat, jnp.int32), pltpu.VMEM(tile, jnp.int32)
    bricks, tiles = pltpu.VMEM(brick, FLOAT), pltpu.VMEM(tile, FLOAT)
    ct_tracer, kappa, kvert, land = (left(a.reshape(flat)) for a in (ct_tracer, kappa, kvert, land))
    kmt, layer_weight = left(kmt), left(layer_weight)
    semaphores = pltpu.SemaphoreType.DMA

    height, surface, s_fx, s_fn, s_dg, q1, base, to_near, to_far, wet = kernel(
        functools.partial(setup_body, levels), vmem(*[tile] * 9, brick), in_hbm(5), in_vmem(10), "setup",
        [scalars, ints, tile_ints, tiles, semaphores((8,))],
    )(layer_weight, land, kmt, left(ct_surface), left(screen))
    near, far = exchange(to_near, to_far)

    rim_near, rim_far, links = kernel(
        functools.partial(rims_body, levels), vmem(rim, rim) + hbm(link_rows), in_hbm(1) + in_vmem(1),
        in_vmem(2) + in_hbm(1), "rims", [whole, bricks, pltpu.VMEM(link_rows, FLOAT), semaphores((4 + levels // 8,))],
    )(kappa, wet)
    links_left = left(links)
    rim_other_near, rim_other_far = exchange(rim_near, rim_far)

    basis, sums = kernel(
        basis_body, vmem((3 * rows, width), (count, 128)), in_vmem(9) + in_hbm(1),
        in_vmem(2), "basis"
    )(base, height, surface, s_fx, s_fn, s_dg, q1, near, far, links_left)
    sums = lax.all_to_all(sums.reshape(count, 1, 128), "tile", 0, 0, tiled=True).reshape(count, 128)

    rims = (rim_near, rim_far, rim_other_near, rim_other_far)
    half = levels // 2
    halved = lambda shape: (shape[0] // 2, shape[1])
    half_bricks, half_links = halved(brick), halved(link_rows)
    solution, carried, ratio, low, links_high, low_near, low_far = kernel(
        functools.partial(columns_body, levels),
        hbm(tile) + vmem(half_bricks, half_bricks, padded(half_bricks), half_links, halved(rim), halved(rim)),
        in_vmem(2) + in_hbm(6), in_hbm(1) + in_vmem(6), "columns",
        [scalars, tile_ints, whole, whole, ints, pltpu.VMEM(half_links, FLOAT), tiles, pltpu.VMEM(half_bricks, FLOAT),
         semaphores((16,)), semaphores((1,))],
    )(sums, basis, layer_weight, kmt, ct_tracer, kvert, land, links_left)
    low_other_near, low_other_far = exchange(low_near, low_far)
    high, high_near, high_far = kernel(
        upper_body, vmem(padded(half_bricks), halved(rim), halved(rim)), in_vmem(4), in_vmem(3), "upper_columns"
    )(carried, ratio, low, links_high)
    high_other_near, high_other_far = exchange(high_near, high_far)
    u2 = kernel(
        functools.partial(inner_body, levels), vmem(flat), in_vmem(2) + in_hbm(3), in_vmem(1), "inner",
        [tile_ints, whole, ints] + [pltpu.VMEM(padded(brick), FLOAT)] * 3 + [semaphores((9,))],
    )(high, low, kmt, kappa, land)[0]

    scratch = [
        pltpu.VMEM((8 * rows * width // 128, 128), FLOAT), pltpu.VMEM(halved(flat), FLOAT), semaphores((half // 8,))
    ]
    deep = kernel(
        functools.partial(finish_body, levels, half, levels, half // 8), hbm(flat), in_vmem(10), in_hbm(1), "finish_low", scratch,
    )(u2, held(links), low_near, low_far, low_other_near, low_other_far, *rims)[0]
    values = kernel(
        functools.partial(finish_body, levels, 0, half, 0), hbm(flat), in_vmem(10) + in_hbm(1), in_hbm(1), "finish_high",
        scratch, aliases={10: 0},
    )(u2, links_high, high_near, high_far, high_other_near, high_other_far, *rims, left(deep))[0]
    return (values.reshape(levels, rows, width), solution)


def solution(mesh):
    in_specs = (
        P(None, ("grp", "tile"), None),
        P(("grp", "tile"), None),
        P(None, "tile", None),
        P(None, "tile", None),
        P(None, "tile", None),
        P("tile", None),
        P("tile", None),
        P(),
    )
    out_specs = (P(None, ("grp", "tile"), None), P(("grp", "tile"), None))
    return jax.shard_map(body, mesh=mesh, in_specs=in_specs, out_specs=out_specs, check_vma=False)
```

```python
import functools

import jax
import jax.numpy as jnp
from jax import lax
from jax.experimental import pallas as pl
from jax.experimental.pallas import tpu as pltpu
from jax.sharding import PartitionSpec as P

ITERS = 3
ROWS = 8
LOW = 0.05
HIGH = 9.0
MID = 0.5 * (HIGH + LOW)
HALF = 0.5 * (HIGH - LOW)
FLOAT = jnp.float32
LINKS = 4
GROUP = 4
UPPER = 8
LIMIT = 24 * 1024 * 1024


def east(values):
    return pltpu.roll(values, values.shape[1] - 1, 1)


def west(values):
    return pltpu.roll(values, 1, 1)


def north(values):
    return pltpu.roll(values, values.shape[0] - 1, 0)


def south(values):
    return pltpu.roll(values, 1, 0)


def stacked(values):
    return jnp.concatenate([values[:, i : i + 128] for i in range(0, values.shape[1], 128)], axis=0)


def unstacked(values):
    return jnp.concatenate([values[i : i + ROWS, :] for i in range(0, values.shape[0], ROWS)], axis=1)


def row_of(ref, block, row, width):
    tall = width // 128 * ROWS
    return jnp.concatenate(
        [ref[pl.ds(block * 8 * tall + j * ROWS + row, 8, stride=tall), :] for j in range(width // 128)], axis=1
    )


def level_at(k, width):
    tall = width // 128 * ROWS
    return pl.ds(pl.multiple_of(k * tall, tall), tall)


def rows_at(k):
    return pl.ds(pl.multiple_of(k * ROWS, ROWS), ROWS)


def row_index(values):
    return lax.broadcasted_iota(jnp.int32, values.shape, 0)


def spread(row, like):
    return jnp.broadcast_to(row, like.shape)


def vmem(*shapes):
    return [pltpu.VMEM(shape, FLOAT) for shape in shapes]


def hbm(*shapes):
    return [pltpu.HBM(shape, FLOAT) for shape in shapes]


def in_vmem(count):
    return [pl.BlockSpec(memory_space=pltpu.VMEM)] * count


def in_hbm(count):
    return [pl.BlockSpec(memory_space=pltpu.HBM)] * count


def kernel(body, outs, ins, out_specs, name, scratch=(), cost=1, aliases={}):
    return pl.pallas_call(
        body,
        out_shape=outs,
        in_specs=ins,
        out_specs=out_specs,
        scratch_shapes=list(scratch),
        name=name,
        input_output_aliases=aliases,
        cost_estimate=pl.CostEstimate(flops=cost, bytes_accessed=cost, transcendentals=0),
        compiler_params=pltpu.CompilerParams(vmem_limit_bytes=LIMIT),
    )


def held(array):
    return pltpu.with_memory_space_constraint(array, pltpu.VMEM)


def left(array):
    return pltpu.with_memory_space_constraint(array, pltpu.HBM)


def is_even():
    return lax.rem(lax.axis_index("tile"), 2) == 0


def dealt(even, low, high):
    return jnp.where(even, high, low), jnp.where(even, low, high)


def loads(pairs, sems, first=0):
    copies = [pltpu.make_async_copy(far, near, sems.at[first + i]) for i, (far, near) in enumerate(pairs)]
    for copy in copies:
        copy.start()
    return copies


def in_parts(far, near, parts):
    size = far.shape[0] // parts
    return [(far.at[pl.ds(i * size, size)], near.at[pl.ds(i * size, size)]) for i in range(parts)]


def weight_sum(weight, levels):
    total = weight[0]
    for k in range(1, levels):
        total = total + weight[k]
    return total


def setup_body(levels, weight_hbm, land_hbm, kmt_hbm, ct_hbm, screen_hbm, height_ref, surface_ref,
               fx_ref, fn_ref, dg_ref, q1_ref, base_ref, near_ref, far_ref, wet_bricks,
               weight, land, kmt, screen, sems):
    chunk = levels // 4
    small = loads(((weight_hbm, weight), (kmt_hbm, kmt)), sems)
    land_copies = loads(in_parts(land_hbm, land, 4), sems, 2)
    small += loads(((ct_hbm, base_ref), (screen_hbm, screen)), sems, 6)
    small[0].wait()
    total = weight_sum(weight, levels)
    small[1].wait()
    depth = kmt[...]
    width = depth.shape[1]
    height = jnp.zeros(depth.shape, FLOAT)
    for i, copy in enumerate(land_copies):
        copy.wait()

        def level(k, height):
            wet = jnp.where(k < depth, land[rows_at(k), :], 0).astype(FLOAT)
            wet_bricks[level_at(k, width), :] = stacked(wet)
            return height + weight[k] * wet

        height = lax.fori_loop(i * chunk, (i + 1) * chunk, level, height, unroll=4)
    height = height / total
    surface = jnp.where(0 < depth, land[0:ROWS, :], 0).astype(FLOAT)
    height_ref[...] = height
    surface_ref[...] = surface
    small[2].wait()
    small[3].wait()
    base = base_ref[...]
    rows = row_index(base)
    scale = 0.5 / HALF
    fx = scale * (height + east(height)) * surface * east(surface)
    fn = scale * (height + north(height)) * surface * north(surface)
    fn = jnp.where(rows < ROWS - 1, fn, 0.0)
    fs = south(fn)
    fw = west(fx)
    dg = (screen[...] - MID) * (1.0 / HALF) + fx + fw + fn + fs

    def apply(v):
        return dg * v - fx * east(v) - fw * west(v) - fn * north(v) - fs * south(v)

    q1 = apply(base)
    q2 = apply(q1)
    fx_ref[...] = fx
    fn_ref[...] = fn
    dg_ref[...] = dg
    q1_ref[...] = q1
    even = is_even()
    near_ref[7:8, :] = jnp.zeros_like(base[0:1, :])
    far_ref[7:8, :] = jnp.zeros_like(base[0:1, :])
    for place, values in enumerate((base, q1, q2, fx, dg, height, surface)):
        at = slice(place, place + 1)
        near_ref[at, :], far_ref[at, :] = dealt(even, values[0:1, :], values[ROWS - 1 : ROWS, :])


def rims_body(levels, kappa_hbm, wet_bricks, near_ref, far_ref, links_hbm, kappa, kappa_bricks, links, sems):
    chunk = levels // 4
    width = kappa.shape[1]
    for i, copy in enumerate(loads(in_parts(kappa_hbm, kappa, 4), sems)):
        copy.wait()

        def brick(k, carry):
            kappa_bricks[level_at(k, width), :] = stacked(kappa[rows_at(k), :])
            return carry

        lax.fori_loop(i * chunk, (i + 1) * chunk, brick, 0, unroll=4)
    even = is_even()
    outs = []
    for block in range(levels // 8):
        found = []
        for side, row, inner in ((0, 0, 1), (1, ROWS - 1, ROWS - 2)):
            kap, kap_in = row_of(kappa_bricks, block, row, width), row_of(kappa_bricks, block, inner, width)
            here, here_in = row_of(wet_bricks, block, row, width), row_of(wet_bricks, block, inner, width)
            at = (block * LINKS + side * 2) * 8
            links[pl.ds(at, 8), :] = 0.5 * (kap + east(kap)) * here * east(here)
            links[pl.ds(at + 8, 8), :] = 0.5 * (kap + kap_in) * here * here_in
            found.append((kap, here))
        for place in range(2):
            at = pl.ds(place * levels + block * 8, 8)
            near_ref[at, :], far_ref[at, :] = dealt(even, found[0][place], found[1][place])
        whole = pl.ds(block * LINKS * 8, LINKS * 8)
        outs += loads([(links.at[whole], links_hbm.at[whole])], sems, 4 + block)
    for copy in outs:
        copy.wait()


def basis_body(ct, height, surface, fx_ref, fn_ref, dg_ref, q1_ref, near, far, links_hbm, basis_ref, sums_ref):
    even = is_even()
    b0 = ct[...]
    rows = row_index(b0)
    first, last = rows == 0, rows == ROWS - 1
    fx, fn, dg = fx_ref[...], fn_ref[...], dg_ref[...]
    fw, fs = west(fx), south(fn)

    def halo(values, row):
        b0_h, q1_h, q2_h, fx_h, dg_h, high_h, wet_h = (values[i : i + 1, :] for i in range(7))
        face = (0.5 / HALF) * (high_h + height[row : row + 1, :]) * wet_h * surface[row : row + 1, :]
        extra = face * (b0_h - ct[row : row + 1, :])
        return b0_h, q1_h + extra, q2_h, fx_h, dg_h, face, extra

    def lift(row):
        return jnp.broadcast_to(row, b0.shape)

    before, after = dealt(even, near[...], far[...])
    sides = (halo(before, 0), halo(after, ROWS - 1))
    face_b, face_a = lift(sides[0][5]), lift(sides[1][5])
    b1 = q1_ref[...] - jnp.where(first, lift(sides[0][6]), 0.0) - jnp.where(last, lift(sides[1][6]), 0.0)
    dg = dg + jnp.where(first, face_b, 0.0) + jnp.where(last, face_a, 0.0)
    fn = jnp.where(last, face_a, fn)
    fs = jnp.where(first, face_b, fs)

    def apply(v, v_before, v_after):
        v_n = jnp.where(last, lift(v_after), north(v))
        v_s = jnp.where(first, lift(v_before), south(v))
        return dg * v - fx * east(v) - fw * west(v) - fn * v_n - fs * v_s

    b2 = 2.0 * apply(b1, sides[0][1], sides[1][1]) - b0

    def outer(side, own):
        b0_h, b1_h, q2_h, fx_h, dg_h, face, extra = side
        b0_h, b1_h, q2_h, fx_h, dg_h, face, extra, own = (lift(v) for v in (b0_h, b1_h, q2_h, fx_h, dg_h, face, extra, own))
        turned = dg_h * extra - fx_h * east(extra) - west(fx_h) * west(extra)
        return (2.0 * (q2_h + turned + face * (b1_h - own)) - b0_h)[0:1, :]

    for place, values in enumerate((b0, b1, b2)):
        basis_ref[pl.ds(place * ROWS, ROWS), :] = values
    b2_b = outer(sides[0], b1[0:1, :])
    b2_a = outer(sides[1], b1[ROWS - 1 : ROWS, :])
    next2 = apply(b2, b2_b, b2_a)
    lanes = lax.broadcasted_iota(jnp.int32, (1, 128), 1)
    packed = jnp.zeros((1, 128), FLOAT)
    for place, (p, q) in enumerate(((b0, b0), (b0, b1), (b1, b1), (b1, b2), (b2, b2), (b2, next2))):
        product = p * q
        folded = product[:, 0:128]
        for j in range(1, product.shape[1] // 128):
            folded = folded + product[:, j * 128 : (j + 1) * 128]
        total = jnp.sum(jnp.sum(folded, axis=0, keepdims=True), axis=1, keepdims=True)
        packed = jnp.where(lanes == place, total, packed)
    sums_ref[...] = jnp.broadcast_to(packed, sums_ref.shape)


def quadratic(left, form):
    total = None
    for i in range(3):
        for j in range(3):
            if left[i] is not None and left[j] is not None:
                term = left[i] * left[j] * form[i][j]
                total = term if total is None else total + term
    return total


def plus(p, q):
    return q if p is None else p if q is None else p + q


def times(scale, p):
    return None if p is None else scale * p


def weights(sums):
    s0, s1, s2, s3, s4, s5 = sums
    g02 = 2.0 * s2 - s0
    gram = ((s0, s1, g02), (s1, s2, s3), (g02, s3, s4))
    b11, b12 = 0.5 * (s3 + s1), 0.5 * (s4 + g02)
    shift = ((s1, s2, s3), (s2, b11, b12), (s3, b12, s5))
    form = [[MID * gram[i][j] + HALF * shift[i][j] for j in range(3)] for i in range(3)]
    one = jnp.ones_like(s0)
    x, r, d = [None] * 3, [one, None, None], [one, None, None]
    rr = s0
    for step in range(ITERS):
        alpha = jnp.clip(rr / quadratic(d, form), 1.0 / HIGH, 1.0 / LOW)
        x = [plus(x[i], times(alpha, d[i])) for i in range(3)]
        if step + 1 < ITERS:
            image = [
                plus(times(MID, d[0]), times(0.5 * HALF, d[1])),
                plus(plus(times(MID, d[1]), times(HALF, d[0])), times(0.5 * HALF, d[2])),
                plus(times(MID, d[2]), times(0.5 * HALF, d[1])),
            ]
            r = [plus(r[i], times(-1.0, times(alpha, image[i]))) for i in range(3)]
            new = quadratic(r, gram)
            beta = jnp.clip(new / rr, 0.0, HIGH / LOW)
            d = [plus(r[i], times(beta, d[i])) for i in range(3)]
            rr = new
    return x


def inverse_of(values):
    guess = pl.reciprocal(values, approx=True)
    guess = guess * (2.0 - values * guess)
    return guess * (2.0 - values * guess)


def send_rows(u, links, near_ref, far_ref, width):
    even = is_even()
    levels = near_ref.shape[0] // 2
    for block in range(levels // 8):
        found = []
        for side, row, inner in ((0, 0, 1), (1, ROWS - 1, ROWS - 2)):
            value, value_in = row_of(u, block, row, width), row_of(u, block, inner, width)
            face, link = (links[pl.ds((block * LINKS + side * 2 + i) * 8, 8), :] for i in range(2))
            flux = face * (east(value) - value)
            found.append((value, value + (flux - west(flux)) + link * (value_in - value)))
        for place in range(2):
            at = pl.ds(place * levels + block * 8, 8)
            near_ref[at, :], far_ref[at, :] = dealt(even, found[0][place], found[1][place])


def segments(start, stop):
    cuts = [start] + ([UPPER] if start < UPPER < stop else []) + [stop]
    return [(a, b, b <= UPPER) for a, b in zip(cuts[:-1], cuts[1:])]


def columns_body(levels, sums, sums_near, basis_ref, weight_hbm, kmt_hbm, source_hbm, kvert_hbm, land_hbm, links_hbm,
                 out_hbm, high, ratio, low, links_high, near_ref, far_ref,
                 weight, kmt, source, kvert, land, links_low, s_ref, ratio_low, sems, out_sems):
    width = source.shape[1]
    parts = 4
    chunk = levels // parts
    small = loads(((weight_hbm, weight), (kmt_hbm, kmt)), sems)
    parted = [in_parts(far, near, parts) for far, near in ((land_hbm, land), (kvert_hbm, kvert), (source_hbm, source))]
    big = loads([pairs[i] for i in range(parts) for pairs in parted], sems, 2)
    top, bottom = pl.ds(0, UPPER * LINKS), pl.ds(UPPER * LINKS, (levels - UPPER) * LINKS)
    links_copies = loads([(links_hbm.at[bottom], links_low), (links_hbm.at[top], links_high)], sems, 2 + 3 * parts)

    total = jnp.sum(sums[...], axis=0, keepdims=True) + jnp.sum(sums_near[...], axis=0, keepdims=True)
    mix = weights([total[:, i : i + 1] for i in range(6)])
    b0, b1, b2 = (basis_ref[i * ROWS : (i + 1) * ROWS, :] for i in range(3))
    s = mix[0] * b0 + mix[1] * b1 + mix[2] * b2
    s_ref[...] = s
    outs = loads([(s_ref, out_hbm)], out_sems)

    small[0].wait()
    scaled = stacked(s) / jnp.full((ROWS * width // 128, 128), weight_sum(weight, levels), FLOAT)
    small[1].wait()
    depth = stacked(kmt[...])

    def sea(k):
        return jnp.where(k < depth, stacked(land[rows_at(k), :]), 0).astype(FLOAT)

    def down(values, parts_of, first, k, carry):
        here, link, passed = carry
        at = level_at(k - first, width)
        below = jnp.where(k + 1 < levels, sea(jnp.minimum(k + 1, levels - 1)), 0.0)
        coupling = stacked(kvert[rows_at(k), :]) * here * below
        over = inverse_of(1.0 + coupling + link)
        value = (stacked(source[rows_at(k), :]) + here * (weight[k] * scaled) + passed) * over
        part = coupling * over
        parts_of[at, :] = part
        values[at, :] = value
        return below, coupling - coupling * part, coupling * value

    zero = jnp.zeros(scaled.shape, FLOAT)
    big[0].wait()
    carry = (sea(0), zero, zero)
    for i in range(parts):
        big[3 * i + 1].wait()
        big[3 * i + 2].wait()
        if i + 1 < parts:
            big[3 * i + 3].wait()
        for start, stop, is_high in segments(i * chunk, (i + 1) * chunk):
            target = (high, ratio, 0) if is_high else (low, ratio_low, UPPER)
            carry = lax.fori_loop(start, stop, functools.partial(down, *target), carry, unroll=4)
    ascend(low, low, ratio_low, zero, width)
    for copy in links_copies:
        copy.wait()
    send_rows(low, links_low, near_ref, far_ref, width)
    for copy in outs:
        copy.wait()


def ascend(target, source, ratio, below, width):
    levels = target.shape[0] * 128 // (ROWS * width)

    def up(i, below):
        at = level_at(levels - 1 - i, width)
        value = source[at, :] + ratio[at, :] * below
        target[at, :] = value
        return value

    lax.fori_loop(0, levels, up, below, unroll=4)


def upper_body(high, ratio, low, links, u, near_ref, far_ref):
    width = near_ref.shape[1]
    ascend(u, high, ratio, low[level_at(0, width), :], width)
    send_rows(u, links, near_ref, far_ref, width)


def inner_body(levels, high, low, kmt_hbm, kappa_hbm, land_hbm, u2_ref, kmt, kappa, land, sems):
    parts = 4
    kmt_copy = loads([(kmt_hbm, kmt)], sems)[0]
    pairs = ((kappa_hbm, kappa), (land_hbm, land))
    parted = [in_parts(far, near, parts) for far, near in pairs]
    copies = loads([pairs[i] for i in range(parts) for pairs in parted], sems, 1)
    kmt_copy.wait()
    depth = kmt[...]
    width = depth.shape[1]
    inside = row_index(depth) < ROWS - 1

    def face(here, there):
        return jnp.where(jnp.minimum(here, there) > 0.0, here + there, 0.0)

    def group(source, first, i, carry):
        ks = [GROUP * i + j for j in range(GROUP)]
        sea = [jnp.where(k < depth, land[rows_at(k), :], 0) > 0 for k in ks]
        halved = [jnp.where(wet, 0.5 * kappa[rows_at(k), :], 0.0) for wet, k in zip(sea, ks)]
        u = [unstacked(source[level_at(k - first, width), :]) for k in ks]
        fx = [face(v, east(v)) for v in halved]
        fn = [jnp.where(inside, face(v, north(v)), 0.0) for v in halved]
        for _ in range(2):
            flux_x = [f * (east(v) - v) for f, v in zip(fx, u)]
            flux_y = [f * (north(v) - v) for f, v in zip(fn, u)]
            u = [v + (x - west(x)) + (y - south(y)) for v, x, y in zip(u, flux_x, flux_y)]
        for k, v in zip(ks, u):
            u2_ref[rows_at(k), :] = v
        return carry

    chunk = levels // parts
    for i in range(parts):
        for copy in copies[2 * i : 2 * i + 2]:
            copy.wait()
        for start, stop, is_high in segments(i * chunk, (i + 1) * chunk):
            step = functools.partial(group, *((high, 0) if is_high else (low, UPPER)))
            lax.fori_loop(start // GROUP, stop // GROUP, step, 0)


def finish_body(levels, first, last, skipped, u2, links, own_near, own_far, near, far, rim_near, rim_far, rim_other_near, rim_other_far,
                *refs):
    out, change_ref, buffer, sems = refs[-4:]
    width = own_near.shape[1]
    tall = width // 128 * ROWS
    count = last - first
    rows = lax.broadcasted_iota(jnp.int32, (ROWS, width), 0)
    on_rim = (rows < 2) | (rows >= ROWS - 2)
    even = is_even()
    copies = []
    for block in range(count // 8):
        at, below = pl.ds(block * 8, 8), pl.ds(count + block * 8, 8)

        def pairs(a, b):
            return [dealt(even, a[part, :], b[part, :]) for part in (at, below)]

        own, other = pairs(own_near, own_far), pairs(near, far)
        kap, wet, kap_other, wet_other = (
            dealt(even, a[pl.ds(part * levels + first + block * 8, 8), :], b[pl.ds(part * levels + first + block * 8, 8), :])
            for a, b in ((rim_near, rim_far), (rim_other_near, rim_other_far)) for part in range(2)
        )
        for side, row, inner in ((0, 0, 1), (1, ROWS - 1, ROWS - 2)):
            face = 0.5 * (kap[side] + kap_other[side]) * wet[side] * wet_other[side]
            change = face * (other[0][side] - own[0][side])
            along, link = (
                links[pl.ds(((skipped + block) * LINKS + side * 2 + i) * 8, 8), :] for i in range(2)
            )
            flux = along * (east(change) - change)
            passed = link * change
            on_row = (change + (flux - west(flux)) - passed
                      + face * (other[1][side] - own[1][side] - 2.0 * change))
            for j in range(width // 128):
                lanes = slice(j * 128, (j + 1) * 128)
                change_ref[pl.ds(j * ROWS + row, 8, stride=tall), :] = on_row[:, lanes]
                change_ref[pl.ds(j * ROWS + inner, 8, stride=tall), :] = passed[:, lanes]
        for k in range(8):
            here = block * 8 + k
            change = jnp.where(on_rim, unstacked(change_ref[level_at(k, width), :]), 0.0)
            buffer[rows_at(here), :] = u2[rows_at(first + here), :] + change
        whole = pl.ds(block * 8 * ROWS, 8 * ROWS)
        target = pl.ds((first + block * 8) * ROWS, 8 * ROWS)
        copies += loads([(buffer.at[whole], out.at[target])], sems, block)
    for copy in copies:
        copy.wait()


def swap(array, start):
    firsts = range(start, lax.axis_size("tile") - 1, 2)
    return lax.ppermute(array, "tile", [(i, i + 1) for i in firsts] + [(i + 1, i) for i in firsts])


def exchange(to_near, to_far):
    from_far = swap(to_far, 1)
    return swap(to_near, 0), from_far


def body(ct_tracer, ct_surface, kappa, kvert, land, kmt, screen, layer_weight):
    levels, rows, width = ct_tracer.shape
    count = lax.axis_size("tile")
    tall = levels * rows
    tile, brick, flat = (rows, width), (tall * width // 128, 128), (tall, width)
    rim, link_rows = (2 * levels, width), (levels * LINKS, width)
    scalars, whole = pltpu.SMEM((levels,), FLOAT), pltpu.VMEM(flat, FLOAT)
    ints, tile_ints = pltpu.VMEM(flat, jnp.int32), pltpu.VMEM(tile, jnp.int32)
    bricks, tiles = pltpu.VMEM(brick, FLOAT), pltpu.VMEM(tile, FLOAT)
    ct_tracer, kappa, kvert, land = (left(a.reshape(flat)) for a in (ct_tracer, kappa, kvert, land))
    kmt, layer_weight = left(kmt), left(layer_weight)
    semaphores = pltpu.SemaphoreType.DMA

    height, surface, s_fx, s_fn, s_dg, q1, base, to_near, to_far, wet = kernel(
        functools.partial(setup_body, levels), vmem(*[tile] * 9, brick), in_hbm(5), in_vmem(10), "setup",
        [scalars, ints, tile_ints, tiles, semaphores((8,))],
    )(layer_weight, land, kmt, left(ct_surface), left(screen))
    near, far = exchange(to_near, to_far)

    rim_near, rim_far, links = kernel(
        functools.partial(rims_body, levels), vmem(rim, rim) + hbm(link_rows), in_hbm(1) + in_vmem(1),
        in_vmem(2) + in_hbm(1), "rims", [whole, bricks, pltpu.VMEM(link_rows, FLOAT), semaphores((4 + levels // 8,))],
    )(kappa, wet)
    links_left = left(links)
    rim_other_near, rim_other_far = exchange(rim_near, rim_far)

    basis, sums = kernel(
        basis_body, vmem((3 * rows, width), (count // 2, 128)), in_vmem(9) + in_hbm(1),
        in_vmem(2), "basis"
    )(base, height, surface, s_fx, s_fn, s_dg, q1, near, far, links_left)
    share = count // 2
    every_other = [[2 * i + core for i in range(share)] for core in range(2)]
    sums = lax.all_to_all(sums.reshape(share, 1, 128), "tile", 0, 0, axis_index_groups=every_other, tiled=True)
    sums = sums.reshape(share, 128)
    sums_near = swap(sums, 0)

    rims = (rim_near, rim_far, rim_other_near, rim_other_far)
    lower = levels - UPPER
    per_level = brick[0] // levels
    high_bricks, low_bricks = (UPPER * per_level, 128), (lower * per_level, 128)
    high_links, low_links = (UPPER * LINKS, width), (lower * LINKS, width)
    high_rim, low_rim = (2 * UPPER, width), (2 * lower, width)
    solution, carried, ratio, low, links_high, low_near, low_far = kernel(
        functools.partial(columns_body, levels),
        hbm(tile) + vmem(high_bricks, high_bricks, low_bricks, high_links, low_rim, low_rim),
        in_vmem(3) + in_hbm(6), in_hbm(1) + in_vmem(6), "columns",
        [scalars, tile_ints, whole, whole, ints, pltpu.VMEM(low_links, FLOAT), tiles, pltpu.VMEM(low_bricks, FLOAT),
         semaphores((16,)), semaphores((1,))],
    )(sums, sums_near, basis, layer_weight, kmt, ct_tracer, kvert, land, links_left)
    low_other_near, low_other_far = exchange(low_near, low_far)
    high, high_near, high_far = kernel(
        upper_body, vmem(high_bricks, high_rim, high_rim), in_vmem(4), in_vmem(3), "upper_columns"
    )(carried, ratio, low, links_high)
    high_other_near, high_other_far = exchange(high_near, high_far)
    u2 = kernel(
        functools.partial(inner_body, levels), vmem(flat), in_vmem(2) + in_hbm(3), in_vmem(1), "inner",
        [tile_ints, whole, ints, semaphores((9,))],
    )(high, low, kmt, kappa, land)[0]

    def finish(first, last, skipped, name, more=(), aliases={}):
        count = last - first
        return kernel(
            functools.partial(finish_body, levels, first, last, skipped), hbm(flat), in_vmem(10) + in_hbm(len(more)),
            in_hbm(1), name,
            [pltpu.VMEM((8 * per_level, 128), FLOAT), pltpu.VMEM((count * rows, width), FLOAT), semaphores((count // 8,))],
            aliases=aliases,
        )

    deep = finish(UPPER, levels, UPPER // 8, "finish_low")(
        u2, held(links), low_near, low_far, low_other_near, low_other_far, *rims
    )[0]
    values = finish(0, UPPER, 0, "finish_high", (deep,), {10: 0})(
        u2, links_high, high_near, high_far, high_other_near, high_other_far, *rims, left(deep)
    )[0]
    return (values.reshape(levels, rows, width), solution)


def solution(mesh):
    in_specs = (
        P(None, ("grp", "tile"), None),
        P(("grp", "tile"), None),
        P(None, "tile", None),
        P(None, "tile", None),
        P(None, "tile", None),
        P("tile", None),
        P("tile", None),
        P(),
    )
    out_specs = (P(None, ("grp", "tile"), None), P(("grp", "tile"), None))
    return jax.shard_map(body, mesh=mesh, in_specs=in_specs, out_specs=out_specs, check_vma=False)
```

```python
import functools

import jax
import jax.numpy as jnp
from jax import lax
from jax.experimental import pallas as pl
from jax.experimental.pallas import tpu as pltpu
from jax.sharding import PartitionSpec as P

ITERS = 3
ROWS = 8
LOW = 0.05
HIGH = 9.0
MID = 0.5 * (HIGH + LOW)
HALF = 0.5 * (HIGH - LOW)
FLOAT = jnp.float32
LINKS = 4
GROUP = 4
PART = 8
BEFORE_SWAP = 16
LIMIT = 24 * 1024 * 1024


def east(values):
    return pltpu.roll(values, values.shape[1] - 1, 1)


def west(values):
    return pltpu.roll(values, 1, 1)


def north(values):
    return pltpu.roll(values, values.shape[0] - 1, 0)


def south(values):
    return pltpu.roll(values, 1, 0)


def stacked(values):
    return jnp.concatenate([values[:, i : i + 128] for i in range(0, values.shape[1], 128)], axis=0)


def unstacked(values):
    return jnp.concatenate([values[i : i + ROWS, :] for i in range(0, values.shape[0], ROWS)], axis=1)


def row_of(ref, block, row, width):
    tall = width // 128 * ROWS
    return jnp.concatenate(
        [ref[pl.ds(block * 8 * tall + j * ROWS + row, 8, stride=tall), :] for j in range(width // 128)], axis=1
    )


def level_at(k, width):
    tall = width // 128 * ROWS
    return pl.ds(pl.multiple_of(k * tall, tall), tall)


def rows_at(k):
    return pl.ds(pl.multiple_of(k * ROWS, ROWS), ROWS)


def row_index(values):
    return lax.broadcasted_iota(jnp.int32, values.shape, 0)


def spread(row, like):
    return jnp.broadcast_to(row, like.shape)


def vmem(*shapes):
    return [pltpu.VMEM(shape, FLOAT) for shape in shapes]


def hbm(*shapes):
    return [pltpu.HBM(shape, FLOAT) for shape in shapes]


def in_vmem(count):
    return [pl.BlockSpec(memory_space=pltpu.VMEM)] * count


def in_hbm(count):
    return [pl.BlockSpec(memory_space=pltpu.HBM)] * count


def kernel(body, outs, ins, out_specs, name, scratch=(), cost=1):
    return pl.pallas_call(
        body,
        out_shape=outs,
        in_specs=ins,
        out_specs=out_specs,
        scratch_shapes=list(scratch),
        name=name,
        cost_estimate=pl.CostEstimate(flops=cost, bytes_accessed=cost, transcendentals=0),
        compiler_params=pltpu.CompilerParams(vmem_limit_bytes=LIMIT),
    )


def held(array):
    return pltpu.with_memory_space_constraint(array, pltpu.VMEM)


def left(array):
    return pltpu.with_memory_space_constraint(array, pltpu.HBM)


def is_even():
    return lax.rem(lax.axis_index("tile"), 2) == 0


def is_first():
    return lax.rem(lax.axis_index("grp"), 2) == 0


def dealt(even, low, high):
    return jnp.where(even, high, low), jnp.where(even, low, high)


def loads(pairs, sems, first=0):
    copies = [pltpu.make_async_copy(far, near, sems.at[first + i]) for i, (far, near) in enumerate(pairs)]
    for copy in copies:
        copy.start()
    return copies


def in_parts(far, near, parts):
    size = far.shape[0] // parts
    return [(far.at[pl.ds(i * size, size)], near.at[pl.ds(i * size, size)]) for i in range(parts)]


def weight_sum(weight, levels):
    total = weight[0]
    for k in range(1, levels):
        total = total + weight[k]
    return total


def setup_body(levels, weight_hbm, land_hbm, kmt_hbm, ct_hbm, screen_hbm, height_ref, surface_ref,
               fx_ref, fn_ref, dg_ref, q1_ref, base_ref, near_ref, far_ref, wet_bricks,
               weight, land, kmt, screen, sems):
    chunk = levels // 4
    small = loads(((weight_hbm, weight), (kmt_hbm, kmt)), sems)
    land_copies = loads(in_parts(land_hbm, land, 4), sems, 2)
    small += loads(((ct_hbm, base_ref), (screen_hbm, screen)), sems, 6)
    small[0].wait()
    total = weight_sum(weight, levels)
    small[1].wait()
    depth = kmt[...]
    width = depth.shape[1]
    height = jnp.zeros(depth.shape, FLOAT)
    for i, copy in enumerate(land_copies):
        copy.wait()

        def level(k, height):
            wet = jnp.where(k < depth, land[rows_at(k), :], 0).astype(FLOAT)
            wet_bricks[level_at(k, width), :] = stacked(wet)
            return height + weight[k] * wet

        height = lax.fori_loop(i * chunk, (i + 1) * chunk, level, height, unroll=4)
    height = height / total
    surface = jnp.where(0 < depth, land[0:ROWS, :], 0).astype(FLOAT)
    height_ref[...] = height
    surface_ref[...] = surface
    small[2].wait()
    small[3].wait()
    base = base_ref[...]
    rows = row_index(base)
    scale = 0.5 / HALF
    fx = scale * (height + east(height)) * surface * east(surface)
    fn = scale * (height + north(height)) * surface * north(surface)
    fn = jnp.where(rows < ROWS - 1, fn, 0.0)
    fs = south(fn)
    fw = west(fx)
    dg = (screen[...] - MID) * (1.0 / HALF) + fx + fw + fn + fs

    def apply(v):
        return dg * v - fx * east(v) - fw * west(v) - fn * north(v) - fs * south(v)

    q1 = apply(base)
    q2 = apply(q1)
    fx_ref[...] = fx
    fn_ref[...] = fn
    dg_ref[...] = dg
    q1_ref[...] = q1
    even = is_even()
    near_ref[7:8, :] = jnp.zeros_like(base[0:1, :])
    far_ref[7:8, :] = jnp.zeros_like(base[0:1, :])
    for place, values in enumerate((base, q1, q2, fx, dg, height, surface)):
        at = slice(place, place + 1)
        near_ref[at, :], far_ref[at, :] = dealt(even, values[0:1, :], values[ROWS - 1 : ROWS, :])


def rims_body(levels, kappa_hbm, wet_bricks, near_ref, far_ref, sent_ref, links_hbm, kappa, kappa_bricks, links, sems):
    chunk = levels // 4
    width = kappa.shape[1]
    for i, copy in enumerate(loads(in_parts(kappa_hbm, kappa, 4), sems)):
        copy.wait()

        def brick(k, carry):
            kappa_bricks[level_at(k, width), :] = stacked(kappa[rows_at(k), :])
            return carry

        lax.fori_loop(i * chunk, (i + 1) * chunk, brick, 0, unroll=4)
    even = is_even()
    first_group = is_first()
    outs = []
    for block in range(levels // 8):
        found = []
        for side, row, inner in ((0, 0, 1), (1, ROWS - 1, ROWS - 2)):
            kap, kap_in = row_of(kappa_bricks, block, row, width), row_of(kappa_bricks, block, inner, width)
            here, here_in = row_of(wet_bricks, block, row, width), row_of(wet_bricks, block, inner, width)
            at = (block * LINKS + side * 2) * 8
            links[pl.ds(at, 8), :] = 0.5 * (kap + east(kap)) * here * east(here)
            links[pl.ds(at + 8, 8), :] = 0.5 * (kap + kap_in) * here * here_in
            found.append((kap, here))
        for place in range(2):
            at = pl.ds(place * levels + block * 8, 8)
            near_ref[at, :], far_ref[at, :] = dealt(even, found[0][place], found[1][place])
        at, below = pl.ds(block * 8, 8), pl.ds(levels + block * 8, 8)
        sent_ref[at, :] = jnp.where(first_group, far_ref[at, :], far_ref[below, :])
        whole = pl.ds(block * LINKS * 8, LINKS * 8)
        outs += loads([(links.at[whole], links_hbm.at[whole])], sems, 4 + block)
    for copy in outs:
        copy.wait()


def basis_body(ct, height, surface, fx_ref, fn_ref, dg_ref, q1_ref, near, far, links_hbm, basis_ref, sums_ref):
    even = is_even()
    b0 = ct[...]
    rows = row_index(b0)
    first, last = rows == 0, rows == ROWS - 1
    fx, fn, dg = fx_ref[...], fn_ref[...], dg_ref[...]
    fw, fs = west(fx), south(fn)

    def halo(values, row):
        b0_h, q1_h, q2_h, fx_h, dg_h, high_h, wet_h = (values[i : i + 1, :] for i in range(7))
        face = (0.5 / HALF) * (high_h + height[row : row + 1, :]) * wet_h * surface[row : row + 1, :]
        extra = face * (b0_h - ct[row : row + 1, :])
        return b0_h, q1_h + extra, q2_h, fx_h, dg_h, face, extra

    def lift(row):
        return jnp.broadcast_to(row, b0.shape)

    before, after = dealt(even, near[...], far[...])
    sides = (halo(before, 0), halo(after, ROWS - 1))
    face_b, face_a = lift(sides[0][5]), lift(sides[1][5])
    b1 = q1_ref[...] - jnp.where(first, lift(sides[0][6]), 0.0) - jnp.where(last, lift(sides[1][6]), 0.0)
    dg = dg + jnp.where(first, face_b, 0.0) + jnp.where(last, face_a, 0.0)
    fn = jnp.where(last, face_a, fn)
    fs = jnp.where(first, face_b, fs)

    def apply(v, v_before, v_after):
        v_n = jnp.where(last, lift(v_after), north(v))
        v_s = jnp.where(first, lift(v_before), south(v))
        return dg * v - fx * east(v) - fw * west(v) - fn * v_n - fs * v_s

    b2 = 2.0 * apply(b1, sides[0][1], sides[1][1]) - b0

    def outer(side, own):
        b0_h, b1_h, q2_h, fx_h, dg_h, face, extra = side
        b0_h, b1_h, q2_h, fx_h, dg_h, face, extra, own = (lift(v) for v in (b0_h, b1_h, q2_h, fx_h, dg_h, face, extra, own))
        turned = dg_h * extra - fx_h * east(extra) - west(fx_h) * west(extra)
        return (2.0 * (q2_h + turned + face * (b1_h - own)) - b0_h)[0:1, :]

    for place, values in enumerate((b0, b1, b2)):
        basis_ref[pl.ds(place * ROWS, ROWS), :] = values
    b2_b = outer(sides[0], b1[0:1, :])
    b2_a = outer(sides[1], b1[ROWS - 1 : ROWS, :])
    next2 = apply(b2, b2_b, b2_a)
    lanes = lax.broadcasted_iota(jnp.int32, (1, 128), 1)
    packed = jnp.zeros((1, 128), FLOAT)
    for place, (p, q) in enumerate(((b0, b0), (b0, b1), (b1, b1), (b1, b2), (b2, b2), (b2, next2))):
        product = p * q
        folded = product[:, 0:128]
        for j in range(1, product.shape[1] // 128):
            folded = folded + product[:, j * 128 : (j + 1) * 128]
        total = jnp.sum(jnp.sum(folded, axis=0, keepdims=True), axis=1, keepdims=True)
        packed = jnp.where(lanes == place, total, packed)
    sums_ref[...] = jnp.broadcast_to(packed, sums_ref.shape)


def quadratic(left, form):
    total = None
    for i in range(3):
        for j in range(3):
            if left[i] is not None and left[j] is not None:
                term = left[i] * left[j] * form[i][j]
                total = term if total is None else total + term
    return total


def plus(p, q):
    return q if p is None else p if q is None else p + q


def times(scale, p):
    return None if p is None else scale * p


def weights(sums):
    s0, s1, s2, s3, s4, s5 = sums
    g02 = 2.0 * s2 - s0
    gram = ((s0, s1, g02), (s1, s2, s3), (g02, s3, s4))
    b11, b12 = 0.5 * (s3 + s1), 0.5 * (s4 + g02)
    shift = ((s1, s2, s3), (s2, b11, b12), (s3, b12, s5))
    form = [[MID * gram[i][j] + HALF * shift[i][j] for j in range(3)] for i in range(3)]
    one = jnp.ones_like(s0)
    x, r, d = [None] * 3, [one, None, None], [one, None, None]
    rr = s0
    for step in range(ITERS):
        alpha = jnp.clip(rr / quadratic(d, form), 1.0 / HIGH, 1.0 / LOW)
        x = [plus(x[i], times(alpha, d[i])) for i in range(3)]
        if step + 1 < ITERS:
            image = [
                plus(times(MID, d[0]), times(0.5 * HALF, d[1])),
                plus(plus(times(MID, d[1]), times(HALF, d[0])), times(0.5 * HALF, d[2])),
                plus(times(MID, d[2]), times(0.5 * HALF, d[1])),
            ]
            r = [plus(r[i], times(-1.0, times(alpha, image[i]))) for i in range(3)]
            new = quadratic(r, gram)
            beta = jnp.clip(new / rr, 0.0, HIGH / LOW)
            d = [plus(r[i], times(beta, d[i])) for i in range(3)]
            rr = new
    return x


def inverse_of(values):
    guess = pl.reciprocal(values, approx=True)
    guess = guess * (2.0 - values * guess)
    return guess * (2.0 - values * guess)


def columns_body(levels, sums, basis_ref, weight_hbm, kmt_hbm, source_hbm, kvert_hbm, land_hbm, links_hbm,
                 out_hbm, u, near_ref, far_ref, weight, kmt, source, kvert, land, links, s_ref, ratio, sems, out_sems):
    width = source.shape[1]
    parts = 4
    chunk = levels // parts
    small = loads(((weight_hbm, weight), (kmt_hbm, kmt)), sems)
    parted = [in_parts(far, near, parts) for far, near in ((land_hbm, land), (kvert_hbm, kvert), (source_hbm, source))]
    big = loads([pairs[i] for i in range(parts) for pairs in parted], sems, 2)
    links_copy = loads([(links_hbm, links)], sems, 2 + 3 * parts)[0]

    total = jnp.sum(sums[...], axis=0, keepdims=True)
    mix = weights([total[:, i : i + 1] for i in range(6)])
    b0, b1, b2 = (basis_ref[i * ROWS : (i + 1) * ROWS, :] for i in range(3))
    s = mix[0] * b0 + mix[1] * b1 + mix[2] * b2
    s_ref[...] = s
    outs = loads([(s_ref, out_hbm)], out_sems)

    small[0].wait()
    scaled = stacked(s) / jnp.full((ROWS * width // 128, 128), weight_sum(weight, levels), FLOAT)
    small[1].wait()
    depth = stacked(kmt[...])

    def sea(k):
        return jnp.where(k < depth, stacked(land[rows_at(k), :]), 0).astype(FLOAT)

    def down(k, carry):
        here, link, passed = carry
        at = level_at(k, width)
        below = jnp.where(k + 1 < levels, sea(jnp.minimum(k + 1, levels - 1)), 0.0)
        coupling = stacked(kvert[rows_at(k), :]) * here * below
        over = inverse_of(1.0 + coupling + link)
        value = (stacked(source[rows_at(k), :]) + here * (weight[k] * scaled) + passed) * over
        part = coupling * over
        ratio[at, :] = part
        u[at, :] = value
        return below, coupling - coupling * part, coupling * value

    zero = jnp.zeros(scaled.shape, FLOAT)
    big[0].wait()
    carry = (sea(0), zero, zero)
    for i in range(parts):
        big[3 * i + 1].wait()
        big[3 * i + 2].wait()
        if i + 1 < parts:
            big[3 * i + 3].wait()
        carry = lax.fori_loop(i * chunk, (i + 1) * chunk, down, carry, unroll=4)

    def up(i, below):
        at = level_at(levels - 1 - i, width)
        value = u[at, :] + ratio[at, :] * below
        u[at, :] = value
        return value

    lax.fori_loop(0, levels, up, zero, unroll=4)
    links_copy.wait()
    even = is_even()
    for block in range(levels // 8):
        found = []
        for side, row, inner in ((0, 0, 1), (1, ROWS - 1, ROWS - 2)):
            value, value_in = row_of(u, block, row, width), row_of(u, block, inner, width)
            face, link = (links[pl.ds((block * LINKS + side * 2 + i) * 8, 8), :] for i in range(2))
            flux = face * (east(value) - value)
            found.append((value, value + (flux - west(flux)) + link * (value_in - value)))
        for place in range(2):
            at = pl.ds(place * levels + block * 8, 8)
            near_ref[at, :], far_ref[at, :] = dealt(even, found[0][place], found[1][place])
    for copy in outs:
        copy.wait()


def inner_body(first, last, with_relay, u0, kmt_hbm, kappa_hbm, land_hbm, *refs):
    if with_relay:
        passed, u2_ref, relay_ref = refs[:3]
        relay_ref[...] = passed[...]
        refs = refs[3:]
    else:
        u2_ref, refs = refs[0], refs[1:]
    kmt, kappa, land, sems = refs
    size = PART * ROWS
    parts = (last - first) // PART
    kmt_copy = loads([(kmt_hbm, kmt)], sems)[0]
    pairs = []
    for i in range(parts):
        source, target = pl.ds((first + i * PART) * ROWS, size), pl.ds(i * size, size)
        pairs += [(kappa_hbm.at[source], kappa.at[target]), (land_hbm.at[source], land.at[target])]
    copies = loads(pairs, sems, 1)
    kmt_copy.wait()
    depth = kmt[...]
    width = depth.shape[1]
    inside = row_index(depth) < ROWS - 1

    def face(here, there):
        return jnp.where(jnp.minimum(here, there) > 0.0, here + there, 0.0)

    def group(i, carry):
        ks = [GROUP * i + j for j in range(GROUP)]
        sea = [jnp.where(k + first < depth, land[rows_at(k), :], 0) > 0 for k in ks]
        halved = [jnp.where(wet, 0.5 * kappa[rows_at(k), :], 0.0) for wet, k in zip(sea, ks)]
        u = [unstacked(u0[level_at(k + first, width), :]) for k in ks]
        fx = [face(v, east(v)) for v in halved]
        fn = [jnp.where(inside, face(v, north(v)), 0.0) for v in halved]
        for _ in range(2):
            flux_x = [f * (east(v) - v) for f, v in zip(fx, u)]
            flux_y = [f * (north(v) - v) for f, v in zip(fn, u)]
            u = [v + (x - west(x)) + (y - south(y)) for v, x, y in zip(u, flux_x, flux_y)]
        for k, v in zip(ks, u):
            u2_ref[rows_at(k), :] = v
        return carry

    for i in range(parts):
        copies[2 * i].wait()
        copies[2 * i + 1].wait()
        lax.fori_loop(i * PART // GROUP, (i + 1) * PART // GROUP, group, 0)


def finish_body(levels, u2_high, u2_low, links, own_near, own_far, rim_near, rim_far, near, far, rim_other_near, kept, swapped,
                out, change_ref, buffer, sems):
    width = own_near.shape[1]
    tall = width // 128 * ROWS
    rows = lax.broadcasted_iota(jnp.int32, (ROWS, width), 0)
    on_rim = (rows < 2) | (rows >= ROWS - 2)
    even = is_even()
    first_group = is_first()
    copies = []
    for block in range(levels // 8):
        at, below = pl.ds(block * 8, 8), pl.ds(levels + block * 8, 8)

        def pairs(a, b):
            return [dealt(even, a[part, :], b[part, :]) for part in (at, below)]

        own, rim = pairs(own_near, own_far), pairs(rim_near, rim_far)
        other = pairs(near, far)
        far_kap = jnp.where(first_group, kept[at, :], swapped[at, :])
        far_wet = jnp.where(first_group, swapped[at, :], kept[at, :])
        rim_other = [dealt(even, rim_other_near[at, :], far_kap), dealt(even, rim_other_near[below, :], far_wet)]
        for side, row, inner in ((0, 0, 1), (1, ROWS - 1, ROWS - 2)):
            face = 0.5 * (rim[0][side] + rim_other[0][side]) * rim[1][side] * rim_other[1][side]
            change = face * (other[0][side] - own[0][side])
            along, link = (links[pl.ds((block * LINKS + side * 2 + i) * 8, 8), :] for i in range(2))
            flux = along * (east(change) - change)
            passed = link * change
            on_row = (change + (flux - west(flux)) - passed
                      + face * (other[1][side] - own[1][side] - 2.0 * change))
            for j in range(width // 128):
                lanes = slice(j * 128, (j + 1) * 128)
                change_ref[pl.ds(j * ROWS + row, 8, stride=tall), :] = on_row[:, lanes]
                change_ref[pl.ds(j * ROWS + inner, 8, stride=tall), :] = passed[:, lanes]
        for k in range(8):
            level = block * 8 + k
            change = jnp.where(on_rim, unstacked(change_ref[level_at(k, width), :]), 0.0)
            u2, first = (u2_high, 0) if level < BEFORE_SWAP else (u2_low, BEFORE_SWAP)
            buffer[rows_at(level), :] = u2[rows_at(level - first), :] + change
        whole = pl.ds(block * 8 * ROWS, 8 * ROWS)
        copy = pltpu.make_async_copy(buffer.at[whole], out.at[whole], sems.at[block])
        copy.start()
        copies.append(copy)
    for copy in copies:
        copy.wait()


def swap(array, start, axis="tile"):
    firsts = range(start, lax.axis_size(axis) - 1, 2)
    return lax.ppermute(array, axis, [(i, i + 1) for i in firsts] + [(i + 1, i) for i in firsts])


def exchange(to_near, to_far):
    from_far = swap(to_far, 1)
    return swap(to_near, 0), from_far


def body(ct_tracer, ct_surface, kappa, kvert, land, kmt, screen, layer_weight):
    levels, rows, width = ct_tracer.shape
    count = lax.axis_size("tile")
    tall = levels * rows
    tile, brick, flat = (rows, width), (tall * width // 128, 128), (tall, width)
    rim, link_rows = (2 * levels, width), (levels * LINKS, width)
    scalars, whole = pltpu.SMEM((levels,), FLOAT), pltpu.VMEM(flat, FLOAT)
    ints, tile_ints = pltpu.VMEM(flat, jnp.int32), pltpu.VMEM(tile, jnp.int32)
    bricks, tiles = pltpu.VMEM(brick, FLOAT), pltpu.VMEM(tile, FLOAT)
    ct_tracer, kappa, kvert, land = (left(a.reshape(flat)) for a in (ct_tracer, kappa, kvert, land))
    kmt, layer_weight = left(kmt), left(layer_weight)
    semaphores = pltpu.SemaphoreType.DMA

    height, surface, s_fx, s_fn, s_dg, q1, base, to_near, to_far, wet = kernel(
        functools.partial(setup_body, levels), vmem(*[tile] * 9, brick), in_hbm(5), in_vmem(10), "setup",
        [scalars, ints, tile_ints, tiles, semaphores((8,))],
    )(layer_weight, land, kmt, left(ct_surface), left(screen))
    near, far = exchange(to_near, to_far)

    rim_near, rim_far, rim_sent, links = kernel(
        functools.partial(rims_body, levels), vmem(rim, rim, (levels, width)) + hbm(link_rows), in_hbm(1) + in_vmem(1),
        in_vmem(3) + in_hbm(1), "rims", [whole, bricks, pltpu.VMEM(link_rows, FLOAT), semaphores((4 + levels // 8,))],
    )(kappa, wet)
    links_free, links = links, left(links)
    rim_other_near, kept = exchange(rim_near, rim_sent)

    basis, sums = kernel(
        basis_body, vmem((3 * rows, width), (count, 128)), in_vmem(9) + in_hbm(1),
        in_vmem(2), "basis"
    )(base, height, surface, s_fx, s_fn, s_dg, q1, near, far, links)
    sums = lax.all_to_all(sums.reshape(count, 1, 128), "tile", 0, 0, tiled=True).reshape(count, 128)

    solution, u0, row_near, row_far = kernel(
        functools.partial(columns_body, levels), hbm(tile) + vmem(brick, rim, rim), in_vmem(2) + in_hbm(6),
        in_hbm(1) + in_vmem(3), "columns",
        [scalars, tile_ints, whole, whole, ints, pltpu.VMEM(link_rows, FLOAT), tiles, bricks, semaphores((15,)),
         semaphores((1,))],
    )(sums, basis, layer_weight, kmt, ct_tracer, kvert, land, links)
    other_near, other_far = exchange(row_near, row_far)

    def inner(first, last, name, *relayed):
        size = ((last - first) * rows, width)
        return kernel(
            functools.partial(inner_body, first, last, bool(relayed)), vmem(size, *[(levels, width) for _ in relayed]),
            in_vmem(1) + in_hbm(3) + in_vmem(len(relayed)), in_vmem(1 + len(relayed)), name,
            [tile_ints, pltpu.VMEM(size, FLOAT), pltpu.VMEM(size, jnp.int32), semaphores((1 + 2 * (last - first) // PART,))],
        )(u0, kmt, kappa, land, *relayed)

    u2_high, relayed = inner(0, BEFORE_SWAP, "inner_high", kept)
    swapped = swap(relayed, 0, "grp")
    (u2_low,) = inner(BEFORE_SWAP, levels, "inner_low")

    values = kernel(
        functools.partial(finish_body, levels), hbm(flat), in_vmem(12), in_hbm(1), "finish",
        [pltpu.VMEM((8 * rows * width // 128, 128), FLOAT), whole, semaphores((levels // 8,))],
    )(u2_high, u2_low, held(links_free), row_near, row_far, rim_near, rim_far, other_near, other_far, rim_other_near,
      kept, swapped)[0]
    return (values.reshape(levels, rows, width), solution)


def solution(mesh):
    in_specs = (
        P(None, ("grp", "tile"), None),
        P(("grp", "tile"), None),
        P(None, "tile", None),
        P(None, "tile", None),
        P(None, "tile", None),
        P("tile", None),
        P("tile", None),
        P(),
    )
    out_specs = (P(None, ("grp", "tile"), None), P(("grp", "tile"), None))
    return jax.shard_map(body, mesh=mesh, in_specs=in_specs, out_specs=out_specs, check_vma=False)
```

```python
import functools

import jax
import jax.numpy as jnp
from jax import lax
from jax.experimental import pallas as pl
from jax.experimental.pallas import tpu as pltpu
from jax.sharding import PartitionSpec as P

ITERS = 3
ROWS = 8
LOW = 0.05
HIGH = 9.0
MID = 0.5 * (HIGH + LOW)
HALF = 0.5 * (HIGH - LOW)
FLOAT = jnp.float32
LINKS = 4
GROUP = 4
UPPER = 24
BEFORE_SWAP = 16
LIMIT = 24 * 1024 * 1024


def east(values):
    return pltpu.roll(values, values.shape[1] - 1, 1)


def west(values):
    return pltpu.roll(values, 1, 1)


def north(values):
    return pltpu.roll(values, values.shape[0] - 1, 0)


def south(values):
    return pltpu.roll(values, 1, 0)


def stacked(values):
    return jnp.concatenate([values[:, i : i + 128] for i in range(0, values.shape[1], 128)], axis=0)


def unstacked(values):
    return jnp.concatenate([values[i : i + ROWS, :] for i in range(0, values.shape[0], ROWS)], axis=1)


def row_of(ref, block, row, width):
    tall = width // 128 * ROWS
    return jnp.concatenate(
        [ref[pl.ds(block * 8 * tall + j * ROWS + row, 8, stride=tall), :] for j in range(width // 128)], axis=1
    )


def level_at(k, width):
    tall = width // 128 * ROWS
    return pl.ds(pl.multiple_of(k * tall, tall), tall)


def rows_at(k):
    return pl.ds(pl.multiple_of(k * ROWS, ROWS), ROWS)


def row_index(values):
    return lax.broadcasted_iota(jnp.int32, values.shape, 0)


def spread(row, like):
    return jnp.broadcast_to(row, like.shape)


def vmem(*shapes):
    return [pltpu.VMEM(shape, FLOAT) for shape in shapes]


def hbm(*shapes):
    return [pltpu.HBM(shape, FLOAT) for shape in shapes]


def in_vmem(count):
    return [pl.BlockSpec(memory_space=pltpu.VMEM)] * count


def in_hbm(count):
    return [pl.BlockSpec(memory_space=pltpu.HBM)] * count


def kernel(body, outs, ins, out_specs, name, scratch=(), cost=1, aliases={}):
    return pl.pallas_call(
        body,
        out_shape=outs,
        in_specs=ins,
        out_specs=out_specs,
        scratch_shapes=list(scratch),
        name=name,
        input_output_aliases=aliases,
        cost_estimate=pl.CostEstimate(flops=cost, bytes_accessed=cost, transcendentals=0),
        compiler_params=pltpu.CompilerParams(vmem_limit_bytes=LIMIT),
    )


def held(array):
    return pltpu.with_memory_space_constraint(array, pltpu.VMEM)


def left(array):
    return pltpu.with_memory_space_constraint(array, pltpu.HBM)


def is_even():
    return lax.rem(lax.axis_index("tile"), 2) == 0


def is_first():
    return lax.rem(lax.axis_index("grp"), 2) == 0


def dealt(even, low, high):
    return jnp.where(even, high, low), jnp.where(even, low, high)


def loads(pairs, sems, first=0):
    copies = [pltpu.make_async_copy(far, near, sems.at[first + i]) for i, (far, near) in enumerate(pairs)]
    for copy in copies:
        copy.start()
    return copies


def in_parts(far, near, parts):
    size = far.shape[0] // parts
    return [(far.at[pl.ds(i * size, size)], near.at[pl.ds(i * size, size)]) for i in range(parts)]


def weight_sum(weight, levels):
    total = weight[0]
    for k in range(1, levels):
        total = total + weight[k]
    return total


def setup_body(levels, weight_hbm, land_hbm, kmt_hbm, ct_hbm, screen_hbm, height_ref, surface_ref,
               fx_ref, fn_ref, dg_ref, q1_ref, base_ref, near_ref, far_ref, wet_bricks,
               weight, land, kmt, screen, sems):
    chunk = levels // 4
    small = loads(((weight_hbm, weight), (kmt_hbm, kmt)), sems)
    land_copies = loads(in_parts(land_hbm, land, 4), sems, 2)
    small += loads(((ct_hbm, base_ref), (screen_hbm, screen)), sems, 6)
    small[0].wait()
    total = weight_sum(weight, levels)
    small[1].wait()
    depth = kmt[...]
    width = depth.shape[1]
    height = jnp.zeros(depth.shape, FLOAT)
    for i, copy in enumerate(land_copies):
        copy.wait()

        def level(k, height):
            wet = jnp.where(k < depth, land[rows_at(k), :], 0).astype(FLOAT)
            wet_bricks[level_at(k, width), :] = stacked(wet)
            return height + weight[k] * wet

        height = lax.fori_loop(i * chunk, (i + 1) * chunk, level, height, unroll=4)
    height = height / total
    surface = jnp.where(0 < depth, land[0:ROWS, :], 0).astype(FLOAT)
    height_ref[...] = height
    surface_ref[...] = surface
    small[2].wait()
    small[3].wait()
    base = base_ref[...]
    rows = row_index(base)
    scale = 0.5 / HALF
    fx = scale * (height + east(height)) * surface * east(surface)
    fn = scale * (height + north(height)) * surface * north(surface)
    fn = jnp.where(rows < ROWS - 1, fn, 0.0)
    fs = south(fn)
    fw = west(fx)
    dg = (screen[...] - MID) * (1.0 / HALF) + fx + fw + fn + fs

    def apply(v):
        return dg * v - fx * east(v) - fw * west(v) - fn * north(v) - fs * south(v)

    q1 = apply(base)
    q2 = apply(q1)
    fx_ref[...] = fx
    fn_ref[...] = fn
    dg_ref[...] = dg
    q1_ref[...] = q1
    even = is_even()
    near_ref[7:8, :] = jnp.zeros_like(base[0:1, :])
    far_ref[7:8, :] = jnp.zeros_like(base[0:1, :])
    for place, values in enumerate((base, q1, q2, fx, dg, height, surface)):
        at = slice(place, place + 1)
        near_ref[at, :], far_ref[at, :] = dealt(even, values[0:1, :], values[ROWS - 1 : ROWS, :])


def rims_body(levels, kappa_hbm, wet_bricks, near_ref, far_ref, sent_ref, links_hbm, kappa, kappa_bricks, links, sems):
    chunk = levels // 4
    width = kappa.shape[1]
    for i, copy in enumerate(loads(in_parts(kappa_hbm, kappa, 4), sems)):
        copy.wait()

        def brick(k, carry):
            kappa_bricks[level_at(k, width), :] = stacked(kappa[rows_at(k), :])
            return carry

        lax.fori_loop(i * chunk, (i + 1) * chunk, brick, 0, unroll=4)
    even = is_even()
    first_group = is_first()
    outs = []
    for block in range(levels // 8):
        found = []
        for side, row, inner in ((0, 0, 1), (1, ROWS - 1, ROWS - 2)):
            kap, kap_in = row_of(kappa_bricks, block, row, width), row_of(kappa_bricks, block, inner, width)
            here, here_in = row_of(wet_bricks, block, row, width), row_of(wet_bricks, block, inner, width)
            at = (block * LINKS + side * 2) * 8
            links[pl.ds(at, 8), :] = 0.5 * (kap + east(kap)) * here * east(here)
            links[pl.ds(at + 8, 8), :] = 0.5 * (kap + kap_in) * here * here_in
            found.append((kap, here))
        for place in range(2):
            at = pl.ds(place * levels + block * 8, 8)
            near_ref[at, :], far_ref[at, :] = dealt(even, found[0][place], found[1][place])
        at, below = pl.ds(block * 8, 8), pl.ds(levels + block * 8, 8)
        sent_ref[at, :] = jnp.where(first_group, far_ref[at, :], far_ref[below, :])
        whole = pl.ds(block * LINKS * 8, LINKS * 8)
        outs += loads([(links.at[whole], links_hbm.at[whole])], sems, 4 + block)
    for copy in outs:
        copy.wait()


def basis_body(ct, height, surface, fx_ref, fn_ref, dg_ref, q1_ref, near, far, links_hbm, basis_ref, sums_ref):
    even = is_even()
    b0 = ct[...]
    rows = row_index(b0)
    first, last = rows == 0, rows == ROWS - 1
    fx, fn, dg = fx_ref[...], fn_ref[...], dg_ref[...]
    fw, fs = west(fx), south(fn)

    def halo(values, row):
        b0_h, q1_h, q2_h, fx_h, dg_h, high_h, wet_h = (values[i : i + 1, :] for i in range(7))
        face = (0.5 / HALF) * (high_h + height[row : row + 1, :]) * wet_h * surface[row : row + 1, :]
        extra = face * (b0_h - ct[row : row + 1, :])
        return b0_h, q1_h + extra, q2_h, fx_h, dg_h, face, extra

    def lift(row):
        return jnp.broadcast_to(row, b0.shape)

    before, after = dealt(even, near[...], far[...])
    sides = (halo(before, 0), halo(after, ROWS - 1))
    face_b, face_a = lift(sides[0][5]), lift(sides[1][5])
    b1 = q1_ref[...] - jnp.where(first, lift(sides[0][6]), 0.0) - jnp.where(last, lift(sides[1][6]), 0.0)
    dg = dg + jnp.where(first, face_b, 0.0) + jnp.where(last, face_a, 0.0)
    fn = jnp.where(last, face_a, fn)
    fs = jnp.where(first, face_b, fs)

    def apply(v, v_before, v_after):
        v_n = jnp.where(last, lift(v_after), north(v))
        v_s = jnp.where(first, lift(v_before), south(v))
        return dg * v - fx * east(v) - fw * west(v) - fn * v_n - fs * v_s

    b2 = 2.0 * apply(b1, sides[0][1], sides[1][1]) - b0

    def outer(side, own):
        b0_h, b1_h, q2_h, fx_h, dg_h, face, extra = side
        b0_h, b1_h, q2_h, fx_h, dg_h, face, extra, own = (lift(v) for v in (b0_h, b1_h, q2_h, fx_h, dg_h, face, extra, own))
        turned = dg_h * extra - fx_h * east(extra) - west(fx_h) * west(extra)
        return (2.0 * (q2_h + turned + face * (b1_h - own)) - b0_h)[0:1, :]

    for place, values in enumerate((b0, b1, b2)):
        basis_ref[pl.ds(place * ROWS, ROWS), :] = values
    b2_b = outer(sides[0], b1[0:1, :])
    b2_a = outer(sides[1], b1[ROWS - 1 : ROWS, :])
    next2 = apply(b2, b2_b, b2_a)
    lanes = lax.broadcasted_iota(jnp.int32, (1, 128), 1)
    packed = jnp.zeros((1, 128), FLOAT)
    for place, (p, q) in enumerate(((b0, b0), (b0, b1), (b1, b1), (b1, b2), (b2, b2), (b2, next2))):
        product = p * q
        folded = product[:, 0:128]
        for j in range(1, product.shape[1] // 128):
            folded = folded + product[:, j * 128 : (j + 1) * 128]
        total = jnp.sum(jnp.sum(folded, axis=0, keepdims=True), axis=1, keepdims=True)
        packed = jnp.where(lanes == place, total, packed)
    sums_ref[...] = jnp.broadcast_to(packed, sums_ref.shape)


def quadratic(left, form):
    total = None
    for i in range(3):
        for j in range(3):
            if left[i] is not None and left[j] is not None:
                term = left[i] * left[j] * form[i][j]
                total = term if total is None else total + term
    return total


def plus(p, q):
    return q if p is None else p if q is None else p + q


def times(scale, p):
    return None if p is None else scale * p


def weights(sums):
    s0, s1, s2, s3, s4, s5 = sums
    g02 = 2.0 * s2 - s0
    gram = ((s0, s1, g02), (s1, s2, s3), (g02, s3, s4))
    b11, b12 = 0.5 * (s3 + s1), 0.5 * (s4 + g02)
    shift = ((s1, s2, s3), (s2, b11, b12), (s3, b12, s5))
    form = [[MID * gram[i][j] + HALF * shift[i][j] for j in range(3)] for i in range(3)]
    one = jnp.ones_like(s0)
    x, r, d = [None] * 3, [one, None, None], [one, None, None]
    rr = s0
    for step in range(ITERS):
        alpha = jnp.clip(rr / quadratic(d, form), 1.0 / HIGH, 1.0 / LOW)
        x = [plus(x[i], times(alpha, d[i])) for i in range(3)]
        if step + 1 < ITERS:
            image = [
                plus(times(MID, d[0]), times(0.5 * HALF, d[1])),
                plus(plus(times(MID, d[1]), times(HALF, d[0])), times(0.5 * HALF, d[2])),
                plus(times(MID, d[2]), times(0.5 * HALF, d[1])),
            ]
            r = [plus(r[i], times(-1.0, times(alpha, image[i]))) for i in range(3)]
            new = quadratic(r, gram)
            beta = jnp.clip(new / rr, 0.0, HIGH / LOW)
            d = [plus(r[i], times(beta, d[i])) for i in range(3)]
            rr = new
    return x


def inverse_of(values):
    guess = pl.reciprocal(values, approx=True)
    guess = guess * (2.0 - values * guess)
    return guess * (2.0 - values * guess)


def send_rows(u, links, near_ref, far_ref, width):
    even = is_even()
    levels = near_ref.shape[0] // 2
    for block in range(levels // 8):
        found = []
        for side, row, inner in ((0, 0, 1), (1, ROWS - 1, ROWS - 2)):
            value, value_in = row_of(u, block, row, width), row_of(u, block, inner, width)
            face, link = (links[pl.ds((block * LINKS + side * 2 + i) * 8, 8), :] for i in range(2))
            flux = face * (east(value) - value)
            found.append((value, value + (flux - west(flux)) + link * (value_in - value)))
        for place in range(2):
            at = pl.ds(place * levels + block * 8, 8)
            near_ref[at, :], far_ref[at, :] = dealt(even, found[0][place], found[1][place])


def segments(start, stop):
    cuts = [start] + ([UPPER] if start < UPPER < stop else []) + [stop]
    return [(a, b, b <= UPPER) for a, b in zip(cuts[:-1], cuts[1:])]


def columns_body(levels, sums, basis_ref, weight_hbm, kmt_hbm, source_hbm, kvert_hbm, land_hbm, links_hbm,
                 kappa_hbm, out_hbm, high, ratio, low, links_high, near_ref, far_ref, kmt, kappa, land,
                 weight, source, kvert, links_low, s_ref, ratio_low, sems, out_sems):
    width = source.shape[1]
    parts = 4
    chunk = levels // parts
    small = loads(((weight_hbm, weight), (kmt_hbm, kmt)), sems)
    parted = [in_parts(far, near, parts) for far, near in ((land_hbm, land), (kvert_hbm, kvert), (source_hbm, source))]
    big = loads([pairs[i] for i in range(parts) for pairs in parted], sems, 2)
    top, bottom = pl.ds(0, UPPER * LINKS), pl.ds(UPPER * LINKS, (levels - UPPER) * LINKS)
    links_copies = loads([(links_hbm.at[bottom], links_low), (links_hbm.at[top], links_high)], sems, 2 + 3 * parts)
    kappa_copies = loads(in_parts(kappa_hbm, kappa, parts), sems, 4 + 3 * parts)

    total = jnp.sum(sums[...], axis=0, keepdims=True)
    mix = weights([total[:, i : i + 1] for i in range(6)])
    b0, b1, b2 = (basis_ref[i * ROWS : (i + 1) * ROWS, :] for i in range(3))
    s = mix[0] * b0 + mix[1] * b1 + mix[2] * b2
    s_ref[...] = s
    outs = loads([(s_ref, out_hbm)], out_sems)

    small[0].wait()
    scaled = stacked(s) / jnp.full((ROWS * width // 128, 128), weight_sum(weight, levels), FLOAT)
    small[1].wait()
    depth = stacked(kmt[...])

    def sea(k):
        return jnp.where(k < depth, stacked(land[rows_at(k), :]), 0).astype(FLOAT)

    def down(values, parts_of, first, k, carry):
        here, link, passed = carry
        at = level_at(k - first, width)
        below = jnp.where(k + 1 < levels, sea(jnp.minimum(k + 1, levels - 1)), 0.0)
        coupling = stacked(kvert[rows_at(k), :]) * here * below
        over = inverse_of(1.0 + coupling + link)
        value = (stacked(source[rows_at(k), :]) + here * (weight[k] * scaled) + passed) * over
        part = coupling * over
        parts_of[at, :] = part
        values[at, :] = value
        return below, coupling - coupling * part, coupling * value

    zero = jnp.zeros(scaled.shape, FLOAT)
    big[0].wait()
    carry = (sea(0), zero, zero)
    for i in range(parts):
        big[3 * i + 1].wait()
        big[3 * i + 2].wait()
        if i + 1 < parts:
            big[3 * i + 3].wait()
        for start, stop, is_high in segments(i * chunk, (i + 1) * chunk):
            target = (high, ratio, 0) if is_high else (low, ratio_low, UPPER)
            carry = lax.fori_loop(start, stop, functools.partial(down, *target), carry, unroll=4)
    ascend(low, low, ratio_low, zero, width)
    for copy in links_copies:
        copy.wait()
    send_rows(low, links_low, near_ref, far_ref, width)
    for copy in kappa_copies + outs:
        copy.wait()


def ascend(target, source, ratio, below, width):
    levels = target.shape[0] * 128 // (ROWS * width)

    def up(i, below):
        at = level_at(levels - 1 - i, width)
        value = source[at, :] + ratio[at, :] * below
        target[at, :] = value
        return value

    lax.fori_loop(0, levels, up, below, unroll=4)


def upper_body(high, ratio, low, links, u, near_ref, far_ref):
    width = near_ref.shape[1]
    ascend(u, high, ratio, low[level_at(0, width), :], width)
    send_rows(u, links, near_ref, far_ref, width)


def inner_body(first, last, with_relay, high, low, kmt, kappa, land, *refs):
    u2_ref = refs[-1]
    if with_relay:
        passed, u2_ref, relay_ref = refs
        relay_ref[...] = passed[...]
    depth = kmt[...]
    width = depth.shape[1]
    inside = row_index(depth) < ROWS - 1

    def face(here, there):
        return jnp.where(jnp.minimum(here, there) > 0.0, here + there, 0.0)

    def group(source, source_first, i, carry):
        ks = [GROUP * i + j for j in range(GROUP)]
        sea = [jnp.where(k < depth, land[rows_at(k), :], 0) > 0 for k in ks]
        halved = [jnp.where(wet, 0.5 * kappa[rows_at(k), :], 0.0) for wet, k in zip(sea, ks)]
        u = [unstacked(source[level_at(k - source_first, width), :]) for k in ks]
        fx = [face(v, east(v)) for v in halved]
        fn = [jnp.where(inside, face(v, north(v)), 0.0) for v in halved]
        for _ in range(2):
            flux_x = [f * (east(v) - v) for f, v in zip(fx, u)]
            flux_y = [f * (north(v) - v) for f, v in zip(fn, u)]
            u = [v + (x - west(x)) + (y - south(y)) for v, x, y in zip(u, flux_x, flux_y)]
        for k, v in zip(ks, u):
            u2_ref[rows_at(k - first), :] = v
        return carry

    for start, stop, is_high in segments(first, last):
        step = functools.partial(group, *((high, 0) if is_high else (low, UPPER)))
        lax.fori_loop(start // GROUP, stop // GROUP, step, 0)


def finish_body(levels, first, last, skipped, u2_high, u2_low, links, own_near, own_far, near, far, rim_near, rim_far, rim_other_near,
                kept, swapped, *refs):
    out, change_ref, buffer, sems = refs[-4:]
    width = own_near.shape[1]
    tall = width // 128 * ROWS
    count = last - first
    rows = lax.broadcasted_iota(jnp.int32, (ROWS, width), 0)
    on_rim = (rows < 2) | (rows >= ROWS - 2)
    even = is_even()
    first_group = is_first()
    copies = []
    for block in range(count // 8):
        at, below = pl.ds(block * 8, 8), pl.ds(count + block * 8, 8)

        def pairs(a, b):
            return [dealt(even, a[part, :], b[part, :]) for part in (at, below)]

        own, other = pairs(own_near, own_far), pairs(near, far)
        here = pl.ds(first + block * 8, 8)
        under = pl.ds(levels + first + block * 8, 8)
        kap, wet = (dealt(even, rim_near[part, :], rim_far[part, :]) for part in (here, under))
        far_kap = jnp.where(first_group, kept[here, :], swapped[here, :])
        far_wet = jnp.where(first_group, swapped[here, :], kept[here, :])
        kap_other = dealt(even, rim_other_near[here, :], far_kap)
        wet_other = dealt(even, rim_other_near[under, :], far_wet)
        for side, row, inner in ((0, 0, 1), (1, ROWS - 1, ROWS - 2)):
            face = 0.5 * (kap[side] + kap_other[side]) * wet[side] * wet_other[side]
            change = face * (other[0][side] - own[0][side])
            along, link = (
                links[pl.ds(((skipped + block) * LINKS + side * 2 + i) * 8, 8), :] for i in range(2)
            )
            flux = along * (east(change) - change)
            passed = link * change
            on_row = (change + (flux - west(flux)) - passed
                      + face * (other[1][side] - own[1][side] - 2.0 * change))
            for j in range(width // 128):
                lanes = slice(j * 128, (j + 1) * 128)
                change_ref[pl.ds(j * ROWS + row, 8, stride=tall), :] = on_row[:, lanes]
                change_ref[pl.ds(j * ROWS + inner, 8, stride=tall), :] = passed[:, lanes]
        for k in range(8):
            level = first + block * 8 + k
            change = jnp.where(on_rim, unstacked(change_ref[level_at(k, width), :]), 0.0)
            u2, u2_first = (u2_high, 0) if level < BEFORE_SWAP else (u2_low, BEFORE_SWAP)
            buffer[rows_at(block * 8 + k), :] = u2[rows_at(level - u2_first), :] + change
        whole = pl.ds(block * 8 * ROWS, 8 * ROWS)
        target = pl.ds((first + block * 8) * ROWS, 8 * ROWS)
        copies += loads([(buffer.at[whole], out.at[target])], sems, block)
    for copy in copies:
        copy.wait()


def swap(array, start, axis="tile"):
    firsts = range(start, lax.axis_size(axis) - 1, 2)
    return lax.ppermute(array, axis, [(i, i + 1) for i in firsts] + [(i + 1, i) for i in firsts])


def exchange(to_near, to_far):
    from_far = swap(to_far, 1)
    return swap(to_near, 0), from_far


def body(ct_tracer, ct_surface, kappa, kvert, land, kmt, screen, layer_weight):
    levels, rows, width = ct_tracer.shape
    count = lax.axis_size("tile")
    tall = levels * rows
    tile, brick, flat = (rows, width), (tall * width // 128, 128), (tall, width)
    rim, link_rows = (2 * levels, width), (levels * LINKS, width)
    scalars, whole = pltpu.SMEM((levels,), FLOAT), pltpu.VMEM(flat, FLOAT)
    ints, tile_ints = pltpu.VMEM(flat, jnp.int32), pltpu.VMEM(tile, jnp.int32)
    bricks, tiles = pltpu.VMEM(brick, FLOAT), pltpu.VMEM(tile, FLOAT)
    ct_tracer, kappa, kvert, land = (left(a.reshape(flat)) for a in (ct_tracer, kappa, kvert, land))
    kmt, layer_weight = left(kmt), left(layer_weight)
    semaphores = pltpu.SemaphoreType.DMA

    height, surface, s_fx, s_fn, s_dg, q1, base, to_near, to_far, wet = kernel(
        functools.partial(setup_body, levels), vmem(*[tile] * 9, brick), in_hbm(5), in_vmem(10), "setup",
        [scalars, ints, tile_ints, tiles, semaphores((8,))],
    )(layer_weight, land, kmt, left(ct_surface), left(screen))
    near, far = exchange(to_near, to_far)

    rim_near, rim_far, rim_sent, links = kernel(
        functools.partial(rims_body, levels), vmem(rim, rim, (levels, width)) + hbm(link_rows), in_hbm(1) + in_vmem(1),
        in_vmem(3) + in_hbm(1), "rims", [whole, bricks, pltpu.VMEM(link_rows, FLOAT), semaphores((4 + levels // 8,))],
    )(kappa, wet)
    links_left = left(links)
    rim_other_near, kept = exchange(rim_near, rim_sent)

    basis, sums = kernel(
        basis_body, vmem((3 * rows, width), (count, 128)), in_vmem(9) + in_hbm(1),
        in_vmem(2), "basis"
    )(base, height, surface, s_fx, s_fn, s_dg, q1, near, far, links_left)
    sums = lax.all_to_all(sums.reshape(count, 1, 128), "tile", 0, 0, tiled=True).reshape(count, 128)

    lower = levels - UPPER
    per_level = brick[0] // levels
    high_bricks, low_bricks = (UPPER * per_level, 128), (lower * per_level, 128)
    high_links, low_links = (UPPER * LINKS, width), (lower * LINKS, width)
    high_rim, low_rim = (2 * UPPER, width), (2 * lower, width)
    solution, carried, ratio, low, links_high, low_near, low_far, kmt_held, kappa_held, land_held = kernel(
        functools.partial(columns_body, levels),
        hbm(tile) + vmem(high_bricks, high_bricks, low_bricks, high_links, low_rim, low_rim) + [tile_ints, whole, ints],
        in_vmem(2) + in_hbm(7), in_hbm(1) + in_vmem(9), "columns",
        [scalars, whole, whole, pltpu.VMEM(low_links, FLOAT), tiles, pltpu.VMEM(low_bricks, FLOAT), semaphores((20,)),
         semaphores((1,))],
    )(sums, basis, layer_weight, kmt, ct_tracer, kvert, land, links_left, kappa)
    low_other_near, low_other_far = exchange(low_near, low_far)
    high, high_near, high_far = kernel(
        upper_body, vmem(high_bricks, high_rim, high_rim), in_vmem(4), in_vmem(3), "upper_columns"
    )(carried, ratio, low, links_high)
    high_other_near, high_other_far = exchange(high_near, high_far)

    def inner(first, last, name, *relayed):
        return kernel(
            functools.partial(inner_body, first, last, bool(relayed)),
            vmem(((last - first) * rows, width), *[(levels, width) for _ in relayed]),
            in_vmem(5 + len(relayed)), in_vmem(1 + len(relayed)), name,
        )(high, low, kmt_held, kappa_held, land_held, *relayed)

    u2_high, relayed = inner(0, BEFORE_SWAP, "inner_high", kept)
    swapped = swap(relayed, 0, "grp")
    (u2_low,) = inner(BEFORE_SWAP, levels, "inner_low")
    rims = (rim_near, rim_far, rim_other_near, kept, swapped)

    def finish(first, last, skipped, name, more=(), aliases={}):
        count = last - first
        return kernel(
            functools.partial(finish_body, levels, first, last, skipped), hbm(flat), in_vmem(12) + in_hbm(len(more)),
            in_hbm(1), name,
            [pltpu.VMEM((8 * per_level, 128), FLOAT), pltpu.VMEM((count * rows, width), FLOAT), semaphores((count // 8,))],
            aliases=aliases,
        )

    deep = finish(UPPER, levels, UPPER // 8, "finish_low")(
        u2_high, u2_low, held(links), low_near, low_far, low_other_near, low_other_far, *rims
    )[0]
    values = finish(0, UPPER, 0, "finish_high", (deep,), {12: 0})(
        u2_high, u2_low, links_high, high_near, high_far, high_other_near, high_other_far, *rims, left(deep)
    )[0]
    return (values.reshape(levels, rows, width), solution)


def solution(mesh):
    in_specs = (
        P(None, ("grp", "tile"), None),
        P(("grp", "tile"), None),
        P(None, "tile", None),
        P(None, "tile", None),
        P(None, "tile", None),
        P("tile", None),
        P("tile", None),
        P(),
    )
    out_specs = (P(None, ("grp", "tile"), None), P(("grp", "tile"), None))
    return jax.shard_map(body, mesh=mesh, in_specs=in_specs, out_specs=out_specs, check_vma=False)
```

```python
import functools

import jax
import jax.numpy as jnp
from jax import lax
from jax.experimental import pallas as pl
from jax.experimental.pallas import tpu as pltpu
from jax.sharding import PartitionSpec as P

ITERS = 3
ROWS = 8
LOW = 0.05
HIGH = 9.0
MID = 0.5 * (HIGH + LOW)
HALF = 0.5 * (HIGH - LOW)
FLOAT = jnp.float32
LINKS = 4
GROUP = 4
PART = 8
BEFORE_SWAP = 16
LIMIT = 24 * 1024 * 1024


def east(values):
    return pltpu.roll(values, values.shape[1] - 1, 1)


def west(values):
    return pltpu.roll(values, 1, 1)


def north(values):
    return pltpu.roll(values, values.shape[0] - 1, 0)


def south(values):
    return pltpu.roll(values, 1, 0)


def stacked(values):
    return jnp.concatenate([values[:, i : i + 128] for i in range(0, values.shape[1], 128)], axis=0)


def unstacked(values):
    return jnp.concatenate([values[i : i + ROWS, :] for i in range(0, values.shape[0], ROWS)], axis=1)


def row_of(ref, block, row, width):
    tall = width // 128 * ROWS
    return jnp.concatenate(
        [ref[pl.ds(block * 8 * tall + j * ROWS + row, 8, stride=tall), :] for j in range(width // 128)], axis=1
    )


def level_at(k, width):
    tall = width // 128 * ROWS
    return pl.ds(pl.multiple_of(k * tall, tall), tall)


def rows_at(k):
    return pl.ds(pl.multiple_of(k * ROWS, ROWS), ROWS)


def row_index(values):
    return lax.broadcasted_iota(jnp.int32, values.shape, 0)


def spread(row, like):
    return jnp.broadcast_to(row, like.shape)


def vmem(*shapes):
    return [pltpu.VMEM(shape, FLOAT) for shape in shapes]


def hbm(*shapes):
    return [pltpu.HBM(shape, FLOAT) for shape in shapes]


def in_vmem(count):
    return [pl.BlockSpec(memory_space=pltpu.VMEM)] * count


def in_hbm(count):
    return [pl.BlockSpec(memory_space=pltpu.HBM)] * count


def kernel(body, outs, ins, out_specs, name, scratch=(), cost=1):
    return pl.pallas_call(
        body,
        out_shape=outs,
        in_specs=ins,
        out_specs=out_specs,
        scratch_shapes=list(scratch),
        name=name,
        cost_estimate=pl.CostEstimate(flops=cost, bytes_accessed=cost, transcendentals=0),
        compiler_params=pltpu.CompilerParams(vmem_limit_bytes=LIMIT),
    )


def held(array):
    return pltpu.with_memory_space_constraint(array, pltpu.VMEM)


def left(array):
    return pltpu.with_memory_space_constraint(array, pltpu.HBM)


def is_even():
    return lax.rem(lax.axis_index("tile"), 2) == 0


def is_first():
    return lax.rem(lax.axis_index("grp"), 2) == 0


def dealt(even, low, high):
    return jnp.where(even, high, low), jnp.where(even, low, high)


def loads(pairs, sems, first=0):
    copies = [pltpu.make_async_copy(far, near, sems.at[first + i]) for i, (far, near) in enumerate(pairs)]
    for copy in copies:
        copy.start()
    return copies


def in_parts(far, near, parts):
    size = far.shape[0] // parts
    return [(far.at[pl.ds(i * size, size)], near.at[pl.ds(i * size, size)]) for i in range(parts)]


def weight_sum(weight, levels):
    total = weight[0]
    for k in range(1, levels):
        total = total + weight[k]
    return total


def setup_body(levels, weight_hbm, land_hbm, kmt_hbm, ct_hbm, screen_hbm, height_ref, surface_ref,
               fx_ref, fn_ref, dg_ref, q1_ref, base_ref, near_ref, far_ref, wet_bricks,
               weight, land, kmt, screen, sems):
    chunk = levels // 4
    small = loads(((weight_hbm, weight), (kmt_hbm, kmt)), sems)
    land_copies = loads(in_parts(land_hbm, land, 4), sems, 2)
    small += loads(((ct_hbm, base_ref), (screen_hbm, screen)), sems, 6)
    small[0].wait()
    total = weight_sum(weight, levels)
    small[1].wait()
    depth = kmt[...]
    width = depth.shape[1]
    height = jnp.zeros(depth.shape, FLOAT)
    for i, copy in enumerate(land_copies):
        copy.wait()

        def level(k, height):
            wet = jnp.where(k < depth, land[rows_at(k), :], 0).astype(FLOAT)
            wet_bricks[level_at(k, width), :] = stacked(wet)
            return height + weight[k] * wet

        height = lax.fori_loop(i * chunk, (i + 1) * chunk, level, height, unroll=4)
    height = height / total
    surface = jnp.where(0 < depth, land[0:ROWS, :], 0).astype(FLOAT)
    height_ref[...] = height
    surface_ref[...] = surface
    small[2].wait()
    small[3].wait()
    base = base_ref[...]
    rows = row_index(base)
    scale = 0.5 / HALF
    fx = scale * (height + east(height)) * surface * east(surface)
    fn = scale * (height + north(height)) * surface * north(surface)
    fn = jnp.where(rows < ROWS - 1, fn, 0.0)
    fs = south(fn)
    fw = west(fx)
    dg = (screen[...] - MID) * (1.0 / HALF) + fx + fw + fn + fs

    def apply(v):
        return dg * v - fx * east(v) - fw * west(v) - fn * north(v) - fs * south(v)

    q1 = apply(base)
    q2 = apply(q1)
    fx_ref[...] = fx
    fn_ref[...] = fn
    dg_ref[...] = dg
    q1_ref[...] = q1
    even = is_even()
    near_ref[7:8, :] = jnp.zeros_like(base[0:1, :])
    far_ref[7:8, :] = jnp.zeros_like(base[0:1, :])
    for place, values in enumerate((base, q1, q2, fx, dg, height, surface)):
        at = slice(place, place + 1)
        near_ref[at, :], far_ref[at, :] = dealt(even, values[0:1, :], values[ROWS - 1 : ROWS, :])


def rims_body(levels, kappa_hbm, wet_bricks, near_ref, far_ref, sent_ref, links_hbm, kappa, kappa_bricks, links, sems):
    chunk = levels // 4
    width = kappa.shape[1]
    for i, copy in enumerate(loads(in_parts(kappa_hbm, kappa, 4), sems)):
        copy.wait()

        def brick(k, carry):
            kappa_bricks[level_at(k, width), :] = stacked(kappa[rows_at(k), :])
            return carry

        lax.fori_loop(i * chunk, (i + 1) * chunk, brick, 0, unroll=4)
    even = is_even()
    first_group = is_first()
    outs = []
    for block in range(levels // 8):
        found = []
        for side, row, inner in ((0, 0, 1), (1, ROWS - 1, ROWS - 2)):
            kap, kap_in = row_of(kappa_bricks, block, row, width), row_of(kappa_bricks, block, inner, width)
            here, here_in = row_of(wet_bricks, block, row, width), row_of(wet_bricks, block, inner, width)
            at = (block * LINKS + side * 2) * 8
            links[pl.ds(at, 8), :] = 0.5 * (kap + east(kap)) * here * east(here)
            links[pl.ds(at + 8, 8), :] = 0.5 * (kap + kap_in) * here * here_in
            found.append((kap, here))
        for place in range(2):
            at = pl.ds(place * levels + block * 8, 8)
            near_ref[at, :], far_ref[at, :] = dealt(even, found[0][place], found[1][place])
        at, below = pl.ds(block * 8, 8), pl.ds(levels + block * 8, 8)
        sent_ref[at, :] = jnp.where(first_group, far_ref[at, :], far_ref[below, :])
        whole = pl.ds(block * LINKS * 8, LINKS * 8)
        outs += loads([(links.at[whole], links_hbm.at[whole])], sems, 4 + block)
    for copy in outs:
        copy.wait()


def basis_body(ct, height, surface, fx_ref, fn_ref, dg_ref, q1_ref, near, far, links_hbm, basis_ref, sums_ref):
    even = is_even()
    b0 = ct[...]
    rows = row_index(b0)
    first, last = rows == 0, rows == ROWS - 1
    fx, fn, dg = fx_ref[...], fn_ref[...], dg_ref[...]
    fw, fs = west(fx), south(fn)

    def halo(values, row):
        b0_h, q1_h, q2_h, fx_h, dg_h, high_h, wet_h = (values[i : i + 1, :] for i in range(7))
        face = (0.5 / HALF) * (high_h + height[row : row + 1, :]) * wet_h * surface[row : row + 1, :]
        extra = face * (b0_h - ct[row : row + 1, :])
        return b0_h, q1_h + extra, q2_h, fx_h, dg_h, face, extra

    def lift(row):
        return jnp.broadcast_to(row, b0.shape)

    before, after = dealt(even, near[...], far[...])
    sides = (halo(before, 0), halo(after, ROWS - 1))
    face_b, face_a = lift(sides[0][5]), lift(sides[1][5])
    b1 = q1_ref[...] - jnp.where(first, lift(sides[0][6]), 0.0) - jnp.where(last, lift(sides[1][6]), 0.0)
    dg = dg + jnp.where(first, face_b, 0.0) + jnp.where(last, face_a, 0.0)
    fn = jnp.where(last, face_a, fn)
    fs = jnp.where(first, face_b, fs)

    def apply(v, v_before, v_after):
        v_n = jnp.where(last, lift(v_after), north(v))
        v_s = jnp.where(first, lift(v_before), south(v))
        return dg * v - fx * east(v) - fw * west(v) - fn * v_n - fs * v_s

    b2 = 2.0 * apply(b1, sides[0][1], sides[1][1]) - b0

    def outer(side, own):
        b0_h, b1_h, q2_h, fx_h, dg_h, face, extra = side
        b0_h, b1_h, q2_h, fx_h, dg_h, face, extra, own = (lift(v) for v in (b0_h, b1_h, q2_h, fx_h, dg_h, face, extra, own))
        turned = dg_h * extra - fx_h * east(extra) - west(fx_h) * west(extra)
        return (2.0 * (q2_h + turned + face * (b1_h - own)) - b0_h)[0:1, :]

    for place, values in enumerate((b0, b1, b2)):
        basis_ref[pl.ds(place * ROWS, ROWS), :] = values
    b2_b = outer(sides[0], b1[0:1, :])
    b2_a = outer(sides[1], b1[ROWS - 1 : ROWS, :])
    next2 = apply(b2, b2_b, b2_a)
    lanes = lax.broadcasted_iota(jnp.int32, (1, 128), 1)
    packed = jnp.zeros((1, 128), FLOAT)
    for place, (p, q) in enumerate(((b0, b0), (b0, b1), (b1, b1), (b1, b2), (b2, b2), (b2, next2))):
        product = p * q
        folded = product[:, 0:128]
        for j in range(1, product.shape[1] // 128):
            folded = folded + product[:, j * 128 : (j + 1) * 128]
        total = jnp.sum(jnp.sum(folded, axis=0, keepdims=True), axis=1, keepdims=True)
        packed = jnp.where(lanes == place, total, packed)
    sums_ref[...] = jnp.broadcast_to(packed, sums_ref.shape)


def quadratic(left, form):
    total = None
    for i in range(3):
        for j in range(3):
            if left[i] is not None and left[j] is not None:
                term = left[i] * left[j] * form[i][j]
                total = term if total is None else total + term
    return total


def plus(p, q):
    return q if p is None else p if q is None else p + q


def times(scale, p):
    return None if p is None else scale * p


def weights(sums):
    s0, s1, s2, s3, s4, s5 = sums
    g02 = 2.0 * s2 - s0
    gram = ((s0, s1, g02), (s1, s2, s3), (g02, s3, s4))
    b11, b12 = 0.5 * (s3 + s1), 0.5 * (s4 + g02)
    shift = ((s1, s2, s3), (s2, b11, b12), (s3, b12, s5))
    form = [[MID * gram[i][j] + HALF * shift[i][j] for j in range(3)] for i in range(3)]
    one = jnp.ones_like(s0)
    x, r, d = [None] * 3, [one, None, None], [one, None, None]
    rr = s0
    for step in range(ITERS):
        alpha = jnp.clip(rr / quadratic(d, form), 1.0 / HIGH, 1.0 / LOW)
        x = [plus(x[i], times(alpha, d[i])) for i in range(3)]
        if step + 1 < ITERS:
            image = [
                plus(times(MID, d[0]), times(0.5 * HALF, d[1])),
                plus(plus(times(MID, d[1]), times(HALF, d[0])), times(0.5 * HALF, d[2])),
                plus(times(MID, d[2]), times(0.5 * HALF, d[1])),
            ]
            r = [plus(r[i], times(-1.0, times(alpha, image[i]))) for i in range(3)]
            new = quadratic(r, gram)
            beta = jnp.clip(new / rr, 0.0, HIGH / LOW)
            d = [plus(r[i], times(beta, d[i])) for i in range(3)]
            rr = new
    return x


def inverse_of(values):
    guess = pl.reciprocal(values, approx=True)
    guess = guess * (2.0 - values * guess)
    return guess * (2.0 - values * guess)


def columns_body(levels, sums, basis_ref, weight_hbm, kmt_hbm, source_hbm, kvert_hbm, land_hbm, links_hbm,
                 out_hbm, u, near_ref, far_ref, weight, kmt, source, kvert, land, links, s_ref, ratio, sems, out_sems):
    width = source.shape[1]
    parts = 4
    chunk = levels // parts
    small = loads(((weight_hbm, weight), (kmt_hbm, kmt)), sems)
    parted = [in_parts(far, near, parts) for far, near in ((land_hbm, land), (kvert_hbm, kvert), (source_hbm, source))]
    big = loads([pairs[i] for i in range(parts) for pairs in parted], sems, 2)
    links_copy = loads([(links_hbm, links)], sems, 2 + 3 * parts)[0]

    total = jnp.sum(sums[...], axis=0, keepdims=True)
    mix = weights([total[:, i : i + 1] for i in range(6)])
    b0, b1, b2 = (basis_ref[i * ROWS : (i + 1) * ROWS, :] for i in range(3))
    s = mix[0] * b0 + mix[1] * b1 + mix[2] * b2
    s_ref[...] = s
    outs = loads([(s_ref, out_hbm)], out_sems)

    small[0].wait()
    scaled = stacked(s) / jnp.full((ROWS * width // 128, 128), weight_sum(weight, levels), FLOAT)
    small[1].wait()
    depth = stacked(kmt[...])

    def sea(k):
        return jnp.where(k < depth, stacked(land[rows_at(k), :]), 0).astype(FLOAT)

    def down(k, carry):
        here, link, passed = carry
        at = level_at(k, width)
        below = jnp.where(k + 1 < levels, sea(jnp.minimum(k + 1, levels - 1)), 0.0)
        coupling = stacked(kvert[rows_at(k), :]) * here * below
        over = inverse_of(1.0 + coupling + link)
        value = (stacked(source[rows_at(k), :]) + here * (weight[k] * scaled) + passed) * over
        part = coupling * over
        ratio[at, :] = part
        u[at, :] = value
        return below, coupling - coupling * part, coupling * value

    zero = jnp.zeros(scaled.shape, FLOAT)
    big[0].wait()
    carry = (sea(0), zero, zero)
    for i in range(parts):
        big[3 * i + 1].wait()
        big[3 * i + 2].wait()
        if i + 1 < parts:
            big[3 * i + 3].wait()
        carry = lax.fori_loop(i * chunk, (i + 1) * chunk, down, carry, unroll=4)

    def up(i, below):
        at = level_at(levels - 1 - i, width)
        value = u[at, :] + ratio[at, :] * below
        u[at, :] = value
        return value

    lax.fori_loop(0, levels, up, zero, unroll=4)
    links_copy.wait()
    even = is_even()
    for block in range(levels // 8):
        found = []
        for side, row, inner in ((0, 0, 1), (1, ROWS - 1, ROWS - 2)):
            value, value_in = row_of(u, block, row, width), row_of(u, block, inner, width)
            face, link = (links[pl.ds((block * LINKS + side * 2 + i) * 8, 8), :] for i in range(2))
            flux = face * (east(value) - value)
            found.append((value, value + (flux - west(flux)) + link * (value_in - value)))
        for place in range(2):
            at = pl.ds(place * levels + block * 8, 8)
            near_ref[at, :], far_ref[at, :] = dealt(even, found[0][place], found[1][place])
    for copy in outs:
        copy.wait()


def inner_body(first, last, relays, u0, kmt_hbm, kappa_hbm, land_hbm, *refs):
    passed, (u2_ref, *relayed), (kmt, kappa, land, sems) = refs[:relays], refs[relays : 2 * relays + 1], refs[-4:]
    for source, target in zip(passed, relayed):
        target[...] = source[...]
    size = PART * ROWS
    parts = (last - first) // PART
    kmt_copy = loads([(kmt_hbm, kmt)], sems)[0]
    pairs = []
    for i in range(parts):
        source, target = pl.ds((first + i * PART) * ROWS, size), pl.ds(i * size, size)
        pairs += [(kappa_hbm.at[source], kappa.at[target]), (land_hbm.at[source], land.at[target])]
    copies = loads(pairs, sems, 1)
    kmt_copy.wait()
    depth = kmt[...]
    width = depth.shape[1]
    inside = row_index(depth) < ROWS - 1

    def face(here, there):
        return jnp.where(jnp.minimum(here, there) > 0.0, here + there, 0.0)

    def group(i, carry):
        ks = [GROUP * i + j for j in range(GROUP)]
        sea = [jnp.where(k + first < depth, land[rows_at(k), :], 0) > 0 for k in ks]
        halved = [jnp.where(wet, 0.5 * kappa[rows_at(k), :], 0.0) for wet, k in zip(sea, ks)]
        u = [unstacked(u0[level_at(k + first, width), :]) for k in ks]
        fx = [face(v, east(v)) for v in halved]
        fn = [jnp.where(inside, face(v, north(v)), 0.0) for v in halved]
        for _ in range(2):
            flux_x = [f * (east(v) - v) for f, v in zip(fx, u)]
            flux_y = [f * (north(v) - v) for f, v in zip(fn, u)]
            u = [v + (x - west(x)) + (y - south(y)) for v, x, y in zip(u, flux_x, flux_y)]
        for k, v in zip(ks, u):
            u2_ref[rows_at(k), :] = v
        return carry

    for i in range(parts):
        copies[2 * i].wait()
        copies[2 * i + 1].wait()
        lax.fori_loop(i * PART // GROUP, (i + 1) * PART // GROUP, group, 0)


def finish_body(levels, u2_high, u2_low, links, own_near, own_far, rim_near, rim_far, near, far, rim_other_near, kept, swapped,
                out, change_ref, buffer, sems):
    width = own_near.shape[1]
    tall = width // 128 * ROWS
    rows = lax.broadcasted_iota(jnp.int32, (ROWS, width), 0)
    on_rim = (rows < 2) | (rows >= ROWS - 2)
    even = is_even()
    first_group = is_first()
    copies = []
    for block in range(levels // 8):
        at, below = pl.ds(block * 8, 8), pl.ds(levels + block * 8, 8)

        def pairs(a, b):
            return [dealt(even, a[part, :], b[part, :]) for part in (at, below)]

        own, rim = pairs(own_near, own_far), pairs(rim_near, rim_far)
        other = pairs(near, far)
        far_kap = jnp.where(first_group, kept[at, :], swapped[at, :])
        far_wet = jnp.where(first_group, swapped[at, :], kept[at, :])
        rim_other = [dealt(even, rim_other_near[at, :], far_kap), dealt(even, rim_other_near[below, :], far_wet)]
        for side, row, inner in ((0, 0, 1), (1, ROWS - 1, ROWS - 2)):
            face = 0.5 * (rim[0][side] + rim_other[0][side]) * rim[1][side] * rim_other[1][side]
            change = face * (other[0][side] - own[0][side])
            along, link = (links[pl.ds((block * LINKS + side * 2 + i) * 8, 8), :] for i in range(2))
            flux = along * (east(change) - change)
            passed = link * change
            on_row = (change + (flux - west(flux)) - passed
                      + face * (other[1][side] - own[1][side] - 2.0 * change))
            for j in range(width // 128):
                lanes = slice(j * 128, (j + 1) * 128)
                change_ref[pl.ds(j * ROWS + row, 8, stride=tall), :] = on_row[:, lanes]
                change_ref[pl.ds(j * ROWS + inner, 8, stride=tall), :] = passed[:, lanes]
        for k in range(8):
            level = block * 8 + k
            change = jnp.where(on_rim, unstacked(change_ref[level_at(k, width), :]), 0.0)
            u2, first = (u2_high, 0) if level < BEFORE_SWAP else (u2_low, BEFORE_SWAP)
            buffer[rows_at(level), :] = u2[rows_at(level - first), :] + change
        whole = pl.ds(block * 8 * ROWS, 8 * ROWS)
        copy = pltpu.make_async_copy(buffer.at[whole], out.at[whole], sems.at[block])
        copy.start()
        copies.append(copy)
    for copy in copies:
        copy.wait()


def swap(array, start, axis="tile"):
    firsts = range(start, lax.axis_size(axis) - 1, 2)
    return lax.ppermute(array, axis, [(i, i + 1) for i in firsts] + [(i + 1, i) for i in firsts])


def exchange(to_near, to_far):
    from_far = swap(to_far, 1)
    return swap(to_near, 0), from_far


def body(ct_tracer, ct_surface, kappa, kvert, land, kmt, screen, layer_weight):
    levels, rows, width = ct_tracer.shape
    count = lax.axis_size("tile")
    tall = levels * rows
    tile, brick, flat = (rows, width), (tall * width // 128, 128), (tall, width)
    rim, link_rows = (2 * levels, width), (levels * LINKS, width)
    scalars, whole = pltpu.SMEM((levels,), FLOAT), pltpu.VMEM(flat, FLOAT)
    ints, tile_ints = pltpu.VMEM(flat, jnp.int32), pltpu.VMEM(tile, jnp.int32)
    bricks, tiles = pltpu.VMEM(brick, FLOAT), pltpu.VMEM(tile, FLOAT)
    ct_tracer, kappa, kvert, land = (left(a.reshape(flat)) for a in (ct_tracer, kappa, kvert, land))
    kmt, layer_weight = left(kmt), left(layer_weight)
    semaphores = pltpu.SemaphoreType.DMA

    height, surface, s_fx, s_fn, s_dg, q1, base, to_near, to_far, wet = kernel(
        functools.partial(setup_body, levels), vmem(*[tile] * 9, brick), in_hbm(5), in_vmem(10), "setup",
        [scalars, ints, tile_ints, tiles, semaphores((8,))],
    )(layer_weight, land, kmt, left(ct_surface), left(screen))
    near, far = exchange(to_near, to_far)

    rim_near, rim_far, rim_sent, links = kernel(
        functools.partial(rims_body, levels), vmem(rim, rim, (levels, width)) + hbm(link_rows), in_hbm(1) + in_vmem(1),
        in_vmem(3) + in_hbm(1), "rims", [whole, bricks, pltpu.VMEM(link_rows, FLOAT), semaphores((4 + levels // 8,))],
    )(kappa, wet)
    links_free, links = links, left(links)
    rim_other_near, kept = exchange(rim_near, rim_sent)

    basis, sums = kernel(
        basis_body, vmem((3 * rows, width), (count, 128)), in_vmem(9) + in_hbm(1),
        in_vmem(2), "basis"
    )(base, height, surface, s_fx, s_fn, s_dg, q1, near, far, links)
    sums = lax.all_to_all(sums.reshape(count, 1, 128), "tile", 0, 0, tiled=True).reshape(count, 128)

    solution, u0, row_near, row_far = kernel(
        functools.partial(columns_body, levels), hbm(tile) + vmem(brick, rim, rim), in_vmem(2) + in_hbm(6),
        in_hbm(1) + in_vmem(3), "columns",
        [scalars, tile_ints, whole, whole, ints, pltpu.VMEM(link_rows, FLOAT), tiles, bricks, semaphores((15,)),
         semaphores((1,))],
    )(sums, basis, layer_weight, kmt, ct_tracer, kvert, land, links)
    other_far = swap(row_far, 1)

    def inner(first, last, name, *relayed):
        size = ((last - first) * rows, width)
        return kernel(
            functools.partial(inner_body, first, last, len(relayed)), vmem(size, *[array.shape for array in relayed]),
            in_vmem(1) + in_hbm(3) + in_vmem(len(relayed)), in_vmem(1 + len(relayed)), name,
            [tile_ints, pltpu.VMEM(size, FLOAT), pltpu.VMEM(size, jnp.int32), semaphores((1 + 2 * (last - first) // PART,))],
        )(u0, kmt, kappa, land, *relayed)

    u2_high, kept_on, near_on = inner(0, BEFORE_SWAP, "inner_high", kept, row_near)
    swapped = swap(kept_on, 0, "grp")
    other_near = swap(near_on, 0)
    (u2_low,) = inner(BEFORE_SWAP, levels, "inner_low")

    values = kernel(
        functools.partial(finish_body, levels), hbm(flat), in_vmem(12), in_hbm(1), "finish",
        [pltpu.VMEM((8 * rows * width // 128, 128), FLOAT), whole, semaphores((levels // 8,))],
    )(u2_high, u2_low, held(links_free), row_near, row_far, rim_near, rim_far, other_near, other_far, rim_other_near,
      kept, swapped)[0]
    return (values.reshape(levels, rows, width), solution)


def solution(mesh):
    in_specs = (
        P(None, ("grp", "tile"), None),
        P(("grp", "tile"), None),
        P(None, "tile", None),
        P(None, "tile", None),
        P(None, "tile", None),
        P("tile", None),
        P("tile", None),
        P(),
    )
    out_specs = (P(None, ("grp", "tile"), None), P(("grp", "tile"), None))
    return jax.shard_map(body, mesh=mesh, in_specs=in_specs, out_specs=out_specs, check_vma=False)
```

```python
import functools

import jax
import jax.numpy as jnp
from jax import lax
from jax.experimental import pallas as pl
from jax.experimental.pallas import tpu as pltpu
from jax.sharding import PartitionSpec as P

ITERS = 3
ROWS = 8
LOW = 0.05
HIGH = 9.0
MID = 0.5 * (HIGH + LOW)
HALF = 0.5 * (HIGH - LOW)
FLOAT = jnp.float32
LINKS = 4
GROUP = 4
PART = 8
BEFORE_SWAP = 16
LIMIT = 24 * 1024 * 1024


def east(values):
    return pltpu.roll(values, values.shape[1] - 1, 1)


def west(values):
    return pltpu.roll(values, 1, 1)


def north(values):
    return pltpu.roll(values, values.shape[0] - 1, 0)


def south(values):
    return pltpu.roll(values, 1, 0)


def stacked(values):
    return jnp.concatenate([values[:, i : i + 128] for i in range(0, values.shape[1], 128)], axis=0)


def unstacked(values):
    return jnp.concatenate([values[i : i + ROWS, :] for i in range(0, values.shape[0], ROWS)], axis=1)


def row_of(ref, block, row, width):
    tall = width // 128 * ROWS
    return jnp.concatenate(
        [ref[pl.ds(block * 8 * tall + j * ROWS + row, 8, stride=tall), :] for j in range(width // 128)], axis=1
    )


def level_at(k, width):
    tall = width // 128 * ROWS
    return pl.ds(pl.multiple_of(k * tall, tall), tall)


def rows_at(k):
    return pl.ds(pl.multiple_of(k * ROWS, ROWS), ROWS)


def row_index(values):
    return lax.broadcasted_iota(jnp.int32, values.shape, 0)


def spread(row, like):
    return jnp.broadcast_to(row, like.shape)


def vmem(*shapes):
    return [pltpu.VMEM(shape, FLOAT) for shape in shapes]


def hbm(*shapes):
    return [pltpu.HBM(shape, FLOAT) for shape in shapes]


def in_vmem(count):
    return [pl.BlockSpec(memory_space=pltpu.VMEM)] * count


def in_hbm(count):
    return [pl.BlockSpec(memory_space=pltpu.HBM)] * count


def kernel(body, outs, ins, out_specs, name, scratch=(), cost=1):
    return pl.pallas_call(
        body,
        out_shape=outs,
        in_specs=ins,
        out_specs=out_specs,
        scratch_shapes=list(scratch),
        name=name,
        cost_estimate=pl.CostEstimate(flops=cost, bytes_accessed=cost, transcendentals=0),
        compiler_params=pltpu.CompilerParams(vmem_limit_bytes=LIMIT),
    )


def held(array):
    return pltpu.with_memory_space_constraint(array, pltpu.VMEM)


def left(array):
    return pltpu.with_memory_space_constraint(array, pltpu.HBM)


def is_even():
    return lax.rem(lax.axis_index("tile"), 2) == 0


def is_first():
    return lax.rem(lax.axis_index("grp"), 2) == 0


def dealt(even, low, high):
    return jnp.where(even, high, low), jnp.where(even, low, high)


def loads(pairs, sems, first=0):
    copies = [pltpu.make_async_copy(far, near, sems.at[first + i]) for i, (far, near) in enumerate(pairs)]
    for copy in copies:
        copy.start()
    return copies


def in_parts(far, near, parts):
    size = far.shape[0] // parts
    return [(far.at[pl.ds(i * size, size)], near.at[pl.ds(i * size, size)]) for i in range(parts)]


def weight_sum(weight, levels):
    total = weight[0]
    for k in range(1, levels):
        total = total + weight[k]
    return total


def setup_body(levels, weight_hbm, land_hbm, kmt_hbm, ct_hbm, screen_hbm, height_ref, surface_ref,
               fx_ref, fn_ref, dg_ref, q1_ref, base_ref, near_ref, far_ref, wet_bricks,
               weight, land, kmt, screen, sems):
    chunk = levels // 4
    small = loads(((weight_hbm, weight), (kmt_hbm, kmt)), sems)
    land_copies = loads(in_parts(land_hbm, land, 4), sems, 2)
    small += loads(((ct_hbm, base_ref), (screen_hbm, screen)), sems, 6)
    small[0].wait()
    total = weight_sum(weight, levels)
    small[1].wait()
    depth = kmt[...]
    width = depth.shape[1]
    height = jnp.zeros(depth.shape, FLOAT)
    for i, copy in enumerate(land_copies):
        copy.wait()

        def level(k, height):
            wet = jnp.where(k < depth, land[rows_at(k), :], 0).astype(FLOAT)
            wet_bricks[level_at(k, width), :] = stacked(wet)
            return height + weight[k] * wet

        height = lax.fori_loop(i * chunk, (i + 1) * chunk, level, height, unroll=4)
    height = height / total
    surface = jnp.where(0 < depth, land[0:ROWS, :], 0).astype(FLOAT)
    height_ref[...] = height
    surface_ref[...] = surface
    small[2].wait()
    small[3].wait()
    base = base_ref[...]
    rows = row_index(base)
    scale = 0.5 / HALF
    fx = scale * (height + east(height)) * surface * east(surface)
    fn = scale * (height + north(height)) * surface * north(surface)
    fn = jnp.where(rows < ROWS - 1, fn, 0.0)
    fs = south(fn)
    fw = west(fx)
    dg = (screen[...] - MID) * (1.0 / HALF) + fx + fw + fn + fs

    def apply(v):
        return dg * v - fx * east(v) - fw * west(v) - fn * north(v) - fs * south(v)

    q1 = apply(base)
    q2 = apply(q1)
    fx_ref[...] = fx
    fn_ref[...] = fn
    dg_ref[...] = dg
    q1_ref[...] = q1
    even = is_even()
    near_ref[7:8, :] = jnp.zeros_like(base[0:1, :])
    far_ref[7:8, :] = jnp.zeros_like(base[0:1, :])
    for place, values in enumerate((base, q1, q2, fx, dg, height, surface)):
        at = slice(place, place + 1)
        near_ref[at, :], far_ref[at, :] = dealt(even, values[0:1, :], values[ROWS - 1 : ROWS, :])


def rims_body(levels, kappa_hbm, wet_bricks, near_ref, far_ref, sent_ref, links_hbm, kappa, kappa_bricks, links, sems):
    chunk = levels // 4
    width = kappa.shape[1]
    for i, copy in enumerate(loads(in_parts(kappa_hbm, kappa, 4), sems)):
        copy.wait()

        def brick(k, carry):
            kappa_bricks[level_at(k, width), :] = stacked(kappa[rows_at(k), :])
            return carry

        lax.fori_loop(i * chunk, (i + 1) * chunk, brick, 0, unroll=4)
    even = is_even()
    first_group = is_first()
    outs = []
    for block in range(levels // 8):
        found = []
        for side, row, inner in ((0, 0, 1), (1, ROWS - 1, ROWS - 2)):
            kap, kap_in = row_of(kappa_bricks, block, row, width), row_of(kappa_bricks, block, inner, width)
            here, here_in = row_of(wet_bricks, block, row, width), row_of(wet_bricks, block, inner, width)
            at = (block * LINKS + side * 2) * 8
            links[pl.ds(at, 8), :] = 0.5 * (kap + east(kap)) * here * east(here)
            links[pl.ds(at + 8, 8), :] = 0.5 * (kap + kap_in) * here * here_in
            found.append((kap, here))
        for place in range(2):
            at = pl.ds(place * levels + block * 8, 8)
            near_ref[at, :], far_ref[at, :] = dealt(even, found[0][place], found[1][place])
        at, below = pl.ds(block * 8, 8), pl.ds(levels + block * 8, 8)
        sent_ref[at, :] = jnp.where(first_group, far_ref[at, :], far_ref[below, :])
        whole = pl.ds(block * LINKS * 8, LINKS * 8)
        outs += loads([(links.at[whole], links_hbm.at[whole])], sems, 4 + block)
    for copy in outs:
        copy.wait()


def basis_body(ct, height, surface, fx_ref, fn_ref, dg_ref, q1_ref, near, far, links_hbm, basis_ref, sums_ref):
    even = is_even()
    b0 = ct[...]
    rows = row_index(b0)
    first, last = rows == 0, rows == ROWS - 1
    fx, fn, dg = fx_ref[...], fn_ref[...], dg_ref[...]
    fw, fs = west(fx), south(fn)

    def halo(values, row):
        b0_h, q1_h, q2_h, fx_h, dg_h, high_h, wet_h = (values[i : i + 1, :] for i in range(7))
        face = (0.5 / HALF) * (high_h + height[row : row + 1, :]) * wet_h * surface[row : row + 1, :]
        extra = face * (b0_h - ct[row : row + 1, :])
        return b0_h, q1_h + extra, q2_h, fx_h, dg_h, face, extra

    def lift(row):
        return jnp.broadcast_to(row, b0.shape)

    before, after = dealt(even, near[...], far[...])
    sides = (halo(before, 0), halo(after, ROWS - 1))
    face_b, face_a = lift(sides[0][5]), lift(sides[1][5])
    b1 = q1_ref[...] - jnp.where(first, lift(sides[0][6]), 0.0) - jnp.where(last, lift(sides[1][6]), 0.0)
    dg = dg + jnp.where(first, face_b, 0.0) + jnp.where(last, face_a, 0.0)
    fn = jnp.where(last, face_a, fn)
    fs = jnp.where(first, face_b, fs)

    def apply(v, v_before, v_after):
        v_n = jnp.where(last, lift(v_after), north(v))
        v_s = jnp.where(first, lift(v_before), south(v))
        return dg * v - fx * east(v) - fw * west(v) - fn * v_n - fs * v_s

    b2 = 2.0 * apply(b1, sides[0][1], sides[1][1]) - b0

    def outer(side, own):
        b0_h, b1_h, q2_h, fx_h, dg_h, face, extra = side
        b0_h, b1_h, q2_h, fx_h, dg_h, face, extra, own = (lift(v) for v in (b0_h, b1_h, q2_h, fx_h, dg_h, face, extra, own))
        turned = dg_h * extra - fx_h * east(extra) - west(fx_h) * west(extra)
        return (2.0 * (q2_h + turned + face * (b1_h - own)) - b0_h)[0:1, :]

    for place, values in enumerate((b0, b1, b2)):
        basis_ref[pl.ds(place * ROWS, ROWS), :] = values
    b2_b = outer(sides[0], b1[0:1, :])
    b2_a = outer(sides[1], b1[ROWS - 1 : ROWS, :])
    next2 = apply(b2, b2_b, b2_a)
    lanes = lax.broadcasted_iota(jnp.int32, (1, 128), 1)
    packed = jnp.zeros((1, 128), FLOAT)
    for place, (p, q) in enumerate(((b0, b0), (b0, b1), (b1, b1), (b1, b2), (b2, b2), (b2, next2))):
        product = p * q
        folded = product[:, 0:128]
        for j in range(1, product.shape[1] // 128):
            folded = folded + product[:, j * 128 : (j + 1) * 128]
        total = jnp.sum(jnp.sum(folded, axis=0, keepdims=True), axis=1, keepdims=True)
        packed = jnp.where(lanes == place, total, packed)
    sums_ref[...] = jnp.broadcast_to(packed, sums_ref.shape)


def quadratic(left, form):
    total = None
    for i in range(3):
        for j in range(3):
            if left[i] is not None and left[j] is not None:
                term = left[i] * left[j] * form[i][j]
                total = term if total is None else total + term
    return total


def plus(p, q):
    return q if p is None else p if q is None else p + q


def times(scale, p):
    return None if p is None else scale * p


def weights(sums):
    s0, s1, s2, s3, s4, s5 = sums
    g02 = 2.0 * s2 - s0
    gram = ((s0, s1, g02), (s1, s2, s3), (g02, s3, s4))
    b11, b12 = 0.5 * (s3 + s1), 0.5 * (s4 + g02)
    shift = ((s1, s2, s3), (s2, b11, b12), (s3, b12, s5))
    form = [[MID * gram[i][j] + HALF * shift[i][j] for j in range(3)] for i in range(3)]
    one = jnp.ones_like(s0)
    x, r, d = [None] * 3, [one, None, None], [one, None, None]
    rr = s0
    for step in range(ITERS):
        alpha = jnp.clip(rr / quadratic(d, form), 1.0 / HIGH, 1.0 / LOW)
        x = [plus(x[i], times(alpha, d[i])) for i in range(3)]
        if step + 1 < ITERS:
            image = [
                plus(times(MID, d[0]), times(0.5 * HALF, d[1])),
                plus(plus(times(MID, d[1]), times(HALF, d[0])), times(0.5 * HALF, d[2])),
                plus(times(MID, d[2]), times(0.5 * HALF, d[1])),
            ]
            r = [plus(r[i], times(-1.0, times(alpha, image[i]))) for i in range(3)]
            new = quadratic(r, gram)
            beta = jnp.clip(new / rr, 0.0, HIGH / LOW)
            d = [plus(r[i], times(beta, d[i])) for i in range(3)]
            rr = new
    return x


def inverse_of(values):
    guess = pl.reciprocal(values, approx=True)
    guess = guess * (2.0 - values * guess)
    return guess * (2.0 - values * guess)


def columns_body(levels, sums, basis_ref, weight_hbm, kmt_hbm, source_hbm, kvert_hbm, land_hbm, links_hbm,
                 out_hbm, u, near_ref, far_ref, weight, kmt, source, kvert, land, links, s_ref, ratio, sems, out_sems):
    width = source.shape[1]
    parts = 8
    chunk = levels // parts
    small = loads(((weight_hbm, weight), (kmt_hbm, kmt)), sems)
    parted = [in_parts(far, near, parts) for far, near in ((land_hbm, land), (kvert_hbm, kvert), (source_hbm, source))]
    big = loads([pairs[i] for i in range(parts) for pairs in parted], sems, 2)
    links_copy = loads([(links_hbm, links)], sems, 2 + 3 * parts)[0]

    total = jnp.sum(sums[...], axis=0, keepdims=True)
    mix = weights([total[:, i : i + 1] for i in range(6)])
    b0, b1, b2 = (basis_ref[i * ROWS : (i + 1) * ROWS, :] for i in range(3))
    s = mix[0] * b0 + mix[1] * b1 + mix[2] * b2
    s_ref[...] = s
    outs = loads([(s_ref, out_hbm)], out_sems)

    small[0].wait()
    scaled = stacked(s) / jnp.full((ROWS * width // 128, 128), weight_sum(weight, levels), FLOAT)
    small[1].wait()
    depth = stacked(kmt[...])

    def sea(k):
        return jnp.where(k < depth, stacked(land[rows_at(k), :]), 0).astype(FLOAT)

    def down(k, carry):
        here, link, passed = carry
        at = level_at(k, width)
        below = jnp.where(k + 1 < levels, sea(jnp.minimum(k + 1, levels - 1)), 0.0)
        coupling = stacked(kvert[rows_at(k), :]) * here * below
        over = inverse_of(1.0 + coupling + link)
        value = (stacked(source[rows_at(k), :]) + here * (weight[k] * scaled) + passed) * over
        part = coupling * over
        ratio[at, :] = part
        u[at, :] = value
        return below, coupling - coupling * part, coupling * value

    zero = jnp.zeros(scaled.shape, FLOAT)
    big[0].wait()
    carry = (sea(0), zero, zero)
    for i in range(parts):
        big[3 * i + 1].wait()
        big[3 * i + 2].wait()
        if i + 1 < parts:
            big[3 * i + 3].wait()
        carry = lax.fori_loop(i * chunk, (i + 1) * chunk, down, carry, unroll=3)

    def up(i, below):
        at = level_at(levels - 1 - i, width)
        value = u[at, :] + ratio[at, :] * below
        u[at, :] = value
        return value

    lax.fori_loop(0, levels, up, zero, unroll=4)
    links_copy.wait()
    even = is_even()
    for block in range(levels // 8):
        found = []
        for side, row, inner in ((0, 0, 1), (1, ROWS - 1, ROWS - 2)):
            value, value_in = row_of(u, block, row, width), row_of(u, block, inner, width)
            face, link = (links[pl.ds((block * LINKS + side * 2 + i) * 8, 8), :] for i in range(2))
            flux = face * (east(value) - value)
            found.append((value, value + (flux - west(flux)) + link * (value_in - value)))
        for place in range(2):
            at = pl.ds(place * levels + block * 8, 8)
            near_ref[at, :], far_ref[at, :] = dealt(even, found[0][place], found[1][place])
    for copy in outs:
        copy.wait()


def inner_body(first, last, with_relay, u0, kmt_hbm, kappa_hbm, land_hbm, *refs):
    if with_relay:
        passed, u2_ref, relay_ref = refs[:3]
        relay_ref[...] = passed[...]
        refs = refs[3:]
    else:
        u2_ref, refs = refs[0], refs[1:]
    kmt, kappa, land, sems = refs
    size = PART * ROWS
    parts = (last - first) // PART
    kmt_copy = loads([(kmt_hbm, kmt)], sems)[0]
    pairs = []
    for i in range(parts):
        source, target = pl.ds((first + i * PART) * ROWS, size), pl.ds(i * size, size)
        pairs += [(kappa_hbm.at[source], kappa.at[target]), (land_hbm.at[source], land.at[target])]
    copies = loads(pairs, sems, 1)
    kmt_copy.wait()
    depth = kmt[...]
    width = depth.shape[1]
    inside = row_index(depth) < ROWS - 1

    def face(here, there):
        return jnp.where(jnp.minimum(here, there) > 0.0, here + there, 0.0)

    def group(i, carry):
        ks = [GROUP * i + j for j in range(GROUP)]
        sea = [jnp.where(k + first < depth, land[rows_at(k), :], 0) > 0 for k in ks]
        halved = [jnp.where(wet, 0.5 * kappa[rows_at(k), :], 0.0) for wet, k in zip(sea, ks)]
        u = [unstacked(u0[level_at(k + first, width), :]) for k in ks]
        fx = [face(v, east(v)) for v in halved]
        fn = [jnp.where(inside, face(v, north(v)), 0.0) for v in halved]
        for _ in range(2):
            flux_x = [f * (east(v) - v) for f, v in zip(fx, u)]
            flux_y = [f * (north(v) - v) for f, v in zip(fn, u)]
            u = [v + (x - west(x)) + (y - south(y)) for v, x, y in zip(u, flux_x, flux_y)]
        for k, v in zip(ks, u):
            u2_ref[rows_at(k), :] = v
        return carry

    for i in range(parts):
        copies[2 * i].wait()
        copies[2 * i + 1].wait()
        lax.fori_loop(i * PART // GROUP, (i + 1) * PART // GROUP, group, 0)


def finish_body(levels, u2_high, u2_low, links, own_near, own_far, rim_near, rim_far, near, far, rim_other_near, kept, swapped,
                out, change_ref, buffer, sems):
    width = own_near.shape[1]
    tall = width // 128 * ROWS
    rows = lax.broadcasted_iota(jnp.int32, (ROWS, width), 0)
    on_rim = (rows < 2) | (rows >= ROWS - 2)
    even = is_even()
    first_group = is_first()
    copies = []
    for block in range(levels // 8):
        at, below = pl.ds(block * 8, 8), pl.ds(levels + block * 8, 8)

        def pairs(a, b):
            return [dealt(even, a[part, :], b[part, :]) for part in (at, below)]

        own, rim = pairs(own_near, own_far), pairs(rim_near, rim_far)
        other = pairs(near, far)
        far_kap = jnp.where(first_group, kept[at, :], swapped[at, :])
        far_wet = jnp.where(first_group, swapped[at, :], kept[at, :])
        rim_other = [dealt(even, rim_other_near[at, :], far_kap), dealt(even, rim_other_near[below, :], far_wet)]
        for side, row, inner in ((0, 0, 1), (1, ROWS - 1, ROWS - 2)):
            face = 0.5 * (rim[0][side] + rim_other[0][side]) * rim[1][side] * rim_other[1][side]
            change = face * (other[0][side] - own[0][side])
            along, link = (links[pl.ds((block * LINKS + side * 2 + i) * 8, 8), :] for i in range(2))
            flux = along * (east(change) - change)
            passed = link * change
            on_row = (change + (flux - west(flux)) - passed
                      + face * (other[1][side] - own[1][side] - 2.0 * change))
            for j in range(width // 128):
                lanes = slice(j * 128, (j + 1) * 128)
                change_ref[pl.ds(j * ROWS + row, 8, stride=tall), :] = on_row[:, lanes]
                change_ref[pl.ds(j * ROWS + inner, 8, stride=tall), :] = passed[:, lanes]
        for k in range(8):
            level = block * 8 + k
            change = jnp.where(on_rim, unstacked(change_ref[level_at(k, width), :]), 0.0)
            u2, first = (u2_high, 0) if level < BEFORE_SWAP else (u2_low, BEFORE_SWAP)
            buffer[rows_at(level), :] = u2[rows_at(level - first), :] + change
        whole = pl.ds(block * 8 * ROWS, 8 * ROWS)
        copy = pltpu.make_async_copy(buffer.at[whole], out.at[whole], sems.at[block])
        copy.start()
        copies.append(copy)
    for copy in copies:
        copy.wait()


def swap(array, start, axis="tile"):
    firsts = range(start, lax.axis_size(axis) - 1, 2)
    return lax.ppermute(array, axis, [(i, i + 1) for i in firsts] + [(i + 1, i) for i in firsts])


def exchange(to_near, to_far):
    from_far = swap(to_far, 1)
    return swap(to_near, 0), from_far


def body(ct_tracer, ct_surface, kappa, kvert, land, kmt, screen, layer_weight):
    levels, rows, width = ct_tracer.shape
    count = lax.axis_size("tile")
    tall = levels * rows
    tile, brick, flat = (rows, width), (tall * width // 128, 128), (tall, width)
    rim, link_rows = (2 * levels, width), (levels * LINKS, width)
    scalars, whole = pltpu.SMEM((levels,), FLOAT), pltpu.VMEM(flat, FLOAT)
    ints, tile_ints = pltpu.VMEM(flat, jnp.int32), pltpu.VMEM(tile, jnp.int32)
    bricks, tiles = pltpu.VMEM(brick, FLOAT), pltpu.VMEM(tile, FLOAT)
    ct_tracer, kappa, kvert, land = (left(a.reshape(flat)) for a in (ct_tracer, kappa, kvert, land))
    kmt, layer_weight = left(kmt), left(layer_weight)
    semaphores = pltpu.SemaphoreType.DMA

    height, surface, s_fx, s_fn, s_dg, q1, base, to_near, to_far, wet = kernel(
        functools.partial(setup_body, levels), vmem(*[tile] * 9, brick), in_hbm(5), in_vmem(10), "setup",
        [scalars, ints, tile_ints, tiles, semaphores((8,))],
    )(layer_weight, land, kmt, left(ct_surface), left(screen))
    near, far = exchange(to_near, to_far)

    rim_near, rim_far, rim_sent, links = kernel(
        functools.partial(rims_body, levels), vmem(rim, rim, (levels, width)) + hbm(link_rows), in_hbm(1) + in_vmem(1),
        in_vmem(3) + in_hbm(1), "rims", [whole, bricks, pltpu.VMEM(link_rows, FLOAT), semaphores((4 + levels // 8,))],
    )(kappa, wet)
    links_free, links = links, left(links)
    rim_other_near, kept = exchange(rim_near, rim_sent)

    basis, sums = kernel(
        basis_body, vmem((3 * rows, width), (count, 128)), in_vmem(9) + in_hbm(1),
        in_vmem(2), "basis"
    )(base, height, surface, s_fx, s_fn, s_dg, q1, near, far, links)
    sums = lax.all_to_all(sums.reshape(count, 1, 128), "tile", 0, 0, tiled=True).reshape(count, 128)

    solution, u0, row_near, row_far = kernel(
        functools.partial(columns_body, levels), hbm(tile) + vmem(brick, rim, rim), in_vmem(2) + in_hbm(6),
        in_hbm(1) + in_vmem(3), "columns",
        [scalars, tile_ints, whole, whole, ints, pltpu.VMEM(link_rows, FLOAT), tiles, bricks, semaphores((27,)),
         semaphores((1,))],
    )(sums, basis, layer_weight, kmt, ct_tracer, kvert, land, links)
    other_near, other_far = exchange(row_near, row_far)

    def inner(first, last, name, *relayed):
        size = ((last - first) * rows, width)
        return kernel(
            functools.partial(inner_body, first, last, bool(relayed)), vmem(size, *[(levels, width) for _ in relayed]),
            in_vmem(1) + in_hbm(3) + in_vmem(len(relayed)), in_vmem(1 + len(relayed)), name,
            [tile_ints, pltpu.VMEM(size, FLOAT), pltpu.VMEM(size, jnp.int32), semaphores((1 + 2 * (last - first) // PART,))],
        )(u0, kmt, kappa, land, *relayed)

    u2_high, relayed = inner(0, BEFORE_SWAP, "inner_high", kept)
    swapped = swap(relayed, 0, "grp")
    (u2_low,) = inner(BEFORE_SWAP, levels, "inner_low")

    values = kernel(
        functools.partial(finish_body, levels), hbm(flat), in_vmem(12), in_hbm(1), "finish",
        [pltpu.VMEM((8 * rows * width // 128, 128), FLOAT), whole, semaphores((levels // 8,))],
    )(u2_high, u2_low, held(links_free), row_near, row_far, rim_near, rim_far, other_near, other_far, rim_other_near,
      kept, swapped)[0]
    return (values.reshape(levels, rows, width), solution)


def solution(mesh):
    in_specs = (
        P(None, ("grp", "tile"), None),
        P(("grp", "tile"), None),
        P(None, "tile", None),
        P(None, "tile", None),
        P(None, "tile", None),
        P("tile", None),
        P("tile", None),
        P(),
    )
    out_specs = (P(None, ("grp", "tile"), None), P(("grp", "tile"), None))
    return jax.shard_map(body, mesh=mesh, in_specs=in_specs, out_specs=out_specs, check_vma=False)
```
